128 devices in a mesh: lat: 16 (over x, y), wave: 8 (over z, core).
Axes of the slice: x: 4, y: 4, z: 4, core: 2. Of those that a mesh axis runs over, the one named last changes fastest.
Arguments:
- fields: bfloat16 [24, 128, 5120], P(None, 'lat', 'wave'), may hold values from -6 to 6
- row_length: int32 [128], P('lat'), may hold values from 2560 to 5120, as said below
- wave_order: int32 [1280], replicated, may hold values from 0 to 1279, each once
- depart_row: int32 [128, 5120], P('lat', 'wave'), may hold values from -7 to 6
- depart_col: int32 [128, 5120], P('lat', 'wave'), may hold values from -7 to 6
- frac_row: float32 [128, 5120], P('lat', 'wave'), may hold values from 0 to 1
- frac_col: float32 [128, 5120], P('lat', 'wave'), may hold values from 0 to 1
- legendre: bfloat16 [1280, 128, 1280], P(('lat', 'wave')), may hold values from -0.5 to 0.5
Outputs:
- spectral: float32 [1280, 48, 1280], P(('lat', 'wave'))
The draws below stay inside these ranges and needn't reach their ends.
Inputs may be any that keep to these rules, and one draw needn't show every extreme that they name: `row_length`: every row length lies between 2560 and 5120; at least one row has 5120 points. `wave_order`: each wavenumber stands in exactly one slot.
All inputs are finite; a program needn't handle non-finite values.
Results may differ from the reference program's by a relative error of at most 0.009.
Values may be sent and summed in bfloat16 or wider, within the bound.
No kernel may reach another device: no remote copies, remote signals or barrier semaphores. Data moves between devices by JAX's collectives and lax.ppermute only.
A program may use at most 128 MiB of HBM per device.

```python
import math
import jax
import jax.numpy as jnp
from jax import lax

WAVES = 1280
DEGREES = 1280
LON = 5120
HALO = 8
LATS = 128
SLICES = 24


def draw_row_length(key, part):
    base_lengths = jax.random.randint(key, (LATS,), LON // 2, LON + 1)
    longest = jax.random.randint(jax.random.fold_in(key, 7), (), 0, LATS)
    return jnp.where(jnp.arange(LATS) == longest, LON, base_lengths).astype(jnp.int32)


def with_ends(array, key, smallest, high):
    spot = [jax.random.randint(jax.random.fold_in(key, axis), (), 0, length) for axis, length in enumerate(array.shape)]
    widest = array.shape.index(max(array.shape))
    neighbour = spot[:widest] + [(spot[widest] + 1) % array.shape[widest]] + spot[widest + 1:]
    return array.at[tuple(spot)].set(smallest).at[tuple(neighbour)].set(high)


def level_of(stream_key, extent, shards, low, high):
    level = 1.0
    for dim, blocks in shards:
        draws = jax.random.uniform(jax.random.fold_in(jax.random.fold_in(stream_key, 6), dim), (blocks,), jnp.float32, low / len(shards), high / len(shards))
        level = level * jnp.repeat(jnp.exp(draws), extent[dim] // blocks).reshape((-1,) + (1,) * (len(extent) - 1 - dim))
    return level


def noise(rng, dims, spread, bound, cuts=(), kind=jnp.bfloat16):
    factor_of = level_of(rng, dims, cuts, -0.22, 0.18) if cuts else 1.0
    array = jax.random.normal(rng, dims, jnp.float32) * spread * factor_of
    return jnp.minimum(jnp.maximum(array, -bound), bound).astype(kind)


def setup_inputs(seed: int = 0) -> dict:
    splits = jax.random.split(jax.random.key(seed), 9)
    fields = noise(splits[0], (SLICES, LATS, LON), 1.0, 6.0, ((1, 16), (2, 8)))
    row_length = draw_row_length(jax.random.fold_in(splits[8], 71), 0)
    wave_order = jax.random.permutation(splits[2], WAVES).astype(jnp.int32)
    depart_row = with_ends(jax.random.randint(splits[3], (LATS, LON), 1 - HALO, HALO - 1), jax.random.fold_in(splits[3], 1), 1 - HALO, (HALO - 1) - 1).astype(jnp.int32)
    depart_col = with_ends(jax.random.randint(splits[4], (LATS, LON), 1 - HALO, HALO - 1), jax.random.fold_in(splits[4], 1), 1 - HALO, (HALO - 1) - 1).astype(jnp.int32)
    frac_row = jnp.clip(1.0 * jax.random.uniform(splits[5], (LATS, LON), jnp.float32) ** level_of(splits[5], (LATS, LON), ((0, 16), (1, 8)), -0.2, 0.2), 0.0, 1.0)
    frac_col = jnp.clip(1.0 * jax.random.uniform(splits[6], (LATS, LON), jnp.float32) ** level_of(splits[6], (LATS, LON), ((0, 16), (1, 8)), -0.2, 0.2), 0.0, 1.0)
    legendre = noise(splits[7], (WAVES, LATS, DEGREES), LATS ** -0.5, 0.5, ((0, 128),))
    return dict(fields=fields, row_length=row_length, wave_order=wave_order, depart_row=depart_row, depart_col=depart_col, frac_row=frac_row, frac_col=frac_col, legendre=legendre)


def cubic_weights(fraction):
    return (-fraction * (fraction - 1.0) * (fraction - 2.0) / 6.0, (fraction + 1.0) * (fraction - 1.0) * (fraction - 2.0) / 2.0, -(fraction + 1.0) * fraction * (fraction - 2.0) / 2.0, (fraction + 1.0) * fraction * (fraction - 1.0) / 6.0)

def interpolate(padded, depart_row, depart_col, frac_row, frac_col, margin, column_start, lengths):
    slices = padded.shape[0]
    row_count, col_count = depart_row.shape
    padded_width = col_count + 2 * margin
    positions = padded.shape[1] * padded_width
    flattened = padded.reshape(slices, positions)
    extended = jnp.pad(flattened, ((0, 0), (0, 3)))
    stacked = jnp.concatenate([extended[:, shift:shift + positions] for shift in range(4)], axis=0).T
    row_index = jnp.arange(row_count, dtype=jnp.int32)[:, None]
    col_index = jnp.arange(col_count, dtype=jnp.int32)[None, :]
    top_rows = row_index + (margin - 1) + depart_row
    left_cols = col_index + (margin - 1) + depart_col
    weight_rows = cubic_weights(frac_row)
    weight_cols = cubic_weights(frac_col)
    total = jnp.zeros((slices, row_count * col_count), jnp.float32)
    for shift_row in range(4):
        indices = ((top_rows + shift_row) * padded_width + left_cols).reshape(-1).astype(jnp.int32)
        picked = jnp.take(stacked, indices, axis=0).T.reshape(4, slices, row_count * col_count)
        partial_value = jnp.zeros_like(total)
        for shift_col in range(4):
            partial_value = partial_value + weight_cols[shift_col].reshape(1, -1) * picked[shift_col].astype(jnp.float32)
        total = total + weight_rows[shift_row].reshape(1, -1) * partial_value
    live_mask = column_start + col_index < lengths[:, None]
    total = jnp.where(live_mask.reshape(1, -1), total, jnp.zeros_like(total))
    return total.reshape(slices, row_count, col_count).astype(jnp.bfloat16)

def transform(grid_rows, lengths, offset, wave_order):
    slices, row_count, row_width = grid_rows.shape
    groups = row_width // 64
    wave_count = wave_order.shape[0]
    blocks = row_count // 4
    shaped = grid_rows.reshape(slices, blocks, 4, groups, 64).transpose(1, 2, 0, 3, 4)
    lengths_block = lengths.reshape(blocks, 4)
    inner_index = jnp.arange(64, dtype=jnp.int32)
    outer_index = offset + 64 * jnp.arange(groups, dtype=jnp.int32)

    def one_row(pieces, length):
        step_angle = 2.0 * math.pi / length.astype(jnp.float32)
        product_one = inner_index[:, None] * wave_order[None, :] % length
        angle_one = product_one.astype(jnp.float32) * step_angle
        twiddle = jnp.concatenate([jnp.cos(angle_one), jnp.sin(angle_one)], axis=1)
        partial_value = jnp.dot(pieces.reshape(slices * groups, 64).astype(jnp.float32), twiddle, precision=lax.Precision.HIGHEST).reshape(slices, groups, 2 * wave_count)
        cosine = partial_value[:, :, :wave_count]
        sine_part = partial_value[:, :, wave_count:]
        product_two = outer_index[:, None] * wave_order[None, :] % length
        angle_two = product_two.astype(jnp.float32) * step_angle
        cos_two = jnp.cos(angle_two)
        sin_two = jnp.sin(angle_two)
        real_part = lax.optimization_barrier(jnp.sum(cos_two * cosine - sin_two * sine_part, axis=1))
        imag_part = -lax.optimization_barrier(jnp.sum(sin_two * cosine + cos_two * sine_part, axis=1))
        normalizer = lax.rsqrt(length.astype(jnp.float32))
        return jnp.stack([real_part, imag_part], axis=1).reshape(2 * slices, wave_count) * normalizer

    def one_block(inputs):
        return jax.vmap(one_row)(inputs[0], inputs[1])
    result = lax.map(one_block, (shaped, lengths_block))
    return result.reshape(row_count, 2 * slices, wave_count)

def reference(fields, row_length, wave_order, depart_row, depart_col, frac_row, frac_col, legendre):
    col_index = jnp.arange(LON, dtype=jnp.int32)
    live_mask = col_index[None, :] < row_length[:, None]
    masked = jnp.where(live_mask[None], fields, jnp.zeros_like(fields))
    wrapped = jnp.concatenate([masked[:, :, LON - HALO:], masked, masked[:, :, :HALO]], axis=2)
    padded = jnp.pad(wrapped, ((0, 0), (HALO, HALO), (0, 0)))
    arrival = interpolate(padded, depart_row, depart_col, frac_row, frac_col, HALO, 0, row_length)
    fourier = transform(arrival, row_length, 0, wave_order).astype(jnp.bfloat16)
    degree = jnp.arange(DEGREES, dtype=jnp.int32)

    def one_block(block_index):
        first_slot = block_index * 128
        four_block = lax.dynamic_slice_in_dim(fourier, first_slot, 128, 2).astype(jnp.float32)
        table_block = lax.dynamic_slice_in_dim(legendre, first_slot, 128, 0).astype(jnp.float32)
        waves_block = lax.dynamic_slice_in_dim(wave_order, first_slot, 128, 0)
        keep_mask = (degree[None, :] >= waves_block[:, None]).astype(jnp.float32)
        return jnp.einsum('rcs,srn->scn', four_block, table_block * keep_mask[:, None, :])
    result = lax.map(one_block, jnp.arange(WAVES // 128, dtype=jnp.int32))
    return result.reshape(WAVES, 2 * SLICES, DEGREES)
```

```python
import math

import jax
import jax.numpy as jnp
from jax import lax
from jax.experimental import pallas as pl
from jax.experimental.pallas import tpu as pltpu
from jax.sharding import PartitionSpec as P

F32 = jnp.float32
BF16 = jnp.bfloat16
VMEM = pl.BlockSpec(memory_space=pltpu.VMEM)
SMEM = pl.BlockSpec(memory_space=pltpu.SMEM)
LIMIT = 48 * 1024 * 1024

SLICES = 24
BAND = 8
WIDE = 640
BLOCKS = 5
SLOTS = 10
DEVICES = 128
ROWS = 4
STACK = 128


def cubic_weights(fraction):
    return (
        -fraction * (fraction - 1.0) * (fraction - 2.0) / 6.0,
        (fraction + 1.0) * (fraction - 1.0) * (fraction - 2.0) / 2.0,
        -(fraction + 1.0) * fraction * (fraction - 2.0) / 2.0,
        (fraction + 1.0) * fraction * (fraction - 1.0) / 6.0,
    )


def picked_weight(distance, weights):
    chosen = jnp.where(distance == 3, weights[3], 0.0)
    for step in (2, 1, 0):
        chosen = jnp.where(distance == step, weights[step], chosen)
    return chosen


def interpolate_kernel(
    place, live, own, above, below, depart_row, depart_col, frac_row, frac_col, keep, send,
    main, edge, columns, row_table, points, stack,
):
    lane = lax.broadcasted_iota(jnp.int32, (1, WIDE), 1) % 128
    for base, first, fraction in (
        (0, depart_col[...] + lane - 1, frac_col),
        (8, depart_row[...] + (BAND - 1), frac_row),
    ):
        for step, value in enumerate((first.astype(F32),) + cubic_weights(fraction[...])):
            for row in range(BAND):
                points[row, base + step : base + step + 1, :] = value[row : row + 1, :]
    count = BAND * SLICES
    for part, ref in enumerate((above, own, below)):
        rows = pl.ds(part * count, count)
        main[rows, :] = ref[:, :WIDE]
        for block in range(BLOCKS):
            right = block + 1
            left = block - 1 if block else BLOCKS
            edge[rows, 128 * block : 128 * block + 128] = jnp.concatenate(
                [ref[:, 128 * right : 128 * right + 64], ref[:, 128 * left + 64 : 128 * left + 128]],
                axis=1,
            )
    columns[...] = jnp.zeros_like(columns)
    stack[...] = jnp.zeros_like(stack)
    core = place[0]

    def one_pair(step, carry):
        pair = step ^ (2 * core)
        window = pl.ds(pl.multiple_of(pair * (2 * SLICES), 2 * SLICES), 18 * SLICES)

        def row_of(item, block):
            return jnp.concatenate(
                [
                    points[2 * pair + half, item : item + 1, 128 * block : 128 * block + 128]
                    for half in range(2)
                ],
                axis=1,
            )

        for block in range(BLOCKS):
            start = row_of(0, block)
            weights = [row_of(1 + k, block) for k in range(4)]
            source = lax.broadcasted_iota(jnp.int32, (144, 256), 0).astype(F32)
            columns[0:144, :] = picked_weight(source - start, weights).astype(BF16)
            source = lax.broadcasted_iota(jnp.int32, (16, 256), 0).astype(F32) - 16.0
            columns[240:256, :] = picked_weight(source - start, weights).astype(BF16)
            half = (lax.broadcasted_iota(jnp.int32, (1, 256), 1) >= 128).astype(F32)
            start = row_of(8, block) + half
            weights = [row_of(9 + k, block) for k in range(4)]
            source = lax.broadcasted_iota(jnp.int32, (24, 256), 0).astype(F32)
            row_table[...] = picked_weight(source - start, weights)
            lanes = slice(128 * block, 128 * block + 128)
            left = jnp.concatenate([main[window, lanes], edge[window, lanes]], axis=1)
            spread = jnp.dot(left, columns[...], preferred_element_type=F32)
            for half in range(2):
                side = slice(128 * half, 128 * half + 128)
                total = jnp.zeros((SLICES, 128), F32)
                for row in range(half, half + 17):
                    total = total + row_table[row : row + 1, side] * spread[
                        SLICES * row : SLICES * row + SLICES, side
                    ]
                position = lax.broadcasted_iota(jnp.int32, (SLICES, 128), 1) + 128 * block
                total = jnp.where(position < live[2 * pair + half], total, 0.0)
                stack[2 * step + half, SLICES * block : SLICES * block + SLICES, :] = total
        return carry

    lax.fori_loop(0, BAND // 2, one_pair, 0)
    keep[...] = stack[0:ROWS].astype(BF16)
    send[...] = stack[ROWS:].astype(BF16)


def turn(count, length, inverse):
    whole = jnp.floor(count * inverse + 0.5)
    angle = (count - whole * length) * (inverse * math.pi)
    square = angle * angle
    sine = angle * (
        1.0
        + square
        * (
            -1.0 / 6
            + square
            * (1.0 / 120 + square * (-1.0 / 5040 + square * (1.0 / 362880 - square / 39916800)))
        )
    )
    cosine = 1.0 + square * (
        -0.5
        + square
        * (
            1.0 / 24
            + square
            * (-1.0 / 720 + square * (1.0 / 40320 + square * (-1.0 / 3628800 + square / 479001600)))
        )
    )
    return 1.0 - 2.0 * sine * sine, 2.0 * sine * cosine


def twiddle_kernel(place, lengths, waves, inner, outer):
    wave_place = place[1]
    step = lax.broadcasted_iota(jnp.int32, (16, 128), 0)
    tile = jnp.where(step < 8, wave_place, wave_place ^ 1)
    offset = (tile * WIDE + (step % 8) * 128).astype(F32)
    coarse = (8 * step).astype(F32)
    fine = lax.broadcasted_iota(jnp.int32, (8, 128), 0).astype(F32)

    def one(index, carry):
        row = index // SLOTS
        slot = index % SLOTS
        length = jnp.full((1, 128), lengths[row], jnp.int32).astype(F32)
        inverse = 1.0 / length
        wave = waves[pl.ds(slot, 1), :]
        lanes = pl.ds(pl.multiple_of(slot * 256, 256), 128)
        lanes_two = pl.ds(pl.multiple_of(slot * 256 + 128, 128), 128)
        cosine, sine = turn(offset * wave, length, inverse)
        norm = lax.rsqrt(length)
        outer[row, :, lanes] = cosine * norm
        outer[row, :, lanes_two] = sine * norm
        cos_one, sin_one = turn(coarse * wave, length, inverse)
        cos_two, sin_two = turn(fine * wave, length, inverse)
        for pair in range(8):
            real = []
            imag = []
            for part in (2 * pair, 2 * pair + 1):
                c, s = cos_one[part : part + 1], sin_one[part : part + 1]
                real.append(c * cos_two - s * sin_two)
                imag.append(s * cos_two + c * sin_two)
            rows = slice(16 * pair, 16 * pair + 16)
            inner[row, rows, lanes] = jnp.concatenate(real, axis=0).astype(BF16)
            inner[row, rows, lanes_two] = jnp.concatenate(imag, axis=0).astype(BF16)
        return carry

    lax.fori_loop(0, ROWS * SLOTS, one, 0)


def fourier_kernel(mine, other, inner, outer, message, sums, shuffled):
    sums[...] = jnp.zeros_like(sums)

    def one(index, carry):
        row = index // SLOTS
        slot = index % SLOTS
        lanes = pl.ds(pl.multiple_of(slot * 256, 256), 256)
        table = inner[row, :, lanes]
        factors = outer[row, :, lanes]
        left = jnp.concatenate([mine[row], other[row]], axis=0)
        parts = jnp.dot(left, table, preferred_element_type=F32)
        real = jnp.zeros((SLICES, 128), F32)
        imag = jnp.zeros((SLICES, 128), F32)
        for side in range(2):
            for block in range(BLOCKS):
                first = STACK * side + SLICES * block
                cosine = parts[first : first + SLICES, :128]
                sine = parts[first : first + SLICES, 128:]
                at = 8 * side + block
                c, s = factors[at : at + 1, :128], factors[at : at + 1, 128:]
                real = real + (c * cosine - s * sine)
                imag = imag - (s * cosine + c * sine)
        base = row * 512 + slot * 48
        sums[pl.ds(base, SLICES, stride=2), :] = real
        sums[pl.ds(base + 1, SLICES, stride=2), :] = imag
        return carry

    lax.fori_loop(0, ROWS * SLOTS, one, 0)
    for part in range(16):
        shuffled[pl.ds(part, DEVICES, stride=16), :] = sums[128 * part : 128 * part + 128, :].T
    message[...] = shuffled[...].astype(BF16)


def legendre_kernel(waves, message, table, out, flat, sorted_rows, left):
    step = pl.program_id(0)

    @pl.when(step == 0)
    def _():
        for band in range(16):
            for core in range(2):
                total = message[8 * band + core].astype(F32)
                for z in range(1, 4):
                    total = total + message[8 * band + 2 * z + core].astype(F32)
                first = (2 * band + core) * 16
                flat[first : first + 16, :] = total
        for row in range(ROWS):
            for part in range(4):
                sorted_rows[pl.ds(128 * part + row, 32, stride=4), :] = flat[
                    pl.ds(4 * row + part, 32, stride=16), :
                ]
        for part in range(4):
            rows = slice(128 * part, 128 * part + 128)
            left[rows, :] = sorted_rows[rows, :].T.astype(BF16)

    rows = pl.ds(pl.multiple_of(step * 48, 16), 48)
    product = jnp.dot(left[rows, :], table[0], preferred_element_type=F32)
    degree = lax.broadcasted_iota(jnp.int32, product.shape, 1)
    out[0] = jnp.where(degree >= waves[step], product, 0.0)


def local(fields, row_length, wave_order, depart_row, depart_col, frac_row, frac_col, legendre):
    wave_place = lax.axis_index("wave")
    lat_place = lax.axis_index("lat")
    core = wave_place % 2
    column_start = wave_place * WIDE
    live = row_length - column_start
    live_mask = jnp.arange(WIDE, dtype=jnp.int32)[None, :] < live[:, None]
    masked = jnp.where(live_mask[None], fields, jnp.zeros_like(fields))
    own = masked.transpose(1, 0, 2).reshape(BAND * SLICES, WIDE)
    place = jnp.stack([core, wave_place]).astype(jnp.int32)

    ring = lax.axis_size("wave")
    from_left = lax.ppermute(
        own[:, WIDE - 128 :], "wave", [(i, (i + 1) % ring) for i in range(ring)]
    )
    from_right = lax.ppermute(own[:, :128], "wave", [((i + 1) % ring, i) for i in range(ring)])
    rim = jnp.concatenate([from_right[:, :64], from_left[:, 64:]], axis=1)
    own = jnp.concatenate([own, rim], axis=1)
    bands = lax.axis_size("lat")
    above = lax.ppermute(own, "lat", [(i, i + 1) for i in range(bands - 1)])
    below = lax.ppermute(own, "lat", [(i + 1, i) for i in range(bands - 1)])

    lengths = lax.dynamic_slice_in_dim(row_length, core * ROWS, ROWS)
    ordered = wave_order.reshape(DEVICES, SLOTS).T.astype(F32)
    inner, outer = pl.pallas_call(
        twiddle_kernel,
        out_shape=(
            jax.ShapeDtypeStruct((ROWS, 128, SLOTS * 256), BF16),
            jax.ShapeDtypeStruct((ROWS, 16, SLOTS * 256), F32),
        ),
        in_specs=[SMEM, SMEM, VMEM],
        out_specs=(VMEM, VMEM),
        compiler_params=pltpu.CompilerParams(vmem_limit_bytes=LIMIT),
        cost_estimate=pl.CostEstimate(flops=20_000_000, bytes_accessed=3_000_000, transcendentals=0),
        name="twiddle",
    )(place, lengths, ordered)

    keep, send = pl.pallas_call(
        interpolate_kernel,
        out_shape=(jax.ShapeDtypeStruct((ROWS, STACK, 128), BF16),) * 2,
        in_specs=[SMEM, SMEM] + [VMEM] * 7,
        out_specs=(VMEM, VMEM),
        scratch_shapes=[
            pltpu.VMEM((3 * BAND * SLICES, WIDE), BF16),
            pltpu.VMEM((3 * BAND * SLICES, WIDE), BF16),
            pltpu.VMEM((256, 256), BF16),
            pltpu.VMEM((24, 256), F32),
            pltpu.VMEM((BAND, 16, WIDE), F32),
            pltpu.VMEM((BAND, STACK, 128), F32),
        ],
        compiler_params=pltpu.CompilerParams(vmem_limit_bytes=LIMIT),
        name="interpolate",
    )(place, live, own, above, below, depart_row, depart_col, frac_row, frac_col)

    other = lax.ppermute(send, "wave", [(i, i ^ 1) for i in range(ring)])
    message = pl.pallas_call(
        fourier_kernel,
        out_shape=jax.ShapeDtypeStruct((DEVICES * 16, 128), BF16),
        in_specs=[VMEM] * 4,
        out_specs=VMEM,
        scratch_shapes=[
            pltpu.VMEM((ROWS * 512, 128), F32),
            pltpu.VMEM((DEVICES * 16, 128), F32),
        ],
        compiler_params=pltpu.CompilerParams(vmem_limit_bytes=LIMIT),
        name="fourier",
    )(keep, other, inner, outer)
    message = lax.all_to_all(
        message.reshape(DEVICES, 16, 128), ("lat", "wave"), split_axis=0, concat_axis=0, tiled=True
    )
    owner = lat_place * ring + wave_place
    own_waves = lax.dynamic_slice_in_dim(wave_order, owner * SLOTS, SLOTS)
    degrees = legendre.shape[2]
    return pl.pallas_call(
        legendre_kernel,
        grid=(SLOTS,),
        out_shape=jax.ShapeDtypeStruct((SLOTS, 2 * SLICES, degrees), F32),
        in_specs=[
            SMEM,
            pl.BlockSpec((DEVICES, 16, 128), lambda s: (0, 0, 0)),
            pl.BlockSpec((1, 128, degrees), lambda s: (s, 0, 0)),
        ],
        out_specs=pl.BlockSpec((1, 2 * SLICES, degrees), lambda s: (s, 0, 0)),
        scratch_shapes=[
            pltpu.VMEM((512, 128), F32),
            pltpu.VMEM((512, 128), F32),
            pltpu.VMEM((512, 128), BF16),
        ],
        compiler_params=pltpu.CompilerParams(vmem_limit_bytes=LIMIT),
        name="legendre",
    )(own_waves, message, legendre)


def solution(mesh):
    placed = (
        P(None, "lat", "wave"),
        P("lat"),
        P(),
        P("lat", "wave"),
        P("lat", "wave"),
        P("lat", "wave"),
        P("lat", "wave"),
        P(("lat", "wave"), None, None),
    )
    return jax.shard_map(
        local, mesh=mesh, in_specs=placed, out_specs=P(("lat", "wave"), None, None), check_vma=False
    )
```

```python
import math

import jax
import jax.numpy as jnp
from jax import lax
from jax.experimental import pallas as pl
from jax.experimental.pallas import tpu as pltpu
from jax.sharding import PartitionSpec as P

F32 = jnp.float32
BF16 = jnp.bfloat16
VMEM = pl.BlockSpec(memory_space=pltpu.VMEM)
SMEM = pl.BlockSpec(memory_space=pltpu.SMEM)
LIMIT = 24 * 1024 * 1024

SLICES = 24
BAND = 8
WIDE = 640
BLOCKS = 5
SLOTS = 10
DEVICES = 128
ROWS = 4
STACK = 128


def cubic_weights(fraction):
    return (
        -fraction * (fraction - 1.0) * (fraction - 2.0) / 6.0,
        (fraction + 1.0) * (fraction - 1.0) * (fraction - 2.0) / 2.0,
        -(fraction + 1.0) * fraction * (fraction - 2.0) / 2.0,
        (fraction + 1.0) * fraction * (fraction - 1.0) / 6.0,
    )


def picked_weight(distance, weights):
    chosen = jnp.where(distance == 3, weights[3], 0.0)
    for step in (2, 1, 0):
        chosen = jnp.where(distance == step, weights[step], chosen)
    return chosen


def interpolate_kernel(
    place, live, own, above, below, columns, rows_of, keep, send, main, edge, stack
):
    count = BAND * SLICES
    for part, ref in enumerate((above, own, below)):
        rows = pl.ds(part * count, count)
        main[rows, :] = ref[:, :WIDE]
        for block in range(BLOCKS):
            right = block + 1
            left = block - 1 if block else BLOCKS
            edge[rows, 128 * block : 128 * block + 128] = jnp.concatenate(
                [ref[:, 128 * right : 128 * right + 64], ref[:, 128 * left + 64 : 128 * left + 128]],
                axis=1,
            )
    core = place[0]

    def one_pair(step, carry):
        pair = step ^ (2 * core)
        window = pl.ds(pl.multiple_of(pair * (2 * SLICES), 2 * SLICES), 18 * SLICES)
        for block in range(BLOCKS):
            lanes = slice(128 * block, 128 * block + 128)
            left = jnp.concatenate([main[window, lanes], edge[window, lanes]], axis=1)
            spread = jnp.dot(left, columns[pair, block], preferred_element_type=F32)
            for half in range(2):
                side = slice(128 * half, 128 * half + 128)
                total = jnp.zeros((SLICES, 128), F32)
                for row in range(half, half + 17):
                    total = total + rows_of[pair, block, row : row + 1, side] * spread[
                        SLICES * row : SLICES * row + SLICES, side
                    ]
                position = lax.broadcasted_iota(jnp.int32, (SLICES, 128), 1) + 128 * block
                total = jnp.where(position < live[2 * pair + half], total, 0.0)
                stack[2 * step + half, SLICES * block : SLICES * block + SLICES, :] = total
        return carry

    for row in range(BAND):
        stack[row, BLOCKS * SLICES :, :] = jnp.zeros((STACK - BLOCKS * SLICES, 128), F32)
    lax.fori_loop(0, BAND // 2, one_pair, 0)
    keep[...] = stack[0:ROWS].astype(BF16)
    send[...] = stack[ROWS:].astype(BF16)


def turn(count, length, inverse):
    whole = jnp.floor(count * inverse + 0.5)
    angle = (count - whole * length) * (inverse * math.pi)
    square = angle * angle
    sine = angle * (
        1.0
        + square
        * (
            -1.0 / 6
            + square
            * (1.0 / 120 + square * (-1.0 / 5040 + square * (1.0 / 362880 - square / 39916800)))
        )
    )
    cosine = 1.0 + square * (
        -0.5
        + square
        * (
            1.0 / 24
            + square
            * (-1.0 / 720 + square * (1.0 / 40320 + square * (-1.0 / 3628800 + square / 479001600)))
        )
    )
    return 1.0 - 2.0 * sine * sine, 2.0 * sine * cosine


def rotated(one, two):
    return one[0] * two[0] - one[1] * two[1], one[1] * two[0] + one[0] * two[1]


def table_kernel(
    place, lengths, waves, depart_row, depart_col, frac_row, frac_col,
    inner, outer, columns, rows_of, points,
):
    wave_place = place[1]
    step = lax.broadcasted_iota(jnp.int32, (8, 128), 0)
    away = ((wave_place ^ 1) - wave_place) * WIDE
    shift = jnp.where(step == 5, away, jnp.where(step == 6, 64, 128 * step + wave_place * WIDE))
    shift = shift.astype(F32)
    fine = step.astype(F32)

    def one(index, carry):
        row = index // SLOTS
        slot = index % SLOTS
        length = jnp.full((1, 128), lengths[row], jnp.int32).astype(F32)
        inverse = 1.0 / length
        wave = waves[pl.ds(slot, 1), :]
        lanes = pl.ds(pl.multiple_of(slot * 256, 256), 128)
        lanes_two = pl.ds(pl.multiple_of(slot * 256 + 128, 128), 128)
        moved = turn(shift * wave, length, inverse)
        norm = lax.rsqrt(length)
        outer[row, :, lanes] = moved[0] * norm
        outer[row, :, lanes_two] = moved[1] * norm
        other = [part[5:6] for part in moved]
        half = [part[6:7] for part in moved]
        small = turn(fine * wave, length, inverse)
        low = turn(8.0 * fine * wave, length, inverse)
        for tile in range(2):
            if tile:
                low = rotated(low, other)
            high = rotated(low, half)
            for coarse in range(0, 16, 2):
                source = low if coarse < 8 else high
                at = coarse % 8
                pairs = [
                    rotated([part[k : k + 1] for part in source], small) for k in (at, at + 1)
                ]
                rows = slice(128 * tile + 8 * coarse, 128 * tile + 8 * coarse + 16)
                for side, to in enumerate((lanes, lanes_two)):
                    inner[row, rows, to] = jnp.concatenate(
                        [pair[side] for pair in pairs], axis=0
                    ).astype(BF16)
        return carry

    lax.fori_loop(0, ROWS * SLOTS, one, 0)

    lane = lax.broadcasted_iota(jnp.int32, (1, WIDE), 1) % 128
    for base, first, fraction in (
        (0, depart_col[...] + lane - 1, frac_col),
        (8, depart_row[...] + (BAND - 1), frac_row),
    ):
        for k, value in enumerate((first.astype(F32),) + cubic_weights(fraction[...])):
            for row in range(BAND):
                points[row, base + k : base + k + 1, :] = value[row : row + 1, :]

    def one_pair(pair, carry):
        def row_of(item, block):
            return jnp.concatenate(
                [
                    points[2 * pair + half, item : item + 1, 128 * block : 128 * block + 128]
                    for half in range(2)
                ],
                axis=1,
            )

        for block in range(BLOCKS):
            start = row_of(0, block)
            weights = [row_of(1 + k, block) for k in range(4)]
            source = lax.broadcasted_iota(jnp.int32, (144, 256), 0).astype(F32)
            columns[pair, block, 0:144, :] = picked_weight(source - start, weights).astype(BF16)
            columns[pair, block, 144:240, :] = jnp.zeros((96, 256), BF16)
            source = lax.broadcasted_iota(jnp.int32, (16, 256), 0).astype(F32) - 16.0
            columns[pair, block, 240:256, :] = picked_weight(source - start, weights).astype(BF16)
            half = (lax.broadcasted_iota(jnp.int32, (1, 256), 1) >= 128).astype(F32)
            start = row_of(8, block) + half
            weights = [row_of(9 + k, block) for k in range(4)]
            source = lax.broadcasted_iota(jnp.int32, (24, 256), 0).astype(F32)
            rows_of[pair, block] = picked_weight(source - start, weights)
        return carry

    lax.fori_loop(0, BAND // 2, one_pair, 0)


def fourier_kernel(mine, other, inner, outer, message, sums, shuffled):
    def one(row, carry):
        left = jnp.concatenate([mine[row], other[row]], axis=1)
        base = pl.multiple_of(row * 512, 512)
        sums[pl.ds(base + 480, 32), :] = jnp.zeros((32, 128), F32)
        for slot in range(SLOTS):
            lanes = slice(256 * slot, 256 * slot + 256)
            parts = jnp.dot(left, inner[row, :, lanes], preferred_element_type=F32)
            real = jnp.zeros((SLICES, 128), F32)
            imag = jnp.zeros((SLICES, 128), F32)
            for block in range(BLOCKS):
                rows = slice(SLICES * block, SLICES * block + SLICES)
                cosine, sine = parts[rows, :128], parts[rows, 128:]
                c = outer[row, block : block + 1, 256 * slot : 256 * slot + 128]
                s = outer[row, block : block + 1, 256 * slot + 128 : 256 * slot + 256]
                real = real + (c * cosine - s * sine)
                imag = imag - (s * cosine + c * sine)
            sums[pl.ds(base + slot * 48, SLICES, stride=2), :] = real
            sums[pl.ds(base + slot * 48 + 1, SLICES, stride=2), :] = imag
        return carry

    lax.fori_loop(0, ROWS, one, 0)
    for part in range(16):
        shuffled[pl.ds(part, DEVICES, stride=16), :] = sums[128 * part : 128 * part + 128, :].T
    message[...] = shuffled[...].astype(BF16)


def legendre_kernel(place, waves, message, table, out, flat, sorted_rows, left, result, done):
    for band in range(16):
        for core in range(2):
            total = message[8 * band + core].astype(F32)
            for z in range(1, 4):
                total = total + message[8 * band + 2 * z + core].astype(F32)
            first = (2 * band + core) * 16
            flat[first : first + 16, :] = total
    for row in range(ROWS):
        for part in range(4):
            sorted_rows[pl.ds(128 * part + row, 32, stride=4), :] = flat[
                pl.ds(4 * row + part, 32, stride=16), :
            ]
    for part in range(4):
        rows = slice(128 * part, 128 * part + 128)
        left[rows, :] = sorted_rows[rows, :].T.astype(BF16)
    copies = []
    for slot in range(SLOTS):
        product = jnp.dot(left[48 * slot : 48 * slot + 48, :], table[slot], preferred_element_type=F32)
        degree = lax.broadcasted_iota(jnp.int32, product.shape, 1)
        result[slot] = jnp.where(degree >= waves[place[2] + slot], product, 0.0)
        copy = pltpu.make_async_copy(result.at[slot], out.at[slot], done.at[slot])
        copy.start()
        copies.append(copy)
    for copy in copies:
        copy.wait()


def local(fields, row_length, wave_order, depart_row, depart_col, frac_row, frac_col, legendre):
    wave_place = lax.axis_index("wave")
    lat_place = lax.axis_index("lat")
    core = wave_place % 2
    column_start = wave_place * WIDE
    live = row_length - column_start
    live_mask = jnp.arange(WIDE, dtype=jnp.int32)[None, :] < live[:, None]
    masked = jnp.where(live_mask[None], fields, jnp.zeros_like(fields))
    own = masked.transpose(1, 0, 2).reshape(BAND * SLICES, WIDE)
    ring = lax.axis_size("wave")
    first_slot = (lat_place * ring + wave_place) * SLOTS
    place = jnp.stack([core, wave_place, first_slot]).astype(jnp.int32)

    from_left = lax.ppermute(
        own[:, WIDE - 128 :], "wave", [(i, (i + 1) % ring) for i in range(ring)]
    )
    from_right = lax.ppermute(own[:, :128], "wave", [((i + 1) % ring, i) for i in range(ring)])
    rim = jnp.concatenate([from_right[:, :64], from_left[:, 64:]], axis=1)
    own = jnp.concatenate([own, rim], axis=1)
    bands = lax.axis_size("lat")
    above = lax.ppermute(own, "lat", [(i, i + 1) for i in range(bands - 1)])
    below = lax.ppermute(own, "lat", [(i + 1, i) for i in range(bands - 1)])

    lengths = lax.dynamic_slice_in_dim(row_length, core * ROWS, ROWS)
    ordered = wave_order.reshape(DEVICES, SLOTS).T.astype(F32)
    inner, outer, columns, rows_of = pl.pallas_call(
        table_kernel,
        out_shape=(
            jax.ShapeDtypeStruct((ROWS, 256, SLOTS * 256), BF16),
            jax.ShapeDtypeStruct((ROWS, 8, SLOTS * 256), F32),
            jax.ShapeDtypeStruct((BAND // 2, BLOCKS, 256, 256), BF16),
            jax.ShapeDtypeStruct((BAND // 2, BLOCKS, 24, 256), F32),
        ),
        in_specs=[SMEM, SMEM] + [VMEM] * 5,
        out_specs=(VMEM,) * 4,
        scratch_shapes=[pltpu.VMEM((BAND, 16, WIDE), F32)],
        compiler_params=pltpu.CompilerParams(vmem_limit_bytes=LIMIT),
        cost_estimate=pl.CostEstimate(flops=5_000_000_000, bytes_accessed=3_000_000, transcendentals=0),
        name="tables",
    )(place, lengths, ordered, depart_row, depart_col, frac_row, frac_col)

    keep, send = pl.pallas_call(
        interpolate_kernel,
        out_shape=(jax.ShapeDtypeStruct((ROWS, STACK, 128), BF16),) * 2,
        in_specs=[SMEM, SMEM] + [VMEM] * 5,
        out_specs=(VMEM, VMEM),
        scratch_shapes=[
            pltpu.VMEM((3 * BAND * SLICES, WIDE), BF16),
            pltpu.VMEM((3 * BAND * SLICES, WIDE), BF16),
            pltpu.VMEM((BAND, STACK, 128), F32),
        ],
        compiler_params=pltpu.CompilerParams(vmem_limit_bytes=LIMIT),
        name="interpolate",
    )(place, live, own, above, below, columns, rows_of)

    other = lax.ppermute(send, "wave", [(i, i ^ 1) for i in range(ring)])
    message = pl.pallas_call(
        fourier_kernel,
        out_shape=jax.ShapeDtypeStruct((DEVICES * 16, 128), BF16),
        in_specs=[VMEM] * 4,
        out_specs=VMEM,
        scratch_shapes=[
            pltpu.VMEM((ROWS * 512, 128), F32),
            pltpu.VMEM((DEVICES * 16, 128), F32),
        ],
        compiler_params=pltpu.CompilerParams(vmem_limit_bytes=LIMIT),
        name="fourier",
    )(keep, other, inner, outer)
    message = lax.all_to_all(
        message.reshape(DEVICES, 16, 128), ("lat", "wave"), split_axis=0, concat_axis=0, tiled=True
    )
    degrees = legendre.shape[2]
    return pl.pallas_call(
        legendre_kernel,
        out_shape=jax.ShapeDtypeStruct((SLOTS, 2 * SLICES, degrees), F32),
        in_specs=[SMEM, SMEM, VMEM, VMEM],
        out_specs=pl.BlockSpec(memory_space=pl.ANY),
        scratch_shapes=[
            pltpu.VMEM((512, 128), F32),
            pltpu.VMEM((512, 128), F32),
            pltpu.VMEM((512, 128), BF16),
            pltpu.VMEM((SLOTS, 2 * SLICES, degrees), F32),
            pltpu.SemaphoreType.DMA((SLOTS,)),
        ],
        compiler_params=pltpu.CompilerParams(vmem_limit_bytes=LIMIT),
        name="legendre",
    )(place, wave_order, message, legendre)


def solution(mesh):
    placed = (
        P(None, "lat", "wave"),
        P("lat"),
        P(),
        P("lat", "wave"),
        P("lat", "wave"),
        P("lat", "wave"),
        P("lat", "wave"),
        P(("lat", "wave"), None, None),
    )
    return jax.shard_map(
        local, mesh=mesh, in_specs=placed, out_specs=P(("lat", "wave"), None, None), check_vma=False
    )
```

```python
import math

import jax
import jax.numpy as jnp
from jax import lax
from jax.experimental import pallas as pl
from jax.experimental.pallas import tpu as pltpu
from jax.sharding import PartitionSpec as P

F32 = jnp.float32
BF16 = jnp.bfloat16
VMEM = pl.BlockSpec(memory_space=pltpu.VMEM)
SMEM = pl.BlockSpec(memory_space=pltpu.SMEM)
LIMIT = 24 * 1024 * 1024

SLICES = 24
BAND = 8
WIDE = 640
BLOCKS = 5
SLOTS = 10
DEVICES = 128
ROWS = 4
STACK = 128
COUNT = 3 * BAND * SLICES
GROUP = 48
LENGTHS = 4


def cubic_weights(fraction):
    return (
        -fraction * (fraction - 1.0) * (fraction - 2.0) / 6.0,
        (fraction + 1.0) * (fraction - 1.0) * (fraction - 2.0) / 2.0,
        -(fraction + 1.0) * fraction * (fraction - 2.0) / 2.0,
        (fraction + 1.0) * fraction * (fraction - 1.0) / 6.0,
    )


def picked_weight(distance, weights):
    chosen = jnp.where(distance == 3, weights[3], 0.0)
    for step in (2, 1, 0):
        chosen = jnp.where(distance == step, weights[step], chosen)
    return chosen


def pack_kernel(place, own, first, second, main, to_left, to_right):
    size = BAND * SLICES
    odd = place[3]
    main[pl.ds(pl.multiple_of(odd * 2 * size, size), size), :] = first[...]
    main[size : 2 * size, :] = own[...]
    main[pl.ds(pl.multiple_of((1 - odd) * 2 * size, size), size), :] = second[...]
    lane = lax.broadcasted_iota(jnp.int32, (GROUP, 128), 1)
    left = jnp.zeros((GROUP, 128), F32)
    right = jnp.zeros((GROUP, 128), F32)
    for group in range(COUNT // GROUP):
        rows = slice(GROUP * group, GROUP * group + GROUP)
        head = jnp.where(lane < 8, main[rows, :128].astype(F32), 0.0)
        tail = jnp.where(lane >= 120, main[rows, WIDE - 128 :].astype(F32), 0.0)
        left = left + pltpu.roll(head, 8 * group, 1)
        right = right + pltpu.roll(tail, 8 * group + 8, 1)
    to_left[...] = left.astype(BF16)
    to_right[...] = right.astype(BF16)


def weighted(spread, rows_of, half):
    side = slice(128 * half, 128 * half + 128)
    total = jnp.zeros((SLICES, 128), F32)
    for row in range(half, half + 17):
        total = total + rows_of[row : row + 1, side] * spread[
            SLICES * row : SLICES * row + SLICES, side
        ]
    return total


def interior_kernel(place, main, columns, rows_of, stack, edge):
    for block in range(BLOCKS):
        sides = [
            main[:, 128 * block + 128 : 128 * block + 192]
            if block < BLOCKS - 1
            else jnp.zeros((COUNT, 64), BF16),
            main[:, 128 * block - 64 : 128 * block] if block else jnp.zeros((COUNT, 64), BF16),
        ]
        edge[:, 128 * block : 128 * block + 128] = jnp.concatenate(sides, axis=1)
    for row in range(BAND):
        stack[row, BLOCKS * SLICES :, :] = jnp.zeros((STACK - BLOCKS * SLICES, 128), F32)
    core = place[0]
    start = place[1] * WIDE

    def one_pair(step, carry):
        pair = step ^ (2 * core)
        window = pl.ds(pl.multiple_of(pair * (2 * SLICES), 2 * SLICES), 18 * SLICES)
        for block in range(BLOCKS):
            lanes = slice(128 * block, 128 * block + 128)
            left = jnp.concatenate([main[window, lanes], edge[window, lanes]], axis=1)
            spread = jnp.dot(left, columns[pair, block], preferred_element_type=F32)
            position = lax.broadcasted_iota(jnp.int32, (SLICES, 128), 1) + 128 * block
            for half in range(2):
                total = weighted(spread, rows_of.at[pair, block], half)
                live = place[LENGTHS + 2 * pair + half] - start
                total = jnp.where(position < live, total, 0.0)
                stack[2 * step + half, SLICES * block : SLICES * block + SLICES, :] = total
        return carry

    lax.fori_loop(0, BAND // 2, one_pair, 0)


def border_kernel(
    place, from_left, from_right, wrap_columns, wrap_rows, stack, keep, send, edge, extra
):
    lane = lax.broadcasted_iota(jnp.int32, (GROUP, 128), 1)
    left = from_left[...].astype(F32)
    right = from_right[...].astype(F32)
    for group in range(COUNT // GROUP):
        one = pltpu.roll(right, (128 - 8 * group) % 128, 1)
        two = pltpu.roll(left, 120 - 8 * group, 1)
        edge[GROUP * group : GROUP * group + GROUP, :] = jnp.where(lane < 64, one, two).astype(BF16)
    core = place[0]
    start = place[1] * WIDE
    column = lax.broadcasted_iota(jnp.int32, (SLICES, 128), 1)
    position = jnp.where(column < 64, column, column + (WIDE - 128))

    def one_pair(step, carry):
        pair = step ^ (2 * core)
        window = pl.ds(pl.multiple_of(pair * (2 * SLICES), 2 * SLICES), 18 * SLICES)
        spread = jnp.dot(edge[window, :], wrap_columns[pair], preferred_element_type=F32)
        for half in range(2):
            total = weighted(spread, wrap_rows.at[pair], half)
            live = place[LENGTHS + 2 * pair + half] - start
            extra[2 * step + half] = jnp.where(position < live, total, 0.0)
        return carry

    lax.fori_loop(0, BAND // 2, one_pair, 0)
    last = SLICES * (BLOCKS - 1)
    for ref, first in ((keep, 0), (send, ROWS)):
        for row in range(ROWS):
            more = extra[first + row]
            full = stack[first + row]
            full = jnp.concatenate(
                [
                    full[:SLICES] + jnp.where(column < 64, more, 0.0),
                    full[SLICES:last],
                    full[last : last + SLICES] + jnp.where(column >= 64, more, 0.0),
                    full[last + SLICES :],
                ],
                axis=0,
            )
            ref[row] = full.astype(BF16)


def turn(count, length, inverse):
    whole = jnp.floor(count * inverse + 0.5)
    angle = (count - whole * length) * (inverse * math.pi)
    square = angle * angle
    sine = angle * (
        1.0
        + square
        * (
            -1.0 / 6
            + square
            * (1.0 / 120 + square * (-1.0 / 5040 + square * (1.0 / 362880 - square / 39916800)))
        )
    )
    cosine = 1.0 + square * (
        -0.5
        + square
        * (
            1.0 / 24
            + square
            * (-1.0 / 720 + square * (1.0 / 40320 + square * (-1.0 / 3628800 + square / 479001600)))
        )
    )
    return 1.0 - 2.0 * sine * sine, 2.0 * sine * cosine


def rotated(one, two):
    return one[0] * two[0] - one[1] * two[1], one[1] * two[0] + one[0] * two[1]


def table_kernel(
    place, waves, stencil, inner, outer, columns, rows_of, wrap_columns, wrap_rows, points
):
    first_row = place[0] * ROWS
    wave_place = place[1]
    step = lax.broadcasted_iota(jnp.int32, (8, 128), 0)
    away = ((wave_place ^ 1) - wave_place) * WIDE
    shift = jnp.where(step == 5, away, jnp.where(step == 6, 64, 128 * step + wave_place * WIDE))
    shift = shift.astype(F32)
    fine = step.astype(F32)

    def one(index, carry):
        row = index // SLOTS
        slot = index % SLOTS
        length = jnp.full((1, 128), place[LENGTHS + first_row + row], jnp.int32).astype(F32)
        inverse = 1.0 / length
        wave = waves[pl.ds(slot, 1), :]
        lanes = pl.ds(pl.multiple_of(slot * 256, 256), 128)
        lanes_two = pl.ds(pl.multiple_of(slot * 256 + 128, 128), 128)
        moved = turn(shift * wave, length, inverse)
        norm = lax.rsqrt(length)
        outer[row, :, lanes] = moved[0] * norm
        outer[row, :, lanes_two] = moved[1] * norm
        other = [part[5:6] for part in moved]
        half = [part[6:7] for part in moved]
        small = turn(fine * wave, length, inverse)
        low = turn(8.0 * fine * wave, length, inverse)
        for tile in range(2):
            if tile:
                low = rotated(low, other)
            high = rotated(low, half)
            for coarse in range(0, 16, 2):
                source = low if coarse < 8 else high
                at = coarse % 8
                pairs = [
                    rotated([part[k : k + 1] for part in source], small) for k in (at, at + 1)
                ]
                rows = slice(128 * tile + 8 * coarse, 128 * tile + 8 * coarse + 16)
                for side, to in enumerate((lanes, lanes_two)):
                    inner[row, rows, to] = jnp.concatenate(
                        [pair[side] for pair in pairs], axis=0
                    ).astype(BF16)
        return carry

    lax.fori_loop(0, ROWS * SLOTS, one, 0)

    lane = lax.broadcasted_iota(jnp.int32, (1, WIDE), 1) % 128
    for base, first, fraction in (
        (0, stencil[1] + (lane - 1).astype(F32), stencil[3]),
        (8, stencil[0] + (BAND - 1.0), stencil[2]),
    ):
        for k, value in enumerate((first,) + cubic_weights(fraction)):
            for row in range(BAND):
                points[row, base + k : base + k + 1, :] = value[row : row + 1, :]

    def one_pair(pair, carry):
        def row_of(item, block):
            return jnp.concatenate(
                [
                    points[2 * pair + half, item : item + 1, 128 * block : 128 * block + 128]
                    for half in range(2)
                ],
                axis=1,
            )

        for block in range(BLOCKS):
            start = row_of(0, block)
            weights = [row_of(1 + k, block) for k in range(4)]
            source = lax.broadcasted_iota(jnp.int32, (144, 256), 0).astype(F32)
            columns[pair, block, 0:144, :] = picked_weight(source - start, weights).astype(BF16)
            columns[pair, block, 144:240, :] = jnp.zeros((96, 256), BF16)
            source = lax.broadcasted_iota(jnp.int32, (16, 256), 0).astype(F32) - 16.0
            columns[pair, block, 240:256, :] = picked_weight(source - start, weights).astype(BF16)
            half = (lax.broadcasted_iota(jnp.int32, (1, 256), 1) >= 128).astype(F32)
            start = row_of(8, block) + half
            weights = [row_of(9 + k, block) for k in range(4)]
            source = lax.broadcasted_iota(jnp.int32, (24, 256), 0).astype(F32)
            rows_of[pair, block] = picked_weight(source - start, weights)
        ends = (0, BLOCKS - 1, 0, BLOCKS - 1)
        wrap_columns[pair] = jnp.concatenate(
            [columns[pair, end, 128:, 64 * k : 64 * k + 64] for k, end in enumerate(ends)], axis=1
        )
        side = lax.broadcasted_iota(jnp.int32, (24, 256), 1) % 128
        wrap_rows[pair] = jnp.where(side < 64, rows_of[pair, 0], rows_of[pair, BLOCKS - 1])
        return carry

    lax.fori_loop(0, BAND // 2, one_pair, 0)


def fourier_kernel(mine, other, inner, outer, message, sums, shuffled):
    def one(row, carry):
        left = jnp.concatenate([mine[row], other[row]], axis=1)
        base = pl.multiple_of(row * 512, 512)
        sums[pl.ds(base + 480, 32), :] = jnp.zeros((32, 128), F32)
        for slot in range(SLOTS):
            lanes = slice(256 * slot, 256 * slot + 256)
            parts = jnp.dot(left, inner[row, :, lanes], preferred_element_type=F32)
            real = jnp.zeros((SLICES, 128), F32)
            imag = jnp.zeros((SLICES, 128), F32)
            for block in range(BLOCKS):
                rows = slice(SLICES * block, SLICES * block + SLICES)
                cosine, sine = parts[rows, :128], parts[rows, 128:]
                c = outer[row, block : block + 1, 256 * slot : 256 * slot + 128]
                s = outer[row, block : block + 1, 256 * slot + 128 : 256 * slot + 256]
                real = real + (c * cosine - s * sine)
                imag = imag - (s * cosine + c * sine)
            sums[pl.ds(base + slot * 48, SLICES, stride=2), :] = real
            sums[pl.ds(base + slot * 48 + 1, SLICES, stride=2), :] = imag
        return carry

    lax.fori_loop(0, ROWS, one, 0)
    for part in range(16):
        shuffled[pl.ds(part, DEVICES, stride=16), :] = sums[128 * part : 128 * part + 128, :].T
    message[...] = shuffled[...].astype(BF16)


def legendre_kernel(place, waves, message, table, out, flat, sorted_rows, left, result, done):
    for band in range(16):
        for core in range(2):
            total = message[8 * band + core].astype(F32)
            for z in range(1, 4):
                total = total + message[8 * band + 2 * z + core].astype(F32)
            first = (2 * band + core) * 16
            flat[first : first + 16, :] = total
    for row in range(ROWS):
        for part in range(4):
            sorted_rows[pl.ds(128 * part + row, 32, stride=4), :] = flat[
                pl.ds(4 * row + part, 32, stride=16), :
            ]
    for part in range(4):
        rows = slice(128 * part, 128 * part + 128)
        left[rows, :] = sorted_rows[rows, :].T.astype(BF16)
    copies = []
    for slot in range(SLOTS):
        product = jnp.dot(left[48 * slot : 48 * slot + 48, :], table[slot], preferred_element_type=F32)
        degree = lax.broadcasted_iota(jnp.int32, product.shape, 1)
        result[slot] = jnp.where(degree >= waves[place[2] + slot], product, 0.0)
        copy = pltpu.make_async_copy(result.at[slot], out.at[slot], done.at[slot])
        copy.start()
        copies.append(copy)
    for copy in copies:
        copy.wait()


def local(fields, row_length, wave_order, depart_row, depart_col, frac_row, frac_col, legendre):
    wave_place = lax.axis_index("wave")
    lat_place = lax.axis_index("lat")
    ring = lax.axis_size("wave")
    bands = lax.axis_size("lat")
    first_slot = (lat_place * ring + wave_place) * SLOTS
    own_place = jnp.stack([wave_place % 2, wave_place, first_slot, lat_place % 2])
    place = jnp.concatenate([own_place.astype(jnp.int32), row_length])
    limit = place[LENGTHS:] - wave_place * WIDE
    live_mask = jnp.arange(WIDE, dtype=jnp.int32)[None, :] < limit[:, None]
    masked = jnp.where(live_mask[None], fields, jnp.zeros_like(fields))
    own = masked.transpose(1, 0, 2).reshape(BAND * SLICES, WIDE)

    def swapped(first):
        pairs = [(i, i + 1) for i in range(first, bands - 1, 2)]
        return lax.ppermute(own, "lat", pairs + [(j, i) for i, j in pairs])

    over = swapped(1)
    under = swapped(0)

    stencil = jnp.stack([depart_row.astype(F32), depart_col.astype(F32), frac_row, frac_col])
    ordered = wave_order.reshape(DEVICES, SLOTS).T.astype(F32)
    inner, outer, columns, rows_of, wrap_columns, wrap_rows = pl.pallas_call(
        table_kernel,
        out_shape=(
            jax.ShapeDtypeStruct((ROWS, 256, SLOTS * 256), BF16),
            jax.ShapeDtypeStruct((ROWS, 8, SLOTS * 256), F32),
            jax.ShapeDtypeStruct((BAND // 2, BLOCKS, 256, 256), BF16),
            jax.ShapeDtypeStruct((BAND // 2, BLOCKS, 24, 256), F32),
            jax.ShapeDtypeStruct((BAND // 2, 128, 256), BF16),
            jax.ShapeDtypeStruct((BAND // 2, 24, 256), F32),
        ),
        in_specs=[SMEM, VMEM, VMEM],
        out_specs=(VMEM,) * 6,
        scratch_shapes=[pltpu.VMEM((BAND, 16, WIDE), F32)],
        compiler_params=pltpu.CompilerParams(vmem_limit_bytes=LIMIT),
        cost_estimate=pl.CostEstimate(flops=5_000_000_000, bytes_accessed=3_000_000, transcendentals=0),
        name="tables",
    )(place, ordered, stencil)

    main, to_left, to_right = pl.pallas_call(
        pack_kernel,
        out_shape=(
            jax.ShapeDtypeStruct((COUNT, WIDE), BF16),
            jax.ShapeDtypeStruct((GROUP, 128), BF16),
            jax.ShapeDtypeStruct((GROUP, 128), BF16),
        ),
        in_specs=[SMEM] + [VMEM] * 3,
        out_specs=(VMEM,) * 3,
        compiler_params=pltpu.CompilerParams(vmem_limit_bytes=LIMIT),
        name="pack",
    )(place, own, over, under)
    from_left = lax.ppermute(to_right, "wave", [(i, (i + 1) % ring) for i in range(ring)])
    from_right = lax.ppermute(to_left, "wave", [((i + 1) % ring, i) for i in range(ring)])
    stack = pl.pallas_call(
        interior_kernel,
        out_shape=jax.ShapeDtypeStruct((BAND, STACK, 128), F32),
        in_specs=[SMEM] + [VMEM] * 3,
        out_specs=VMEM,
        scratch_shapes=[pltpu.VMEM((COUNT, WIDE), BF16)],
        compiler_params=pltpu.CompilerParams(vmem_limit_bytes=LIMIT),
        cost_estimate=pl.CostEstimate(flops=5_000_000_000, bytes_accessed=3_000_000, transcendentals=0),
        name="interior",
    )(place, main, columns, rows_of)
    keep, send = pl.pallas_call(
        border_kernel,
        out_shape=(jax.ShapeDtypeStruct((ROWS, STACK, 128), BF16),) * 2,
        in_specs=[SMEM] + [VMEM] * 5,
        out_specs=(VMEM, VMEM),
        scratch_shapes=[pltpu.VMEM((COUNT, 128), BF16), pltpu.VMEM((BAND, SLICES, 128), F32)],
        compiler_params=pltpu.CompilerParams(vmem_limit_bytes=LIMIT),
        name="border",
    )(place, from_left, from_right, wrap_columns, wrap_rows, stack)

    other = lax.ppermute(send, "wave", [(i, i ^ 1) for i in range(ring)])
    message = pl.pallas_call(
        fourier_kernel,
        out_shape=jax.ShapeDtypeStruct((DEVICES * 16, 128), BF16),
        in_specs=[VMEM] * 4,
        out_specs=VMEM,
        scratch_shapes=[
            pltpu.VMEM((ROWS * 512, 128), F32),
            pltpu.VMEM((DEVICES * 16, 128), F32),
        ],
        compiler_params=pltpu.CompilerParams(vmem_limit_bytes=LIMIT),
        name="fourier",
    )(keep, other, inner, outer)
    message = lax.all_to_all(
        message.reshape(DEVICES, 16, 128), ("lat", "wave"), split_axis=0, concat_axis=0, tiled=True
    )
    degrees = legendre.shape[2]
    return pl.pallas_call(
        legendre_kernel,
        out_shape=jax.ShapeDtypeStruct((SLOTS, 2 * SLICES, degrees), F32),
        in_specs=[SMEM, SMEM, VMEM, VMEM],
        out_specs=pl.BlockSpec(memory_space=pl.ANY),
        scratch_shapes=[
            pltpu.VMEM((512, 128), F32),
            pltpu.VMEM((512, 128), F32),
            pltpu.VMEM((512, 128), BF16),
            pltpu.VMEM((SLOTS, 2 * SLICES, degrees), F32),
            pltpu.SemaphoreType.DMA((SLOTS,)),
        ],
        compiler_params=pltpu.CompilerParams(vmem_limit_bytes=LIMIT),
        name="legendre",
    )(place, wave_order, message, legendre)


def solution(mesh):
    placed = (
        P(None, "lat", "wave"),
        P("lat"),
        P(),
        P("lat", "wave"),
        P("lat", "wave"),
        P("lat", "wave"),
        P("lat", "wave"),
        P(("lat", "wave"), None, None),
    )
    return jax.shard_map(
        local, mesh=mesh, in_specs=placed, out_specs=P(("lat", "wave"), None, None), check_vma=False
    )
```

```python
import math

import jax
import jax.numpy as jnp
from jax import lax
from jax.experimental import pallas as pl
from jax.experimental.pallas import tpu as pltpu
from jax.sharding import PartitionSpec as P

F32 = jnp.float32
BF16 = jnp.bfloat16
VMEM = pl.BlockSpec(memory_space=pltpu.VMEM)
SMEM = pl.BlockSpec(memory_space=pltpu.SMEM)
LIMIT = 24 * 1024 * 1024

SLICES = 24
BAND = 8
WIDE = 640
BLOCKS = 5
SLOTS = 10
DEVICES = 128
ROWS = 4
STACK = 128
COUNT = 3 * BAND * SLICES
GROUP = 48
LENGTHS = 4


def cubic_weights(fraction):
    return (
        -fraction * (fraction - 1.0) * (fraction - 2.0) / 6.0,
        (fraction + 1.0) * (fraction - 1.0) * (fraction - 2.0) / 2.0,
        -(fraction + 1.0) * fraction * (fraction - 2.0) / 2.0,
        (fraction + 1.0) * fraction * (fraction - 1.0) / 6.0,
    )


def picked_weight(distance, weights):
    chosen = jnp.where(distance == 3, weights[3], jnp.zeros_like(weights[3]))
    for step in (2, 1, 0):
        chosen = jnp.where(distance == step, weights[step], chosen)
    return chosen


def pack_kernel(own, first, second, main, to_left, to_right):
    size = BAND * SLICES
    odd = lax.axis_index("lat") % 2
    main[pl.ds(pl.multiple_of(odd * 2 * size, size), size), :] = first[...]
    main[size : 2 * size, :] = own[...]
    main[pl.ds(pl.multiple_of((1 - odd) * 2 * size, size), size), :] = second[...]
    lane = lax.broadcasted_iota(jnp.int32, (GROUP, 128), 1)
    left = jnp.zeros((GROUP, 128), F32)
    right = jnp.zeros((GROUP, 128), F32)
    for group in range(COUNT // GROUP):
        rows = slice(GROUP * group, GROUP * group + GROUP)
        head = jnp.where(lane < 8, main[rows, :128].astype(F32), 0.0)
        tail = jnp.where(lane >= 120, main[rows, WIDE - 128 :].astype(F32), 0.0)
        left = left + pltpu.roll(head, 8 * group, 1)
        right = right + pltpu.roll(tail, 8 * group + 8, 1)
    to_left[...] = left.astype(BF16)
    to_right[...] = right.astype(BF16)


def weighted(spread, rows_of, half):
    side = slice(128 * half, 128 * half + 128)
    total = jnp.zeros((SLICES, 128), F32)
    for row in range(half, half + 17):
        total = total + rows_of[row : row + 1, side] * spread[
            SLICES * row : SLICES * row + SLICES, side
        ]
    return total


def interior_kernel(main, columns, rows_of, stack, edge):
    for block in range(BLOCKS):
        sides = [
            main[:, 128 * block + 128 : 128 * block + 192]
            if block < BLOCKS - 1
            else jnp.zeros((COUNT, 64), BF16),
            main[:, 128 * block - 64 : 128 * block] if block else jnp.zeros((COUNT, 64), BF16),
        ]
        edge[:, 128 * block : 128 * block + 128] = jnp.concatenate(sides, axis=1)
    for row in range(BAND):
        stack[row, BLOCKS * SLICES :, :] = jnp.zeros((STACK - BLOCKS * SLICES, 128), F32)
    core = lax.axis_index("wave") % 2

    def one_pair(step, carry):
        pair = step ^ (2 * core)
        window = pl.ds(pl.multiple_of(pair * (2 * SLICES), 2 * SLICES), 18 * SLICES)
        for block in range(BLOCKS):
            lanes = slice(128 * block, 128 * block + 128)
            left = jnp.concatenate([main[window, lanes], edge[window, lanes]], axis=1)
            spread = jnp.dot(left, columns[pair, block], preferred_element_type=F32)
            for half in range(2):
                total = weighted(spread, rows_of.at[pair, block], half)
                stack[2 * step + half, SLICES * block : SLICES * block + SLICES, :] = total
        return carry

    lax.fori_loop(0, BAND // 2, one_pair, 0)


def border(steps, edge, wrap_columns, wrap_rows, stack, out):
    core = lax.axis_index("wave") % 2
    column = lax.broadcasted_iota(jnp.int32, (SLICES, 128), 1)
    last = SLICES * (BLOCKS - 1)
    for step in steps:
        pair = step ^ (2 * core)
        window = pl.ds(pl.multiple_of(pair * (2 * SLICES), 2 * SLICES), 18 * SLICES)
        spread = jnp.dot(edge[window, :], wrap_columns[pair], preferred_element_type=F32)
        for half in range(2):
            more = weighted(spread, wrap_rows.at[pair], half)
            full = stack[2 * step + half]
            full = jnp.concatenate(
                [
                    full[:SLICES] + jnp.where(column < 64, more, 0.0),
                    full[SLICES:last],
                    full[last : last + SLICES] + jnp.where(column >= 64, more, 0.0),
                    full[last + SLICES :],
                ],
                axis=0,
            )
            out[(2 * step + half) % ROWS] = full.astype(BF16)


def border_send_kernel(from_left, from_right, wrap_columns, wrap_rows, stack, send, edge):
    lane = lax.broadcasted_iota(jnp.int32, (GROUP, 128), 1)
    left = from_left[...].astype(F32)
    right = from_right[...].astype(F32)
    for group in range(COUNT // GROUP):
        one = pltpu.roll(right, (128 - 8 * group) % 128, 1)
        two = pltpu.roll(left, 120 - 8 * group, 1)
        edge[GROUP * group : GROUP * group + GROUP, :] = jnp.where(lane < 64, one, two).astype(BF16)
    border((2, 3), edge, wrap_columns, wrap_rows, stack, send)


def border_keep_kernel(edge, wrap_columns, wrap_rows, stack, keep):
    border((0, 1), edge, wrap_columns, wrap_rows, stack, keep)


def turn(count, length, inverse):
    whole = jnp.floor(count * inverse + 0.5)
    angle = (count - whole * length) * (inverse * math.pi)
    square = angle * angle
    sine = angle * (
        1.0
        + square
        * (
            -1.0 / 6
            + square
            * (1.0 / 120 + square * (-1.0 / 5040 + square * (1.0 / 362880 - square / 39916800)))
        )
    )
    cosine = 1.0 + square * (
        -0.5
        + square
        * (
            1.0 / 24
            + square
            * (-1.0 / 720 + square * (1.0 / 40320 + square * (-1.0 / 3628800 + square / 479001600)))
        )
    )
    return 1.0 - 2.0 * sine * sine, 2.0 * sine * cosine


def rotated(one, two):
    return one[0] * two[0] - one[1] * two[1], one[1] * two[0] + one[0] * two[1]


def table_kernel(
    place, waves, stencil, inner, outer, columns, rows_of, wrap_columns, wrap_rows, points
):
    wave_place = place[1]
    first_row = place[0] * ROWS
    step = lax.broadcasted_iota(jnp.int32, (8, 128), 0)
    away = ((wave_place ^ 1) - wave_place) * WIDE
    shift = jnp.where(step == 5, away, jnp.where(step == 6, 64, 128 * step + wave_place * WIDE))
    shift = shift.astype(F32)
    fine = step.astype(F32)

    def one(row, carry):
        length = jnp.full((1, 128), place[LENGTHS + first_row + row], jnp.int32).astype(F32)
        inverse = 1.0 / length
        norm = lax.rsqrt(length)
        for slot in range(SLOTS):
            wave = waves[slot : slot + 1, :]
            lanes = slice(slot * 256, slot * 256 + 128)
            lanes_two = slice(slot * 256 + 128, slot * 256 + 256)
            moved = turn(shift * wave, length, inverse)
            outer[row, :, lanes] = moved[0] * norm
            outer[row, :, lanes_two] = moved[1] * norm
            other = [part[5:6] for part in moved]
            half = [part[6:7] for part in moved]
            small = turn(fine * wave, length, inverse)
            low = turn(8.0 * fine * wave, length, inverse)
            for tile in range(2):
                if tile:
                    low = rotated(low, other)
                high = rotated(low, half)
                for coarse in range(0, 16, 2):
                    source = low if coarse < 8 else high
                    at = coarse % 8
                    pairs = [
                        rotated([part[k : k + 1] for part in source], small) for k in (at, at + 1)
                    ]
                    rows = slice(128 * tile + 8 * coarse, 128 * tile + 8 * coarse + 16)
                    for side, to in enumerate((lanes, lanes_two)):
                        inner[row, rows, to] = jnp.concatenate(
                            [pair[side] for pair in pairs], axis=0
                        ).astype(BF16)
        return carry

    lax.fori_loop(0, ROWS, one, 0)

    column = lax.broadcasted_iota(jnp.int32, (1, WIDE), 1)
    lane = (column % 128).astype(F32)
    for base, first, fraction in (
        (0, stencil[1] + (lane - 1.0), stencil[3]),
        (8, stencil[0] + (BAND - 1.0), stencil[2]),
    ):
        for k, value in enumerate((first,) + cubic_weights(fraction)):
            for row in range(BAND):
                part = value[row : row + 1, :]
                if base and k:
                    part = jnp.where(column < place[LENGTHS + row] - wave_place * WIDE, part, 0.0)
                points[row, base + k : base + k + 1, :] = part

    def one_pair(pair, carry):
        def row_of(item, block):
            return jnp.concatenate(
                [
                    points[2 * pair + half, item : item + 1, 128 * block : 128 * block + 128]
                    for half in range(2)
                ],
                axis=1,
            )

        for block in range(BLOCKS):
            start = row_of(0, block).astype(BF16)
            weights = [row_of(1 + k, block).astype(BF16) for k in range(4)]
            source = lax.broadcasted_iota(jnp.int32, (144, 256), 0).astype(F32).astype(BF16)
            columns[pair, block, 0:144, :] = picked_weight(source - start, weights)
            columns[pair, block, 144:240, :] = jnp.zeros((96, 256), BF16)
            source = lax.broadcasted_iota(jnp.int32, (16, 256), 0).astype(F32) - 16.0
            columns[pair, block, 240:256, :] = picked_weight(source.astype(BF16) - start, weights)
            half = (lax.broadcasted_iota(jnp.int32, (1, 256), 1) >= 128).astype(F32)
            start = row_of(8, block) + half
            weights = [row_of(9 + k, block) for k in range(4)]
            source = lax.broadcasted_iota(jnp.int32, (24, 256), 0).astype(F32)
            rows_of[pair, block] = picked_weight(source - start, weights)
        ends = (0, BLOCKS - 1, 0, BLOCKS - 1)
        wrap_columns[pair] = jnp.concatenate(
            [columns[pair, end, 128:, 64 * k : 64 * k + 64] for k, end in enumerate(ends)], axis=1
        )
        side = lax.broadcasted_iota(jnp.int32, (24, 256), 1) % 128
        wrap_rows[pair] = jnp.where(side < 64, rows_of[pair, 0], rows_of[pair, BLOCKS - 1])
        return carry

    lax.fori_loop(0, BAND // 2, one_pair, 0)


def fourier_kernel(mine, other, inner, outer, message, sums, shuffled):
    def one(row, carry):
        left = jnp.concatenate([mine[row], other[row]], axis=1)
        base = pl.multiple_of(row * 512, 512)
        sums[pl.ds(base + 480, 32), :] = jnp.zeros((32, 128), F32)
        for slot in range(SLOTS):
            lanes = slice(256 * slot, 256 * slot + 256)
            parts = jnp.dot(left, inner[row, :, lanes], preferred_element_type=F32)
            real = jnp.zeros((SLICES, 128), F32)
            imag = jnp.zeros((SLICES, 128), F32)
            for block in range(BLOCKS):
                rows = slice(SLICES * block, SLICES * block + SLICES)
                cosine, sine = parts[rows, :128], parts[rows, 128:]
                c = outer[row, block : block + 1, 256 * slot : 256 * slot + 128]
                s = outer[row, block : block + 1, 256 * slot + 128 : 256 * slot + 256]
                real = real + (c * cosine - s * sine)
                imag = imag - (s * cosine + c * sine)
            sums[pl.ds(base + slot * 48, SLICES, stride=2), :] = real
            sums[pl.ds(base + slot * 48 + 1, SLICES, stride=2), :] = imag
        return carry

    lax.fori_loop(0, ROWS, one, 0)
    for part in range(16):
        shuffled[pl.ds(part, DEVICES, stride=16), :] = sums[128 * part : 128 * part + 128, :].T
    message[...] = shuffled[...].astype(BF16)


def legendre_kernel(place, waves, message, table, out, flat, sorted_rows, left, result, done):
    for band in range(16):
        for core in range(2):
            total = message[8 * band + core].astype(F32)
            for z in range(1, 4):
                total = total + message[8 * band + 2 * z + core].astype(F32)
            first = (2 * band + core) * 16
            flat[first : first + 16, :] = total
    for row in range(ROWS):
        for part in range(4):
            sorted_rows[pl.ds(128 * part + row, 32, stride=4), :] = flat[
                pl.ds(4 * row + part, 32, stride=16), :
            ]
    for part in range(4):
        rows = slice(128 * part, 128 * part + 128)
        left[rows, :] = sorted_rows[rows, :].T.astype(BF16)
    copies = []
    for slot in range(SLOTS):
        product = jnp.dot(left[48 * slot : 48 * slot + 48, :], table[slot], preferred_element_type=F32)
        degree = lax.broadcasted_iota(jnp.int32, product.shape, 1)
        result[slot] = jnp.where(degree >= waves[place[2] + slot], product, 0.0)
        copy = pltpu.make_async_copy(result.at[slot], out.at[slot], done.at[slot])
        copy.start()
        copies.append(copy)
    for copy in copies:
        copy.wait()


def local(fields, row_length, wave_order, depart_row, depart_col, frac_row, frac_col, legendre):
    wave_place = lax.axis_index("wave")
    lat_place = lax.axis_index("lat")
    ring = lax.axis_size("wave")
    bands = lax.axis_size("lat")
    first_slot = (lat_place * ring + wave_place) * SLOTS
    own_place = jnp.stack([wave_place % 2, wave_place, first_slot, lat_place % 2])
    scalars = jnp.concatenate([own_place.astype(jnp.int32), row_length, wave_order])
    scalars = lax.optimization_barrier(scalars)
    place = scalars[: LENGTHS + BAND]
    ordered = scalars[LENGTHS + BAND :].reshape(DEVICES, SLOTS).T.astype(F32)
    limit = place[LENGTHS:] - wave_place * WIDE
    live_mask = jnp.arange(WIDE, dtype=jnp.int32)[None, :] < limit[:, None]
    masked = jnp.where(live_mask[None], fields, jnp.zeros_like(fields))
    own = masked.transpose(1, 0, 2).reshape(BAND * SLICES, WIDE)

    def swapped(first):
        pairs = [(i, i + 1) for i in range(first, bands - 1, 2)]
        return lax.ppermute(own, "lat", pairs + [(j, i) for i, j in pairs])

    over = swapped(1)
    under = swapped(0)

    stencil = jnp.stack([depart_row.astype(F32), depart_col.astype(F32), frac_row, frac_col])
    inner, outer, columns, rows_of, wrap_columns, wrap_rows = pl.pallas_call(
        table_kernel,
        out_shape=(
            jax.ShapeDtypeStruct((ROWS, 256, SLOTS * 256), BF16),
            jax.ShapeDtypeStruct((ROWS, 8, SLOTS * 256), F32),
            jax.ShapeDtypeStruct((BAND // 2, BLOCKS, 256, 256), BF16),
            jax.ShapeDtypeStruct((BAND // 2, BLOCKS, 24, 256), F32),
            jax.ShapeDtypeStruct((BAND // 2, 128, 256), BF16),
            jax.ShapeDtypeStruct((BAND // 2, 24, 256), F32),
        ),
        in_specs=[SMEM, VMEM, VMEM],
        out_specs=(VMEM,) * 6,
        scratch_shapes=[pltpu.VMEM((BAND, 16, WIDE), F32)],
        compiler_params=pltpu.CompilerParams(vmem_limit_bytes=LIMIT),
        cost_estimate=pl.CostEstimate(flops=5_000_000_000, bytes_accessed=3_000_000, transcendentals=0),
        name="tables",
    )(place, ordered, stencil)

    main, to_left, to_right = pl.pallas_call(
        pack_kernel,
        out_shape=(
            jax.ShapeDtypeStruct((COUNT, WIDE), BF16),
            jax.ShapeDtypeStruct((GROUP, 128), BF16),
            jax.ShapeDtypeStruct((GROUP, 128), BF16),
        ),
        in_specs=[VMEM] * 3,
        out_specs=(VMEM,) * 3,
        compiler_params=pltpu.CompilerParams(vmem_limit_bytes=LIMIT),
        name="pack",
    )(own, over, under)
    from_left = lax.ppermute(to_right, "wave", [(i, (i + 1) % ring) for i in range(ring)])
    from_right = lax.ppermute(to_left, "wave", [((i + 1) % ring, i) for i in range(ring)])
    stack = pl.pallas_call(
        interior_kernel,
        out_shape=jax.ShapeDtypeStruct((BAND, STACK, 128), F32),
        in_specs=[VMEM] * 3,
        out_specs=VMEM,
        scratch_shapes=[pltpu.VMEM((COUNT, WIDE), BF16)],
        compiler_params=pltpu.CompilerParams(vmem_limit_bytes=LIMIT),
        cost_estimate=pl.CostEstimate(flops=5_000_000_000, bytes_accessed=3_000_000, transcendentals=0),
        name="interior",
    )(main, columns, rows_of)
    send, edge = pl.pallas_call(
        border_send_kernel,
        out_shape=(
            jax.ShapeDtypeStruct((ROWS, STACK, 128), BF16),
            jax.ShapeDtypeStruct((COUNT, 128), BF16),
        ),
        in_specs=[VMEM] * 5,
        out_specs=(VMEM, VMEM),
        compiler_params=pltpu.CompilerParams(vmem_limit_bytes=LIMIT),
        name="border_send",
    )(from_left, from_right, wrap_columns, wrap_rows, stack)
    other = lax.ppermute(send, "wave", [(i, i ^ 1) for i in range(ring)])
    keep = pl.pallas_call(
        border_keep_kernel,
        out_shape=jax.ShapeDtypeStruct((ROWS, STACK, 128), BF16),
        in_specs=[VMEM] * 4,
        out_specs=VMEM,
        compiler_params=pltpu.CompilerParams(vmem_limit_bytes=LIMIT),
        cost_estimate=pl.CostEstimate(flops=5_000_000_000, bytes_accessed=3_000_000, transcendentals=0),
        name="border_keep",
    )(edge, wrap_columns, wrap_rows, stack)
    message = pl.pallas_call(
        fourier_kernel,
        out_shape=jax.ShapeDtypeStruct((DEVICES * 16, 128), BF16),
        in_specs=[VMEM] * 4,
        out_specs=VMEM,
        scratch_shapes=[
            pltpu.VMEM((ROWS * 512, 128), F32),
            pltpu.VMEM((DEVICES * 16, 128), F32),
        ],
        compiler_params=pltpu.CompilerParams(vmem_limit_bytes=LIMIT),
        name="fourier",
    )(keep, other, inner, outer)
    message = lax.all_to_all(
        message.reshape(DEVICES, 16, 128), ("lat", "wave"), split_axis=0, concat_axis=0, tiled=True
    )
    degrees = legendre.shape[2]
    return pl.pallas_call(
        legendre_kernel,
        out_shape=jax.ShapeDtypeStruct((SLOTS, 2 * SLICES, degrees), F32),
        in_specs=[SMEM, SMEM, VMEM, VMEM],
        out_specs=pl.BlockSpec(memory_space=pl.ANY),
        scratch_shapes=[
            pltpu.VMEM((512, 128), F32),
            pltpu.VMEM((512, 128), F32),
            pltpu.VMEM((512, 128), BF16),
            pltpu.VMEM((SLOTS, 2 * SLICES, degrees), F32),
            pltpu.SemaphoreType.DMA((SLOTS,)),
        ],
        compiler_params=pltpu.CompilerParams(vmem_limit_bytes=LIMIT),
        name="legendre",
    )(place, wave_order, message, legendre)


def solution(mesh):
    placed = (
        P(None, "lat", "wave"),
        P("lat"),
        P(),
        P("lat", "wave"),
        P("lat", "wave"),
        P("lat", "wave"),
        P("lat", "wave"),
        P(("lat", "wave"), None, None),
    )
    return jax.shard_map(
        local, mesh=mesh, in_specs=placed, out_specs=P(("lat", "wave"), None, None), check_vma=False
    )
```

```python
import math

import jax
import jax.numpy as jnp
from jax import lax
from jax.experimental import pallas as pl
from jax.experimental.pallas import tpu as pltpu
from jax.sharding import PartitionSpec as P

F32 = jnp.float32
BF16 = jnp.bfloat16
VMEM = pl.BlockSpec(memory_space=pltpu.VMEM)
LIMIT = 24 * 1024 * 1024

SLICES = 24
BAND = 8
WIDE = 640
BLOCKS = 5
SLOTS = 10
DEVICES = 128
ROWS = 4
STACK = 144
COUNT = 3 * BAND * SLICES


def cubic_weights(fraction):
    return (
        -fraction * (fraction - 1.0) * (fraction - 2.0) / 6.0,
        (fraction + 1.0) * (fraction - 1.0) * (fraction - 2.0) / 2.0,
        -(fraction + 1.0) * fraction * (fraction - 2.0) / 2.0,
        (fraction + 1.0) * fraction * (fraction - 1.0) / 6.0,
    )


def picked_weight(distance, weights):
    chosen = jnp.where(distance == 3, weights[3], jnp.zeros_like(weights[3]))
    for step in (2, 1, 0):
        chosen = jnp.where(distance == step, weights[step], chosen)
    return chosen


def weighted(spread, rows_of, half):
    side = slice(128 * half, 128 * half + 128)
    total = jnp.zeros((SLICES, 128), F32)
    for row in range(half, half + 17):
        total = total + rows_of[row : row + 1, side] * spread[
            SLICES * row : SLICES * row + SLICES, side
        ]
    return total


def interpolate(steps, main, edge, columns, rows_of, wrap_columns, wrap_rows, out):
    core = lax.axis_index("wave") % 2
    for step in steps:
        pair = step ^ (2 * core)
        window = pl.ds(pl.multiple_of(pair * (2 * SLICES), 2 * SLICES), 18 * SLICES)
        totals = ([], [])
        for block in range(BLOCKS + 1):
            lanes = slice(128 * block, 128 * block + 128)
            if block < BLOCKS:
                left = jnp.concatenate([main[window, lanes], edge[window, lanes]], axis=1)
                table, rows = columns[pair, block], rows_of.at[pair, block]
            else:
                left, table, rows = edge[window, lanes], wrap_columns[pair], wrap_rows.at[pair]
            spread = jnp.dot(left, table, preferred_element_type=F32)
            for half in range(2):
                totals[half].append(weighted(spread, rows, half))
        for half in range(2):
            out[(2 * step + half) % ROWS] = jnp.concatenate(totals[half], axis=0).astype(BF16)


def send_kernel(
    own, first, second, columns, rows_of, wrap_columns, wrap_rows, send, main, edge
):
    size = BAND * SLICES
    odd = lax.axis_index("lat") % 2
    main[pl.ds(pl.multiple_of(odd * 2 * size, size), size), :] = first[...]
    main[size : 2 * size, :] = own[...]
    main[pl.ds(pl.multiple_of((1 - odd) * 2 * size, size), size), :] = second[...]
    nothing = jnp.zeros((COUNT, 64), BF16)
    for block in range(BLOCKS):
        at = 128 * block
        sides = [
            main[:, at + 128 : at + 192] if block < BLOCKS - 1 else nothing,
            main[:, at - 64 : at] if block else nothing,
        ]
        edge[:, at : at + 128] = jnp.concatenate(sides, axis=1)
    edge[:, WIDE:] = jnp.concatenate([main[:, :64], main[:, WIDE - 64 :]], axis=1)
    interpolate((2, 3), main, edge, columns, rows_of, wrap_columns, wrap_rows, send)


def keep_kernel(main, edge, columns, rows_of, wrap_columns, wrap_rows, keep):
    interpolate((0, 1), main, edge, columns, rows_of, wrap_columns, wrap_rows, keep)


def turn(count, length, inverse):
    whole = jnp.floor(count * inverse + 0.5)
    angle = (count - whole * length) * (inverse * math.pi)
    square = angle * angle
    sine = angle * (
        1.0
        + square
        * (
            -1.0 / 6
            + square
            * (1.0 / 120 + square * (-1.0 / 5040 + square * (1.0 / 362880 - square / 39916800)))
        )
    )
    cosine = 1.0 + square * (
        -0.5
        + square
        * (
            1.0 / 24
            + square
            * (-1.0 / 720 + square * (1.0 / 40320 + square * (-1.0 / 3628800 + square / 479001600)))
        )
    )
    return 1.0 - 2.0 * sine * sine, 2.0 * sine * cosine


def rotated(one, two):
    return one[0] * two[0] - one[1] * two[1], one[1] * two[0] + one[0] * two[1]


def ring_start(place):
    return lax.rem(place + 8, 8) * WIDE


def table_kernel(
    lengths, waves, stencil, from_left, from_right,
    inner, outer, columns, rows_of, wrap_columns, wrap_rows, own_waves,
    points, wrap_points, length_rows,
):
    wave_place = lax.axis_index("wave")
    core = wave_place % 2
    owner = lax.axis_index("lat") * 8 + wave_place
    lane = lax.broadcasted_iota(jnp.int32, (SLOTS, 128), 1)
    mine = jnp.sum(jnp.where(lane == owner, waves[...], 0.0), axis=1, keepdims=True)
    own_waves[...] = jnp.broadcast_to(mine, (SLOTS, 128))
    for row in range(BAND):
        length_rows[row] = lengths[row : row + 1, :]
    first_row = core * ROWS
    step = lax.broadcasted_iota(jnp.int32, (8, 128), 0)
    other_place = wave_place ^ 1
    away = (other_place - wave_place) * WIDE
    before = ring_start(wave_place - 1) + (WIDE - 128)
    behind = ring_start(wave_place + 1)
    other_before = ring_start(other_place - 1) + (WIDE - 128)
    other_behind = ring_start(other_place + 1)
    outside = jnp.where(core == 0, before, behind)
    other_outside = jnp.where(core == 0, other_behind, other_before) - away
    shift = 128 * step + wave_place * WIDE
    for at, value in ((5, outside), (6, other_outside), (7, away)):
        shift = jnp.where(step == at, value, shift)
    shift = shift.astype(F32)
    fine = step.astype(F32)

    def one(row, carry):
        length = length_rows[first_row + row]
        inverse = 1.0 / length
        norm = lax.rsqrt(length)
        for slot in range(SLOTS):
            wave = waves[slot : slot + 1, :]
            lanes = slice(slot * 256, slot * 256 + 128)
            lanes_two = slice(slot * 256 + 128, slot * 256 + 256)
            moved = turn(shift * wave, length, inverse)
            outer[row, :, lanes] = moved[0] * norm
            outer[row, :, lanes_two] = moved[1] * norm
            other = [part[7:8] for part in moved]
            small = turn(fine * wave, length, inverse)
            low = turn(8.0 * fine * wave, length, inverse)
            half = rotated([part[7:8] for part in low], [part[1:2] for part in low])
            for tile in range(2):
                if tile:
                    low = rotated(low, other)
                high = rotated(low, half)
                for coarse in range(0, 16, 2):
                    source = low if coarse < 8 else high
                    at = coarse % 8
                    pairs = [
                        rotated([part[k : k + 1] for part in source], small) for k in (at, at + 1)
                    ]
                    rows = slice(128 * tile + 8 * coarse, 128 * tile + 8 * coarse + 16)
                    for side, to in enumerate((lanes, lanes_two)):
                        inner[row, rows, to] = jnp.concatenate(
                            [pair[side] for pair in pairs], axis=0
                        ).astype(BF16)
        return carry

    lax.fori_loop(0, ROWS, one, 0)

    def spread_points(target, values, width, position):
        lane = (lax.broadcasted_iota(jnp.int32, (1, width), 1) % 128).astype(F32)
        limit = jnp.concatenate([lengths[...]] * (width // 128), axis=1)
        live = position.astype(F32) < limit
        for base, first, fraction in (
            (0, values[1] + (lane - 1.0), values[3]),
            (8, values[0] + (BAND - 1.0), values[2]),
        ):
            for k, value in enumerate((first,) + cubic_weights(fraction)):
                if base and k:
                    value = jnp.where(live, value, 0.0)
                for row in range(BAND):
                    target[row, base + k : base + k + 1, :] = value[row : row + 1, :]

    column = lax.broadcasted_iota(jnp.int32, (BAND, WIDE), 1)
    spread_points(points, [stencil[k] for k in range(4)], WIDE, column + wave_place * WIDE)
    column = lax.broadcasted_iota(jnp.int32, (BAND, 128), 1)
    values = [jnp.where(column < 64, from_right[k], from_left[k]) for k in range(4)]
    spread_points(wrap_points, values, 128, column + jnp.where(column < 64, behind, before))

    def one_pair(pair, carry):
        def row_of(ref, item, block):
            return jnp.concatenate(
                [
                    ref[2 * pair + half, item : item + 1, 128 * block : 128 * block + 128]
                    for half in range(2)
                ],
                axis=1,
            )

        def picks(ref, block):
            start = row_of(ref, 0, block).astype(BF16)
            weights = [row_of(ref, 1 + k, block).astype(BF16) for k in range(4)]

            def pick(count, first):
                source = lax.broadcasted_iota(jnp.int32, (count, 256), 0) + first
                return picked_weight(source.astype(F32).astype(BF16) - start, weights)

            return pick

        def row_table(ref, block):
            half = (lax.broadcasted_iota(jnp.int32, (1, 256), 1) >= 128).astype(F32)
            start = row_of(ref, 8, block) + half
            weights = [row_of(ref, 9 + k, block) for k in range(4)]
            source = lax.broadcasted_iota(jnp.int32, (24, 256), 0).astype(F32)
            return picked_weight(source - start, weights)

        for block in range(BLOCKS):
            pick = picks(points, block)
            columns[pair, block, 0:144, :] = pick(144, 0)
            columns[pair, block, 144:240, :] = jnp.zeros((96, 256), BF16)
            columns[pair, block, 240:256, :] = pick(16, -16)
            rows_of[pair, block] = row_table(points, block)
        pick = picks(wrap_points, 0)
        wrap_columns[pair, 0:16, :] = pick(16, 128)
        wrap_columns[pair, 16:112, :] = jnp.zeros((96, 256), BF16)
        wrap_columns[pair, 112:128, :] = pick(16, -16)
        wrap_rows[pair] = row_table(wrap_points, 0)
        return carry

    lax.fori_loop(0, BAND // 2, one_pair, 0)


def fourier_kernel(mine, other, inner, outer, message, sums, shuffled):
    odd = jnp.full((SLICES, 128), lax.axis_index("wave") % 2, jnp.int32).astype(F32)
    low = (lax.broadcasted_iota(jnp.int32, (SLICES, 128), 1) < 64).astype(F32)
    to_mine = (low * odd, (1.0 - low) * (1.0 - odd))
    to_other = (low * (1.0 - odd), (1.0 - low) * odd)
    last = SLICES * (BLOCKS - 1)
    nothing = jnp.zeros((SLICES, 128), F32)

    def one(row, carry):
        own = mine[row].astype(F32)
        far = other[row].astype(F32)
        own_wrap, far_wrap = own[last + SLICES :], far[last + SLICES :]
        halves = [
            [
                own[:SLICES] + far_wrap * to_mine[0],
                own[SLICES:last],
                own[last : last + SLICES] + far_wrap * to_mine[1],
                own_wrap * (to_mine[0] + to_mine[1]),
                nothing,
                nothing[:8],
            ],
            [
                far[:SLICES] + own_wrap * to_other[0],
                far[SLICES:last],
                far[last : last + SLICES] + own_wrap * to_other[1],
                nothing,
                far_wrap * (to_other[0] + to_other[1]),
                nothing[:8],
            ],
        ]
        left = jnp.concatenate([jnp.concatenate(half, axis=0) for half in halves], axis=1)
        left = left.astype(BF16)
        base = pl.multiple_of(row * 512, 512)
        sums[pl.ds(base + 480, 32), :] = jnp.zeros((32, 128), F32)
        for slot in range(SLOTS):
            lanes = slice(256 * slot, 256 * slot + 256)
            parts = jnp.dot(left, inner[row, :, lanes], preferred_element_type=F32)
            real = jnp.zeros((SLICES, 128), F32)
            imag = jnp.zeros((SLICES, 128), F32)
            for block in range(BLOCKS + 2):
                rows = slice(SLICES * block, SLICES * block + SLICES)
                cosine, sine = parts[rows, :128], parts[rows, 128:]
                c = outer[row, block : block + 1, 256 * slot : 256 * slot + 128]
                s = outer[row, block : block + 1, 256 * slot + 128 : 256 * slot + 256]
                real = real + (c * cosine - s * sine)
                imag = imag - (s * cosine + c * sine)
            sums[pl.ds(base + slot * 48, SLICES, stride=2), :] = real
            sums[pl.ds(base + slot * 48 + 1, SLICES, stride=2), :] = imag
        return carry

    lax.fori_loop(0, ROWS, one, 0)
    for part in range(16):
        shuffled[pl.ds(part, DEVICES, stride=16), :] = sums[128 * part : 128 * part + 128, :].T
    message[...] = shuffled[...].astype(BF16)


def legendre_kernel(waves, message, table, out, flat, sorted_rows, left, result, done):
    for band in range(16):
        for core in range(2):
            total = message[8 * band + core].astype(F32)
            for z in range(1, 4):
                total = total + message[8 * band + 2 * z + core].astype(F32)
            first = (2 * band + core) * 16
            flat[first : first + 16, :] = total
    for row in range(ROWS):
        for part in range(4):
            sorted_rows[pl.ds(128 * part + row, 32, stride=4), :] = flat[
                pl.ds(4 * row + part, 32, stride=16), :
            ]
    for part in range(4):
        rows = slice(128 * part, 128 * part + 128)
        left[rows, :] = sorted_rows[rows, :].T.astype(BF16)
    copies = []
    for slot in range(SLOTS):
        product = jnp.dot(left[48 * slot : 48 * slot + 48, :], table[slot], preferred_element_type=F32)
        wave = jnp.concatenate([waves[slot : slot + 1, :]] * (product.shape[1] // 128), axis=1)
        degree = lax.broadcasted_iota(jnp.int32, product.shape, 1).astype(F32)
        result[slot] = jnp.where(degree >= wave, product, 0.0)
        copy = pltpu.make_async_copy(result.at[slot], out.at[slot], done.at[slot])
        copy.start()
        copies.append(copy)
    for copy in copies:
        copy.wait()


def local(fields, row_length, wave_order, depart_row, depart_col, frac_row, frac_col, legendre):
    ring = lax.axis_size("wave")
    bands = lax.axis_size("lat")
    scalars = lax.optimization_barrier(jnp.concatenate([row_length, wave_order]))
    lengths = scalars[:BAND]
    ordered = scalars[BAND:].reshape(DEVICES, SLOTS).T.astype(F32)
    limit = lengths - lax.axis_index("wave") * WIDE
    live_mask = jnp.arange(WIDE, dtype=jnp.int32)[None, :] < limit[:, None]
    masked = jnp.where(live_mask[None], fields, jnp.zeros_like(fields))
    own = masked.transpose(1, 0, 2).reshape(BAND * SLICES, WIDE)

    def swapped(first):
        pairs = [(i, i + 1) for i in range(first, bands - 1, 2)]
        return lax.ppermute(own, "lat", pairs + [(j, i) for i, j in pairs])

    over = swapped(1)
    under = swapped(0)

    own, depart_row = lax.optimization_barrier((own, depart_row))
    stencil = jnp.stack([depart_row.astype(F32), depart_col.astype(F32), frac_row, frac_col])
    from_left = lax.ppermute(
        stencil[:, :, WIDE - 128 :], "wave", [(i, (i + 1) % ring) for i in range(ring)]
    )
    from_right = lax.ppermute(
        stencil[:, :, :128], "wave", [((i + 1) % ring, i) for i in range(ring)]
    )
    length_table = jnp.broadcast_to(lengths.astype(F32)[:, None], (BAND, 128))
    inner, outer, columns, rows_of, wrap_columns, wrap_rows, own_waves = pl.pallas_call(
        table_kernel,
        out_shape=(
            jax.ShapeDtypeStruct((ROWS, 256, SLOTS * 256), BF16),
            jax.ShapeDtypeStruct((ROWS, 8, SLOTS * 256), F32),
            jax.ShapeDtypeStruct((BAND // 2, BLOCKS, 256, 256), BF16),
            jax.ShapeDtypeStruct((BAND // 2, BLOCKS, 24, 256), F32),
            jax.ShapeDtypeStruct((BAND // 2, 128, 256), BF16),
            jax.ShapeDtypeStruct((BAND // 2, 24, 256), F32),
            jax.ShapeDtypeStruct((SLOTS, 128), F32),
        ),
        in_specs=[VMEM] * 5,
        out_specs=(VMEM,) * 7,
        scratch_shapes=[
            pltpu.VMEM((BAND, 16, WIDE), F32),
            pltpu.VMEM((BAND, 16, 128), F32),
            pltpu.VMEM((BAND, 1, 128), F32),
        ],
        compiler_params=pltpu.CompilerParams(vmem_limit_bytes=LIMIT),
        cost_estimate=pl.CostEstimate(flops=5_000_000_000, bytes_accessed=3_000_000, transcendentals=0),
        name="tables",
    )(length_table, ordered, stencil, from_left, from_right)

    weights = (columns, rows_of, wrap_columns, wrap_rows)
    part = jax.ShapeDtypeStruct((ROWS, STACK, 128), BF16)
    send, main, edge = pl.pallas_call(
        send_kernel,
        out_shape=(
            part,
            jax.ShapeDtypeStruct((COUNT, WIDE), BF16),
            jax.ShapeDtypeStruct((COUNT, WIDE + 128), BF16),
        ),
        in_specs=[VMEM] * 7,
        out_specs=(VMEM,) * 3,
        compiler_params=pltpu.CompilerParams(vmem_limit_bytes=LIMIT),
        name="interpolate_send",
    )(own, over, under, *weights)
    other = lax.ppermute(send, "wave", [(i, i ^ 1) for i in range(ring)])
    keep = pl.pallas_call(
        keep_kernel,
        out_shape=part,
        in_specs=[VMEM] * 6,
        out_specs=VMEM,
        compiler_params=pltpu.CompilerParams(vmem_limit_bytes=LIMIT),
        cost_estimate=pl.CostEstimate(flops=5_000_000_000, bytes_accessed=3_000_000, transcendentals=0),
        name="interpolate_keep",
    )(main, edge, *weights)
    message = pl.pallas_call(
        fourier_kernel,
        out_shape=jax.ShapeDtypeStruct((DEVICES * 16, 128), BF16),
        in_specs=[VMEM] * 4,
        out_specs=VMEM,
        scratch_shapes=[
            pltpu.VMEM((ROWS * 512, 128), F32),
            pltpu.VMEM((DEVICES * 16, 128), F32),
        ],
        compiler_params=pltpu.CompilerParams(vmem_limit_bytes=LIMIT),
        name="fourier",
    )(keep, other, inner, outer)
    message = lax.all_to_all(
        message.reshape(DEVICES, 16, 128), ("lat", "wave"), split_axis=0, concat_axis=0, tiled=True
    )
    degrees = legendre.shape[2]
    return pl.pallas_call(
        legendre_kernel,
        out_shape=jax.ShapeDtypeStruct((SLOTS, 2 * SLICES, degrees), F32),
        in_specs=[VMEM] * 3,
        out_specs=pl.BlockSpec(memory_space=pl.ANY),
        scratch_shapes=[
            pltpu.VMEM((512, 128), F32),
            pltpu.VMEM((512, 128), F32),
            pltpu.VMEM((512, 128), BF16),
            pltpu.VMEM((SLOTS, 2 * SLICES, degrees), F32),
            pltpu.SemaphoreType.DMA((SLOTS,)),
        ],
        compiler_params=pltpu.CompilerParams(vmem_limit_bytes=LIMIT),
        name="legendre",
    )(own_waves, message, legendre)


def solution(mesh):
    placed = (
        P(None, "lat", "wave"),
        P("lat"),
        P(),
        P("lat", "wave"),
        P("lat", "wave"),
        P("lat", "wave"),
        P("lat", "wave"),
        P(("lat", "wave"), None, None),
    )
    return jax.shard_map(
        local, mesh=mesh, in_specs=placed, out_specs=P(("lat", "wave"), None, None), check_vma=False
    )
```

```python
import math

import jax
import jax.numpy as jnp
from jax import lax
from jax.experimental import pallas as pl
from jax.experimental.pallas import tpu as pltpu
from jax.sharding import PartitionSpec as P

F32 = jnp.float32
BF16 = jnp.bfloat16
VMEM = pl.BlockSpec(memory_space=pltpu.VMEM)
LIMIT = 24 * 1024 * 1024

SLICES = 24
BAND = 8
WIDE = 640
BLOCKS = 5
SLOTS = 10
DEVICES = 128
ROWS = 4
STACK = 144
COUNT = 3 * BAND * SLICES


def cubic_weights(fraction):
    return (
        -fraction * (fraction - 1.0) * (fraction - 2.0) / 6.0,
        (fraction + 1.0) * (fraction - 1.0) * (fraction - 2.0) / 2.0,
        -(fraction + 1.0) * fraction * (fraction - 2.0) / 2.0,
        (fraction + 1.0) * fraction * (fraction - 1.0) / 6.0,
    )


def picked_weight(distance, weights):
    chosen = jnp.where(distance == 3, weights[3], jnp.zeros_like(weights[3]))
    for step in (2, 1, 0):
        chosen = jnp.where(distance == step, weights[step], chosen)
    return chosen


def weighted(spread, rows_of, half):
    side = slice(128 * half, 128 * half + 128)
    total = jnp.zeros((SLICES, 128), F32)
    for row in range(half, half + 17):
        total = total + rows_of[row : row + 1, side] * spread[
            SLICES * row : SLICES * row + SLICES, side
        ]
    return total


def interpolate(steps, main, edge, columns, rows_of, wrap_columns, wrap_rows, out):
    core = lax.axis_index("wave") % 2
    for step in steps:
        pair = step ^ (2 * core)
        window = pl.ds(pl.multiple_of(pair * (2 * SLICES), 2 * SLICES), 18 * SLICES)
        totals = ([], [])
        for block in range(BLOCKS + 1):
            lanes = slice(128 * block, 128 * block + 128)
            if block < BLOCKS:
                left = jnp.concatenate([main[window, lanes], edge[window, lanes]], axis=1)
                table, rows = columns[pair, block], rows_of.at[pair, block]
            else:
                left, table, rows = edge[window, lanes], wrap_columns[pair], wrap_rows.at[pair]
            spread = jnp.dot(left, table, preferred_element_type=F32)
            for half in range(2):
                totals[half].append(weighted(spread, rows, half))
        for half in range(2):
            out[(2 * step + half) % ROWS] = jnp.concatenate(totals[half], axis=0).astype(BF16)


def send_kernel(
    own, first, second, columns, rows_of, wrap_columns, wrap_rows, send, main, edge
):
    size = BAND * SLICES
    odd = lax.axis_index("lat") % 2
    main[pl.ds(pl.multiple_of(odd * 2 * size, size), size), :] = first[...]
    main[size : 2 * size, :] = own[...]
    main[pl.ds(pl.multiple_of((1 - odd) * 2 * size, size), size), :] = second[...]
    nothing = jnp.zeros((COUNT, 64), BF16)
    for block in range(BLOCKS):
        at = 128 * block
        sides = [
            main[:, at + 128 : at + 192] if block < BLOCKS - 1 else nothing,
            main[:, at - 64 : at] if block else nothing,
        ]
        edge[:, at : at + 128] = jnp.concatenate(sides, axis=1)
    edge[:, WIDE:] = jnp.concatenate([main[:, :64], main[:, WIDE - 64 :]], axis=1)
    interpolate((2, 3), main, edge, columns, rows_of, wrap_columns, wrap_rows, send)


def keep_kernel(main, edge, columns, rows_of, wrap_columns, wrap_rows, keep):
    interpolate((0, 1), main, edge, columns, rows_of, wrap_columns, wrap_rows, keep)


def turn(count, length, inverse):
    whole = jnp.floor(count * inverse + 0.5)
    angle = (count - whole * length) * (inverse * math.pi)
    square = angle * angle
    sine = angle * (
        1.0
        + square
        * (
            -1.0 / 6
            + square
            * (1.0 / 120 + square * (-1.0 / 5040 + square * (1.0 / 362880 - square / 39916800)))
        )
    )
    cosine = 1.0 + square * (
        -0.5
        + square
        * (
            1.0 / 24
            + square
            * (-1.0 / 720 + square * (1.0 / 40320 + square * (-1.0 / 3628800 + square / 479001600)))
        )
    )
    return 1.0 - 2.0 * sine * sine, 2.0 * sine * cosine


def rotated(one, two):
    return one[0] * two[0] - one[1] * two[1], one[1] * two[0] + one[0] * two[1]


def ring_start(place):
    return lax.rem(place + 8, 8) * WIDE


def spread_points(target, lengths, values, width, position):
    lane = (lax.broadcasted_iota(jnp.int32, (1, width), 1) % 128).astype(F32)
    limit = jnp.concatenate([lengths[...]] * (width // 128), axis=1)
    live = position.astype(F32) < limit
    for base, first, fraction in (
        (0, values[1] + (lane - 1.0), values[3]),
        (8, values[0] + (BAND - 1.0), values[2]),
    ):
        for k, value in enumerate((first,) + cubic_weights(fraction)):
            if base and k:
                value = jnp.where(live, value, 0.0)
            for row in range(BAND):
                target[row, base + k : base + k + 1, :] = value[row : row + 1, :]


def row_of(ref, pair, item, block):
    return jnp.concatenate(
        [
            ref[2 * pair + half, item : item + 1, 128 * block : 128 * block + 128]
            for half in range(2)
        ],
        axis=1,
    )


def picks(ref, pair, block):
    start = row_of(ref, pair, 0, block).astype(BF16)
    weights = [row_of(ref, pair, 1 + k, block).astype(BF16) for k in range(4)]

    def pick(count, first):
        source = lax.broadcasted_iota(jnp.int32, (count, 256), 0) + first
        return picked_weight(source.astype(F32).astype(BF16) - start, weights)

    return pick


def row_table(ref, pair, block):
    half = (lax.broadcasted_iota(jnp.int32, (1, 256), 1) >= 128).astype(F32)
    start = row_of(ref, pair, 8, block) + half
    weights = [row_of(ref, pair, 9 + k, block) for k in range(4)]
    source = lax.broadcasted_iota(jnp.int32, (24, 256), 0).astype(F32)
    return picked_weight(source - start, weights)


def table_kernel(
    lengths, waves, stencil, inner, outer, columns, rows_of, own_waves, points, length_rows
):
    wave_place = lax.axis_index("wave")
    core = wave_place % 2
    owner = lax.axis_index("lat") * 8 + wave_place
    lane = lax.broadcasted_iota(jnp.int32, (SLOTS, 128), 1)
    mine = jnp.sum(jnp.where(lane == owner, waves[...], 0.0), axis=1, keepdims=True)
    own_waves[...] = jnp.broadcast_to(mine, (SLOTS, 128))
    for row in range(BAND):
        length_rows[row] = lengths[row : row + 1, :]
    first_row = core * ROWS
    step = lax.broadcasted_iota(jnp.int32, (8, 128), 0)
    other_place = wave_place ^ 1
    away = (other_place - wave_place) * WIDE
    before = ring_start(wave_place - 1) + (WIDE - 128)
    behind = ring_start(wave_place + 1)
    other_before = ring_start(other_place - 1) + (WIDE - 128)
    other_behind = ring_start(other_place + 1)
    outside = jnp.where(core == 0, before, behind)
    other_outside = jnp.where(core == 0, other_behind, other_before) - away
    shift = 128 * step + wave_place * WIDE
    for at, value in ((5, outside), (6, other_outside), (7, away)):
        shift = jnp.where(step == at, value, shift)
    shift = shift.astype(F32)
    fine = step.astype(F32)

    def one(row, carry):
        length = length_rows[first_row + row]
        inverse = 1.0 / length
        norm = lax.rsqrt(length)
        for slot in range(SLOTS):
            wave = waves[slot : slot + 1, :]
            lanes = slice(slot * 256, slot * 256 + 128)
            lanes_two = slice(slot * 256 + 128, slot * 256 + 256)
            moved = turn(shift * wave, length, inverse)
            outer[row, :, lanes] = moved[0] * norm
            outer[row, :, lanes_two] = moved[1] * norm
            other = [part[7:8] for part in moved]
            small = turn(fine * wave, length, inverse)
            low = turn(8.0 * fine * wave, length, inverse)
            half = rotated([part[7:8] for part in low], [part[1:2] for part in low])
            for tile in range(2):
                if tile:
                    low = rotated(low, other)
                high = rotated(low, half)
                for coarse in range(0, 16, 2):
                    source = low if coarse < 8 else high
                    at = coarse % 8
                    pairs = [
                        rotated([part[k : k + 1] for part in source], small) for k in (at, at + 1)
                    ]
                    rows = slice(128 * tile + 8 * coarse, 128 * tile + 8 * coarse + 16)
                    for side, to in enumerate((lanes, lanes_two)):
                        inner[row, rows, to] = jnp.concatenate(
                            [pair[side] for pair in pairs], axis=0
                        ).astype(BF16)
        return carry

    lax.fori_loop(0, ROWS, one, 0)

    column = lax.broadcasted_iota(jnp.int32, (BAND, WIDE), 1)
    values = [stencil[k] for k in range(4)]
    spread_points(points, lengths, values, WIDE, column + wave_place * WIDE)

    def one_pair(pair, carry):
        for block in range(BLOCKS):
            pick = picks(points, pair, block)
            columns[pair, block, 0:144, :] = pick(144, 0)
            columns[pair, block, 144:240, :] = jnp.zeros((96, 256), BF16)
            columns[pair, block, 240:256, :] = pick(16, -16)
            rows_of[pair, block] = row_table(points, pair, block)
        return carry

    lax.fori_loop(0, BAND // 2, one_pair, 0)


def wrap_kernel(lengths, from_left, from_right, wrap_columns, wrap_rows, points):
    wave_place = lax.axis_index("wave")
    before = ring_start(wave_place - 1) + (WIDE - 128)
    behind = ring_start(wave_place + 1)
    column = lax.broadcasted_iota(jnp.int32, (BAND, 128), 1)
    values = [jnp.where(column < 64, from_right[k], from_left[k]) for k in range(4)]
    position = column + jnp.where(column < 64, behind, before)
    spread_points(points, lengths, values, 128, position)
    for pair in range(BAND // 2):
        pick = picks(points, pair, 0)
        wrap_columns[pair, 0:16, :] = pick(16, 128)
        wrap_columns[pair, 16:112, :] = jnp.zeros((96, 256), BF16)
        wrap_columns[pair, 112:128, :] = pick(16, -16)
        wrap_rows[pair] = row_table(points, pair, 0)


def fourier_kernel(mine, other, inner, outer, message, sums, shuffled):
    odd = jnp.full((SLICES, 128), lax.axis_index("wave") % 2, jnp.int32).astype(F32)
    low = (lax.broadcasted_iota(jnp.int32, (SLICES, 128), 1) < 64).astype(F32)
    to_mine = (low * odd, (1.0 - low) * (1.0 - odd))
    to_other = (low * (1.0 - odd), (1.0 - low) * odd)
    last = SLICES * (BLOCKS - 1)
    nothing = jnp.zeros((SLICES, 128), F32)

    def one(row, carry):
        own = mine[row].astype(F32)
        far = other[row].astype(F32)
        own_wrap, far_wrap = own[last + SLICES :], far[last + SLICES :]
        halves = [
            [
                own[:SLICES] + far_wrap * to_mine[0],
                own[SLICES:last],
                own[last : last + SLICES] + far_wrap * to_mine[1],
                own_wrap * (to_mine[0] + to_mine[1]),
                nothing,
                nothing[:8],
            ],
            [
                far[:SLICES] + own_wrap * to_other[0],
                far[SLICES:last],
                far[last : last + SLICES] + own_wrap * to_other[1],
                nothing,
                far_wrap * (to_other[0] + to_other[1]),
                nothing[:8],
            ],
        ]
        left = jnp.concatenate([jnp.concatenate(half, axis=0) for half in halves], axis=1)
        left = left.astype(BF16)
        base = pl.multiple_of(row * 512, 512)
        sums[pl.ds(base + 480, 32), :] = jnp.zeros((32, 128), F32)
        for slot in range(SLOTS):
            lanes = slice(256 * slot, 256 * slot + 256)
            parts = jnp.dot(left, inner[row, :, lanes], preferred_element_type=F32)
            real = jnp.zeros((SLICES, 128), F32)
            imag = jnp.zeros((SLICES, 128), F32)
            for block in range(BLOCKS + 2):
                rows = slice(SLICES * block, SLICES * block + SLICES)
                cosine, sine = parts[rows, :128], parts[rows, 128:]
                c = outer[row, block : block + 1, 256 * slot : 256 * slot + 128]
                s = outer[row, block : block + 1, 256 * slot + 128 : 256 * slot + 256]
                real = real + (c * cosine - s * sine)
                imag = imag - (s * cosine + c * sine)
            sums[pl.ds(base + slot * 48, SLICES, stride=2), :] = real
            sums[pl.ds(base + slot * 48 + 1, SLICES, stride=2), :] = imag
        return carry

    lax.fori_loop(0, ROWS, one, 0)
    for part in range(16):
        shuffled[pl.ds(part, DEVICES, stride=16), :] = sums[128 * part : 128 * part + 128, :].T
    message[...] = shuffled[...].astype(BF16)


def legendre_kernel(waves, message, table, out, flat, sorted_rows, left, result, done):
    for band in range(16):
        for core in range(2):
            total = message[8 * band + core].astype(F32)
            for z in range(1, 4):
                total = total + message[8 * band + 2 * z + core].astype(F32)
            first = (2 * band + core) * 16
            flat[first : first + 16, :] = total
    for row in range(ROWS):
        for part in range(4):
            sorted_rows[pl.ds(128 * part + row, 32, stride=4), :] = flat[
                pl.ds(4 * row + part, 32, stride=16), :
            ]
    for part in range(4):
        rows = slice(128 * part, 128 * part + 128)
        left[rows, :] = sorted_rows[rows, :].T.astype(BF16)
    copies = []
    for slot in range(SLOTS):
        product = jnp.dot(left[48 * slot : 48 * slot + 48, :], table[slot], preferred_element_type=F32)
        wave = jnp.concatenate([waves[slot : slot + 1, :]] * (product.shape[1] // 128), axis=1)
        degree = lax.broadcasted_iota(jnp.int32, product.shape, 1).astype(F32)
        result[slot] = jnp.where(degree >= wave, product, 0.0)
        copy = pltpu.make_async_copy(result.at[slot], out.at[slot], done.at[slot])
        copy.start()
        copies.append(copy)
    for copy in copies:
        copy.wait()


def local(fields, row_length, wave_order, depart_row, depart_col, frac_row, frac_col, legendre):
    ring = lax.axis_size("wave")
    bands = lax.axis_size("lat")
    scalars = lax.optimization_barrier(jnp.concatenate([row_length, wave_order]))
    lengths = scalars[:BAND]
    limit = lengths - lax.axis_index("wave") * WIDE
    live_mask = jnp.arange(WIDE, dtype=jnp.int32)[None, :] < limit[:, None]
    masked = jnp.where(live_mask[None], fields, jnp.zeros_like(fields))
    own = masked.transpose(1, 0, 2).reshape(BAND * SLICES, WIDE)

    def swapped(first):
        pairs = [(i, i + 1) for i in range(first, bands - 1, 2)]
        return lax.ppermute(own, "lat", pairs + [(j, i) for i, j in pairs])

    over = swapped(1)
    under = swapped(0)

    own, depart_row = lax.optimization_barrier((own, depart_row))
    stencil = jnp.stack([depart_row.astype(F32), depart_col.astype(F32), frac_row, frac_col])
    stencil, scalars = lax.optimization_barrier((stencil, scalars))
    ordered = scalars[BAND:].reshape(DEVICES, SLOTS).T.astype(F32)
    from_left = lax.ppermute(
        stencil[:, :, WIDE - 128 :], "wave", [(i, (i + 1) % ring) for i in range(ring)]
    )
    from_right = lax.ppermute(
        stencil[:, :, :128], "wave", [((i + 1) % ring, i) for i in range(ring)]
    )
    length_table = jnp.broadcast_to(lengths.astype(F32)[:, None], (BAND, 128))
    inner, outer, columns, rows_of, own_waves = pl.pallas_call(
        table_kernel,
        out_shape=(
            jax.ShapeDtypeStruct((ROWS, 256, SLOTS * 256), BF16),
            jax.ShapeDtypeStruct((ROWS, 8, SLOTS * 256), F32),
            jax.ShapeDtypeStruct((BAND // 2, BLOCKS, 256, 256), BF16),
            jax.ShapeDtypeStruct((BAND // 2, BLOCKS, 24, 256), F32),
            jax.ShapeDtypeStruct((SLOTS, 128), F32),
        ),
        in_specs=[VMEM] * 3,
        out_specs=(VMEM,) * 5,
        scratch_shapes=[pltpu.VMEM((BAND, 16, WIDE), F32), pltpu.VMEM((BAND, 1, 128), F32)],
        compiler_params=pltpu.CompilerParams(vmem_limit_bytes=LIMIT),
        cost_estimate=pl.CostEstimate(flops=5_000_000_000, bytes_accessed=3_000_000, transcendentals=0),
        name="tables",
    )(length_table, ordered, stencil)
    wrap_columns, wrap_rows = pl.pallas_call(
        wrap_kernel,
        out_shape=(
            jax.ShapeDtypeStruct((BAND // 2, 128, 256), BF16),
            jax.ShapeDtypeStruct((BAND // 2, 24, 256), F32),
        ),
        in_specs=[VMEM] * 3,
        out_specs=(VMEM,) * 2,
        scratch_shapes=[pltpu.VMEM((BAND, 16, 128), F32)],
        compiler_params=pltpu.CompilerParams(vmem_limit_bytes=LIMIT),
        name="wrap_tables",
    )(length_table, from_left, from_right)

    weights = (columns, rows_of, wrap_columns, wrap_rows)
    part = jax.ShapeDtypeStruct((ROWS, STACK, 128), BF16)
    send, main, edge = pl.pallas_call(
        send_kernel,
        out_shape=(
            part,
            jax.ShapeDtypeStruct((COUNT, WIDE), BF16),
            jax.ShapeDtypeStruct((COUNT, WIDE + 128), BF16),
        ),
        in_specs=[VMEM] * 7,
        out_specs=(VMEM,) * 3,
        compiler_params=pltpu.CompilerParams(vmem_limit_bytes=LIMIT),
        name="interpolate_send",
    )(own, over, under, *weights)
    other = lax.ppermute(send, "wave", [(i, i ^ 1) for i in range(ring)])
    keep = pl.pallas_call(
        keep_kernel,
        out_shape=part,
        in_specs=[VMEM] * 6,
        out_specs=VMEM,
        compiler_params=pltpu.CompilerParams(vmem_limit_bytes=LIMIT),
        cost_estimate=pl.CostEstimate(flops=5_000_000_000, bytes_accessed=3_000_000, transcendentals=0),
        name="interpolate_keep",
    )(main, edge, *weights)
    message = pl.pallas_call(
        fourier_kernel,
        out_shape=jax.ShapeDtypeStruct((DEVICES * 16, 128), BF16),
        in_specs=[VMEM] * 4,
        out_specs=VMEM,
        scratch_shapes=[
            pltpu.VMEM((ROWS * 512, 128), F32),
            pltpu.VMEM((DEVICES * 16, 128), F32),
        ],
        compiler_params=pltpu.CompilerParams(vmem_limit_bytes=LIMIT),
        name="fourier",
    )(keep, other, inner, outer)
    message = lax.all_to_all(
        message.reshape(DEVICES, 16, 128), ("lat", "wave"), split_axis=0, concat_axis=0, tiled=True
    )
    degrees = legendre.shape[2]
    return pl.pallas_call(
        legendre_kernel,
        out_shape=jax.ShapeDtypeStruct((SLOTS, 2 * SLICES, degrees), F32),
        in_specs=[VMEM] * 3,
        out_specs=pl.BlockSpec(memory_space=pl.ANY),
        scratch_shapes=[
            pltpu.VMEM((512, 128), F32),
            pltpu.VMEM((512, 128), F32),
            pltpu.VMEM((512, 128), BF16),
            pltpu.VMEM((SLOTS, 2 * SLICES, degrees), F32),
            pltpu.SemaphoreType.DMA((SLOTS,)),
        ],
        compiler_params=pltpu.CompilerParams(vmem_limit_bytes=LIMIT),
        name="legendre",
    )(own_waves, message, legendre)


def solution(mesh):
    placed = (
        P(None, "lat", "wave"),
        P("lat"),
        P(),
        P("lat", "wave"),
        P("lat", "wave"),
        P("lat", "wave"),
        P("lat", "wave"),
        P(("lat", "wave"), None, None),
    )
    return jax.shard_map(
        local, mesh=mesh, in_specs=placed, out_specs=P(("lat", "wave"), None, None), check_vma=False
    )
```

```python
import math

import jax
import jax.numpy as jnp
from jax import lax
from jax.experimental import pallas as pl
from jax.experimental.pallas import tpu as pltpu
from jax.sharding import PartitionSpec as P

F32 = jnp.float32
BF16 = jnp.bfloat16
VMEM = pl.BlockSpec(memory_space=pltpu.VMEM)
LIMIT = 24 * 1024 * 1024

SLICES = 24
BAND = 8
WIDE = 640
BLOCKS = 5
SLOTS = 10
PEERS = 64
GROUPS = 5
ROWS = 4
STACK = 144
COUNT = 3 * BAND * SLICES


def cubic_weights(fraction):
    return (
        -fraction * (fraction - 1.0) * (fraction - 2.0) / 6.0,
        (fraction + 1.0) * (fraction - 1.0) * (fraction - 2.0) / 2.0,
        -(fraction + 1.0) * fraction * (fraction - 2.0) / 2.0,
        (fraction + 1.0) * fraction * (fraction - 1.0) / 6.0,
    )


def picked_weight(distance, weights):
    chosen = jnp.where(distance == 3, weights[3], jnp.zeros_like(weights[3]))
    for step in (2, 1, 0):
        chosen = jnp.where(distance == step, weights[step], chosen)
    return chosen


def weighted(spread, rows_of, half):
    side = slice(128 * half, 128 * half + 128)
    total = jnp.zeros((SLICES, 128), F32)
    for row in range(half, half + 17):
        total = total + rows_of[row : row + 1, side] * spread[
            SLICES * row : SLICES * row + SLICES, side
        ]
    return total


def interpolate(steps, main, edge, columns, rows_of, wrap_columns, wrap_rows, out):
    for pair in steps:
        window = slice(pair * 2 * SLICES, pair * 2 * SLICES + 18 * SLICES)
        totals = ([], [])
        for block in range(BLOCKS + 1):
            lanes = slice(128 * block, 128 * block + 128)
            if block < BLOCKS:
                left = jnp.concatenate([main[window, lanes], edge[window, lanes]], axis=1)
                table, rows = columns[pair, block], rows_of.at[pair, block]
            else:
                left, table, rows = edge[window, lanes], wrap_columns[pair], wrap_rows.at[pair]
            spread = jnp.dot(left, table, preferred_element_type=F32)
            for half in range(2):
                totals[half].append(weighted(spread, rows, half))
        for half in range(2):
            out[(2 * pair + half) % ROWS] = jnp.concatenate(totals[half], axis=0).astype(BF16)


def upper_kernel(
    own, first, second, columns, rows_of, wrap_columns, wrap_rows, out, main, edge
):
    size = BAND * SLICES
    odd = lax.axis_index("lat") % 2
    main[pl.ds(pl.multiple_of(odd * 2 * size, size), size), :] = first[...]
    main[size : 2 * size, :] = own[...]
    main[pl.ds(pl.multiple_of((1 - odd) * 2 * size, size), size), :] = second[...]
    nothing = jnp.zeros((COUNT, 64), BF16)
    for block in range(BLOCKS):
        at = 128 * block
        sides = [
            main[:, at + 128 : at + 192] if block < BLOCKS - 1 else nothing,
            main[:, at - 64 : at] if block else nothing,
        ]
        edge[:, at : at + 128] = jnp.concatenate(sides, axis=1)
    edge[:, WIDE:] = jnp.concatenate([main[:, :64], main[:, WIDE - 64 :]], axis=1)
    interpolate((0, 1), main, edge, columns, rows_of, wrap_columns, wrap_rows, out)


def lower_kernel(main, edge, columns, rows_of, wrap_columns, wrap_rows, out):
    interpolate((2, 3), main, edge, columns, rows_of, wrap_columns, wrap_rows, out)


def turn(count, length, inverse):
    whole = jnp.floor(count * inverse + 0.5)
    angle = (count - whole * length) * (inverse * math.pi)
    square = angle * angle
    sine = angle * (
        1.0
        + square
        * (
            -1.0 / 6
            + square
            * (1.0 / 120 + square * (-1.0 / 5040 + square * (1.0 / 362880 - square / 39916800)))
        )
    )
    cosine = 1.0 + square * (
        -0.5
        + square
        * (
            1.0 / 24
            + square
            * (-1.0 / 720 + square * (1.0 / 40320 + square * (-1.0 / 3628800 + square / 479001600)))
        )
    )
    return 1.0 - 2.0 * sine * sine, 2.0 * sine * cosine


def rotated(one, two):
    return one[0] * two[0] - one[1] * two[1], one[1] * two[0] + one[0] * two[1]


def ring_start(place):
    return lax.rem(place + 8, 8) * WIDE


def spread_points(target, lengths, values, width, position):
    lane = (lax.broadcasted_iota(jnp.int32, (1, width), 1) % 128).astype(F32)
    limit = jnp.concatenate([lengths[...]] * (width // 128), axis=1)
    live = position.astype(F32) < limit
    for base, first, fraction in (
        (0, values[1] + (lane - 1.0), values[3]),
        (8, values[0] + (BAND - 1.0), values[2]),
    ):
        for k, value in enumerate((first,) + cubic_weights(fraction)):
            if base and k:
                value = jnp.where(live, value, 0.0)
            for row in range(BAND):
                target[row, base + k : base + k + 1, :] = value[row : row + 1, :]


def row_of(ref, pair, item, block):
    return jnp.concatenate(
        [
            ref[2 * pair + half, item : item + 1, 128 * block : 128 * block + 128]
            for half in range(2)
        ],
        axis=1,
    )


def picks(ref, pair, block):
    start = row_of(ref, pair, 0, block).astype(BF16)
    weights = [row_of(ref, pair, 1 + k, block).astype(BF16) for k in range(4)]

    def pick(count, first):
        source = lax.broadcasted_iota(jnp.int32, (count, 256), 0) + first
        return picked_weight(source.astype(F32).astype(BF16) - start, weights)

    return pick


def row_table(ref, pair, block):
    half = (lax.broadcasted_iota(jnp.int32, (1, 256), 1) >= 128).astype(F32)
    start = row_of(ref, pair, 8, block) + half
    weights = [row_of(ref, pair, 9 + k, block) for k in range(4)]
    source = lax.broadcasted_iota(jnp.int32, (24, 256), 0).astype(F32)
    return picked_weight(source - start, weights)


def table_kernel(
    lengths, waves, stencil, inner, outer, columns, rows_of, own_waves, points, length_rows
):
    wave_place = lax.axis_index("wave")
    core = wave_place % 2
    peer = lax.axis_index("lat") * 4 + wave_place // 2
    slots = jnp.where(core == 0, waves[:SLOTS, :], waves[SLOTS:, :])
    lane = lax.broadcasted_iota(jnp.int32, (SLOTS, PEERS), 1)
    mine = jnp.sum(jnp.where(lane == peer, slots, 0.0), axis=1, keepdims=True)
    own_waves[...] = jnp.broadcast_to(mine, (SLOTS, 128))
    groups = [
        jnp.concatenate([slots[k : k + 1], slots[k + 1 : k + 2]], axis=1)
        for k in range(0, SLOTS, 2)
    ]
    for row in range(BAND):
        length_rows[row] = lengths[row : row + 1, :]
    step = lax.broadcasted_iota(jnp.int32, (8, 128), 0)
    other_place = wave_place ^ 1
    away = (other_place - wave_place) * WIDE
    before = ring_start(wave_place - 1) + (WIDE - 128)
    behind = ring_start(wave_place + 1)
    other_before = ring_start(other_place - 1) + (WIDE - 128)
    other_behind = ring_start(other_place + 1)
    outside = jnp.where(core == 0, before, behind)
    other_outside = jnp.where(core == 0, other_behind, other_before) - away
    shift = 128 * step + wave_place * WIDE
    for at, value in ((5, outside), (6, other_outside), (7, away)):
        shift = jnp.where(step == at, value, shift)
    shift = shift.astype(F32)
    fine = step.astype(F32)

    def one(row, carry):
        length = length_rows[row]
        inverse = 1.0 / length
        norm = lax.rsqrt(length)
        for group, wave in enumerate(groups):
            lanes = slice(group * 256, group * 256 + 128)
            lanes_two = slice(group * 256 + 128, group * 256 + 256)
            moved = turn(shift * wave, length, inverse)
            outer[row, :, lanes] = moved[0] * norm
            outer[row, :, lanes_two] = moved[1] * norm
            other = [part[7:8] for part in moved]
            small = turn(fine * wave, length, inverse)
            low = turn(8.0 * fine * wave, length, inverse)
            half = rotated([part[7:8] for part in low], [part[1:2] for part in low])
            for tile in range(2):
                if tile:
                    low = rotated(low, other)
                high = rotated(low, half)
                for coarse in range(0, 16, 2):
                    source = low if coarse < 8 else high
                    at = coarse % 8
                    pairs = [
                        rotated([part[k : k + 1] for part in source], small) for k in (at, at + 1)
                    ]
                    rows = slice(128 * tile + 8 * coarse, 128 * tile + 8 * coarse + 16)
                    for side, to in enumerate((lanes, lanes_two)):
                        inner[row, rows, to] = jnp.concatenate(
                            [pair[side] for pair in pairs], axis=0
                        ).astype(BF16)
        return carry

    lax.fori_loop(0, BAND, one, 0)

    column = lax.broadcasted_iota(jnp.int32, (BAND, WIDE), 1)
    values = [stencil[k] for k in range(4)]
    spread_points(points, lengths, values, WIDE, column + wave_place * WIDE)

    def one_pair(pair, carry):
        for block in range(BLOCKS):
            pick = picks(points, pair, block)
            columns[pair, block, 0:144, :] = pick(144, 0)
            columns[pair, block, 144:240, :] = jnp.zeros((96, 256), BF16)
            columns[pair, block, 240:256, :] = pick(16, -16)
            rows_of[pair, block] = row_table(points, pair, block)
        return carry

    lax.fori_loop(0, BAND // 2, one_pair, 0)


def wrap_kernel(lengths, from_left, from_right, wrap_columns, wrap_rows, points):
    wave_place = lax.axis_index("wave")
    before = ring_start(wave_place - 1) + (WIDE - 128)
    behind = ring_start(wave_place + 1)
    column = lax.broadcasted_iota(jnp.int32, (BAND, 128), 1)
    values = [jnp.where(column < 64, from_right[k], from_left[k]) for k in range(4)]
    position = column + jnp.where(column < 64, behind, before)
    spread_points(points, lengths, values, 128, position)
    for pair in range(BAND // 2):
        pick = picks(points, pair, 0)
        wrap_columns[pair, 0:16, :] = pick(16, 128)
        wrap_columns[pair, 16:112, :] = jnp.zeros((96, 256), BF16)
        wrap_columns[pair, 112:128, :] = pick(16, -16)
        wrap_rows[pair] = row_table(points, pair, 0)


def fourier(first, mine, other, inner, outer, sums, shuffled):
    odd = jnp.full((SLICES, 128), lax.axis_index("wave") % 2, jnp.int32).astype(F32)
    low = (lax.broadcasted_iota(jnp.int32, (SLICES, 128), 1) < 64).astype(F32)
    to_mine = (low * odd, (1.0 - low) * (1.0 - odd))
    to_other = (low * (1.0 - odd), (1.0 - low) * odd)
    last = SLICES * (BLOCKS - 1)
    nothing = jnp.zeros((SLICES, 128), F32)

    for row in range(ROWS):
        own = mine[row].astype(F32)
        far = other[row].astype(F32)
        own_wrap, far_wrap = own[last + SLICES :], far[last + SLICES :]
        halves = [
            [
                own[:SLICES] + far_wrap * to_mine[0],
                own[SLICES:last],
                own[last : last + SLICES] + far_wrap * to_mine[1],
                own_wrap * (to_mine[0] + to_mine[1]),
                nothing,
                nothing[:8],
            ],
            [
                far[:SLICES] + own_wrap * to_other[0],
                far[SLICES:last],
                far[last : last + SLICES] + own_wrap * to_other[1],
                nothing,
                far_wrap * (to_other[0] + to_other[1]),
                nothing[:8],
            ],
        ]
        left = jnp.concatenate([jnp.concatenate(half, axis=0) for half in halves], axis=1)
        left = left.astype(BF16)
        base = 256 * row
        sums[base + 240 : base + 256, :] = jnp.zeros((16, 128), F32)
        for group in range(GROUPS):
            lanes = slice(256 * group, 256 * group + 256)
            parts = jnp.dot(left, inner[first + row, :, lanes], preferred_element_type=F32)
            real = jnp.zeros((SLICES, 128), F32)
            imag = jnp.zeros((SLICES, 128), F32)
            for block in range(BLOCKS + 2):
                rows = slice(SLICES * block, SLICES * block + SLICES)
                cosine, sine = parts[rows, :128], parts[rows, 128:]
                factor = outer[first + row, block : block + 1, lanes]
                c, s = factor[:, :128], factor[:, 128:]
                real = real + (c * cosine - s * sine)
                imag = imag - (s * cosine + c * sine)
            sums[pl.ds(base + group * 48, SLICES, stride=2), :] = real
            sums[pl.ds(base + group * 48 + 1, SLICES, stride=2), :] = imag
        for half in range(2):
            turned = sums[base + 128 * half : base + 128 * half + 128, :].T
            for side in range(2):
                at = 4 * row + 2 * side + half
                shuffled[pl.ds(at, PEERS, stride=16), :] = turned[PEERS * side : PEERS * side + PEERS]


def upper_fourier_kernel(mine, other, inner, outer, message, sums, shuffled):
    fourier(0, mine, other, inner, outer, sums, shuffled)
    message[...] = shuffled[...].astype(BF16)


def lower_fourier_kernel(mine, other, inner, outer, upper, message, sums, shuffled):
    fourier(ROWS, mine, other, inner, outer, sums, shuffled)
    for peer in range(PEERS):
        rows = slice(16 * peer, 16 * peer + 16)
        message[32 * peer : 32 * peer + 16, :] = upper[rows, :]
        message[32 * peer + 16 : 32 * peer + 32, :] = shuffled[rows, :].astype(BF16)


def legendre_kernel(waves, message, table, out, flat, sorted_rows, left, result, done):
    for band in range(16):
        total = message[4 * band].astype(F32)
        for z in range(1, 4):
            total = total + message[4 * band + z].astype(F32)
        flat[32 * band : 32 * band + 32, :] = total
    for row in range(BAND):
        for part in range(4):
            sorted_rows[pl.ds(128 * part + row, 16, stride=8), :] = flat[
                pl.ds(4 * row + part, 16, stride=32), :
            ]
    for part in range(4):
        rows = slice(128 * part, 128 * part + 128)
        left[rows, :] = sorted_rows[rows, :].T.astype(BF16)
    copies = []
    for slot in range(SLOTS):
        first = 256 * (slot % 2) + 48 * (slot // 2)
        product = jnp.dot(left[first : first + 48, :], table[slot], preferred_element_type=F32)
        wave = jnp.concatenate([waves[slot : slot + 1, :]] * (product.shape[1] // 128), axis=1)
        degree = lax.broadcasted_iota(jnp.int32, product.shape, 1).astype(F32)
        result[slot] = jnp.where(degree >= wave, product, 0.0)
        copy = pltpu.make_async_copy(result.at[slot], out.at[slot], done.at[slot])
        copy.start()
        copies.append(copy)
    for copy in copies:
        copy.wait()


def local(fields, row_length, wave_order, depart_row, depart_col, frac_row, frac_col, legendre):
    ring = lax.axis_size("wave")
    bands = lax.axis_size("lat")
    scalars = lax.optimization_barrier(jnp.concatenate([row_length, wave_order]))
    lengths = scalars[:BAND]
    limit = lengths - lax.axis_index("wave") * WIDE
    live_mask = jnp.arange(WIDE, dtype=jnp.int32)[None, :] < limit[:, None]
    masked = jnp.where(live_mask[None], fields, jnp.zeros_like(fields))
    own = masked.transpose(1, 0, 2).reshape(BAND * SLICES, WIDE)

    def swapped(first):
        pairs = [(i, i + 1) for i in range(first, bands - 1, 2)]
        return lax.ppermute(own, "lat", pairs + [(j, i) for i, j in pairs])

    over = swapped(1)
    under = swapped(0)

    own, depart_row = lax.optimization_barrier((own, depart_row))
    stencil = jnp.stack([depart_row.astype(F32), depart_col.astype(F32), frac_row, frac_col])
    stencil, scalars = lax.optimization_barrier((stencil, scalars))
    ordered = scalars[BAND:].reshape(PEERS, 2 * SLOTS).T.astype(F32)
    from_left = lax.ppermute(
        stencil[:, :, WIDE - 128 :], "wave", [(i, (i + 1) % ring) for i in range(ring)]
    )
    from_right = lax.ppermute(
        stencil[:, :, :128], "wave", [((i + 1) % ring, i) for i in range(ring)]
    )
    length_table = jnp.broadcast_to(lengths.astype(F32)[:, None], (BAND, 128))
    inner, outer, columns, rows_of, own_waves = pl.pallas_call(
        table_kernel,
        out_shape=(
            jax.ShapeDtypeStruct((BAND, 256, GROUPS * 256), BF16),
            jax.ShapeDtypeStruct((BAND, 8, GROUPS * 256), F32),
            jax.ShapeDtypeStruct((BAND // 2, BLOCKS, 256, 256), BF16),
            jax.ShapeDtypeStruct((BAND // 2, BLOCKS, 24, 256), F32),
            jax.ShapeDtypeStruct((SLOTS, 128), F32),
        ),
        in_specs=[VMEM] * 3,
        out_specs=(VMEM,) * 5,
        scratch_shapes=[pltpu.VMEM((BAND, 16, WIDE), F32), pltpu.VMEM((BAND, 1, 128), F32)],
        compiler_params=pltpu.CompilerParams(vmem_limit_bytes=LIMIT),
        cost_estimate=pl.CostEstimate(flops=5_000_000_000, bytes_accessed=3_000_000, transcendentals=0),
        name="tables",
    )(length_table, ordered, stencil)
    wrap_columns, wrap_rows = pl.pallas_call(
        wrap_kernel,
        out_shape=(
            jax.ShapeDtypeStruct((BAND // 2, 128, 256), BF16),
            jax.ShapeDtypeStruct((BAND // 2, 24, 256), F32),
        ),
        in_specs=[VMEM] * 3,
        out_specs=(VMEM,) * 2,
        scratch_shapes=[pltpu.VMEM((BAND, 16, 128), F32)],
        compiler_params=pltpu.CompilerParams(vmem_limit_bytes=LIMIT),
        name="wrap_tables",
    )(length_table, from_left, from_right)

    weights = (columns, rows_of, wrap_columns, wrap_rows)
    part = jax.ShapeDtypeStruct((ROWS, STACK, 128), BF16)
    upper, main, edge = pl.pallas_call(
        upper_kernel,
        out_shape=(
            part,
            jax.ShapeDtypeStruct((COUNT, WIDE), BF16),
            jax.ShapeDtypeStruct((COUNT, WIDE + 128), BF16),
        ),
        in_specs=[VMEM] * 7,
        out_specs=(VMEM,) * 3,
        compiler_params=pltpu.CompilerParams(vmem_limit_bytes=LIMIT),
        name="interpolate_upper",
    )(own, over, under, *weights)
    cores = [(i, i ^ 1) for i in range(ring)]
    other_upper = lax.ppermute(upper, "wave", cores)
    lower = pl.pallas_call(
        lower_kernel,
        out_shape=part,
        in_specs=[VMEM] * 6,
        out_specs=VMEM,
        compiler_params=pltpu.CompilerParams(vmem_limit_bytes=LIMIT),
        cost_estimate=pl.CostEstimate(flops=5_000_000_000, bytes_accessed=3_000_000, transcendentals=0),
        name="interpolate_lower",
    )(main, edge, *weights)
    other_lower = lax.ppermute(lower, "wave", cores)
    scratch = [pltpu.VMEM((ROWS * 256, 128), F32), pltpu.VMEM((PEERS * 16, 128), F32)]
    message = pl.pallas_call(
        upper_fourier_kernel,
        out_shape=jax.ShapeDtypeStruct((PEERS * 16, 128), BF16),
        in_specs=[VMEM] * 4,
        out_specs=VMEM,
        scratch_shapes=scratch,
        compiler_params=pltpu.CompilerParams(vmem_limit_bytes=LIMIT),
        cost_estimate=pl.CostEstimate(flops=5_000_000_000, bytes_accessed=3_000_000, transcendentals=0),
        name="fourier_upper",
    )(upper, other_upper, inner, outer)
    message = pl.pallas_call(
        lower_fourier_kernel,
        out_shape=jax.ShapeDtypeStruct((PEERS * 32, 128), BF16),
        in_specs=[VMEM] * 5,
        out_specs=VMEM,
        scratch_shapes=scratch,
        compiler_params=pltpu.CompilerParams(vmem_limit_bytes=LIMIT),
        name="fourier_lower",
    )(lower, other_lower, inner, outer, message)
    message = lax.all_to_all(
        message.reshape(PEERS, 32, 128),
        ("lat", "wave"),
        split_axis=0,
        concat_axis=0,
        tiled=True,
        axis_index_groups=[[2 * peer + core for peer in range(PEERS)] for core in range(2)],
    )
    degrees = legendre.shape[2]
    return pl.pallas_call(
        legendre_kernel,
        out_shape=jax.ShapeDtypeStruct((SLOTS, 2 * SLICES, degrees), F32),
        in_specs=[VMEM] * 3,
        out_specs=pl.BlockSpec(memory_space=pl.ANY),
        scratch_shapes=[
            pltpu.VMEM((512, 128), F32),
            pltpu.VMEM((512, 128), F32),
            pltpu.VMEM((512, 128), BF16),
            pltpu.VMEM((SLOTS, 2 * SLICES, degrees), F32),
            pltpu.SemaphoreType.DMA((SLOTS,)),
        ],
        compiler_params=pltpu.CompilerParams(vmem_limit_bytes=LIMIT),
        name="legendre",
    )(own_waves, message, legendre)


def solution(mesh):
    placed = (
        P(None, "lat", "wave"),
        P("lat"),
        P(),
        P("lat", "wave"),
        P("lat", "wave"),
        P("lat", "wave"),
        P("lat", "wave"),
        P(("lat", "wave"), None, None),
    )
    return jax.shard_map(
        local, mesh=mesh, in_specs=placed, out_specs=P(("lat", "wave"), None, None), check_vma=False
    )
```

```python
import math

import jax
import jax.numpy as jnp
from jax import lax
from jax.experimental import pallas as pl
from jax.experimental.pallas import tpu as pltpu
from jax.sharding import PartitionSpec as P

F32 = jnp.float32
BF16 = jnp.bfloat16
VMEM = pl.BlockSpec(memory_space=pltpu.VMEM)
LIMIT = 24 * 1024 * 1024

SLICES = 24
BAND = 8
WIDE = 640
BLOCKS = 5
SLOTS = 10
PEERS = 64
GROUPS = 5
ROWS = 4
STACK = 144
COUNT = 3 * BAND * SLICES


def cubic_weights(fraction):
    return (
        -fraction * (fraction - 1.0) * (fraction - 2.0) / 6.0,
        (fraction + 1.0) * (fraction - 1.0) * (fraction - 2.0) / 2.0,
        -(fraction + 1.0) * fraction * (fraction - 2.0) / 2.0,
        (fraction + 1.0) * fraction * (fraction - 1.0) / 6.0,
    )


def picked_weight(distance, weights):
    chosen = jnp.where(distance == 3, weights[3], jnp.zeros_like(weights[3]))
    for step in (2, 1, 0):
        chosen = jnp.where(distance == step, weights[step], chosen)
    return chosen


def weighted(spread, rows_of, half):
    side = slice(128 * half, 128 * half + 128)
    total = jnp.zeros((SLICES, 128), F32)
    for row in range(half, half + 17):
        total = total + rows_of[row : row + 1, side] * spread[
            SLICES * row : SLICES * row + SLICES, side
        ]
    return total


def interpolate(steps, main, edge, columns, rows_of, wrap_columns, wrap_rows, out):
    for pair in steps:
        window = slice(pair * 2 * SLICES, pair * 2 * SLICES + 18 * SLICES)
        totals = ([], [])
        for block in range(BLOCKS + 1):
            lanes = slice(128 * block, 128 * block + 128)
            if block < BLOCKS:
                left = jnp.concatenate([main[window, lanes], edge[window, lanes]], axis=1)
                table, rows = columns[pair, block], rows_of.at[pair, block]
            else:
                left, table, rows = edge[window, lanes], wrap_columns[pair], wrap_rows.at[pair]
            spread = jnp.dot(left, table, preferred_element_type=F32)
            for half in range(2):
                totals[half].append(weighted(spread, rows, half))
        for half in range(2):
            out[(2 * pair + half) % ROWS] = jnp.concatenate(totals[half], axis=0).astype(BF16)


def upper_kernel(
    own, second, first, columns, rows_of, wrap_columns, wrap_rows, out, main, edge
):
    size = BAND * SLICES
    odd = lax.axis_index("lat") % 2
    main[pl.ds(pl.multiple_of(odd * 2 * size, size), size), :] = first[...]
    main[size : 2 * size, :] = own[...]
    main[pl.ds(pl.multiple_of((1 - odd) * 2 * size, size), size), :] = second[...]
    nothing = jnp.zeros((COUNT, 64), BF16)
    for block in range(BLOCKS):
        at = 128 * block
        sides = [
            main[:, at + 128 : at + 192] if block < BLOCKS - 1 else nothing,
            main[:, at - 64 : at] if block else nothing,
        ]
        edge[:, at : at + 128] = jnp.concatenate(sides, axis=1)
    edge[:, WIDE:] = jnp.concatenate([main[:, :64], main[:, WIDE - 64 :]], axis=1)
    interpolate((0, 1), main, edge, columns, rows_of, wrap_columns, wrap_rows, out)


def lower_kernel(main, edge, columns, rows_of, wrap_columns, wrap_rows, out):
    interpolate((2, 3), main, edge, columns, rows_of, wrap_columns, wrap_rows, out)


def turn(count, length, inverse):
    whole = jnp.floor(count * inverse + 0.5)
    angle = (count - whole * length) * (inverse * math.pi)
    square = angle * angle
    sine = angle * (
        1.0
        + square
        * (
            -1.0 / 6
            + square
            * (1.0 / 120 + square * (-1.0 / 5040 + square * (1.0 / 362880 - square / 39916800)))
        )
    )
    cosine = 1.0 + square * (
        -0.5
        + square
        * (
            1.0 / 24
            + square
            * (-1.0 / 720 + square * (1.0 / 40320 + square * (-1.0 / 3628800 + square / 479001600)))
        )
    )
    return 1.0 - 2.0 * sine * sine, 2.0 * sine * cosine


def rotated(one, two):
    return one[0] * two[0] - one[1] * two[1], one[1] * two[0] + one[0] * two[1]


def ring_start(place):
    return lax.rem(place + 8, 8) * WIDE


def spread_points(target, lengths, values, width, position):
    lane = (lax.broadcasted_iota(jnp.int32, (1, width), 1) % 128).astype(F32)
    limit = jnp.concatenate([lengths[...]] * (width // 128), axis=1)
    live = position.astype(F32) < limit
    for base, first, fraction in (
        (0, values[1] + (lane - 1.0), values[3]),
        (8, values[0] + (BAND - 1.0), values[2]),
    ):
        for k, value in enumerate((first,) + cubic_weights(fraction)):
            if base and k:
                value = jnp.where(live, value, 0.0)
            for row in range(BAND):
                target[row, base + k : base + k + 1, :] = value[row : row + 1, :]


def row_of(ref, pair, item, block):
    return jnp.concatenate(
        [
            ref[2 * pair + half, item : item + 1, 128 * block : 128 * block + 128]
            for half in range(2)
        ],
        axis=1,
    )


def picks(ref, pair, block):
    start = row_of(ref, pair, 0, block).astype(BF16)
    weights = [row_of(ref, pair, 1 + k, block).astype(BF16) for k in range(4)]

    def pick(count, first):
        source = lax.broadcasted_iota(jnp.int32, (count, 256), 0) + first
        return picked_weight(source.astype(F32).astype(BF16) - start, weights)

    return pick


def row_table(ref, pair, block):
    half = (lax.broadcasted_iota(jnp.int32, (1, 256), 1) >= 128).astype(F32)
    start = row_of(ref, pair, 8, block) + half
    weights = [row_of(ref, pair, 9 + k, block) for k in range(4)]
    source = lax.broadcasted_iota(jnp.int32, (24, 256), 0).astype(F32)
    return picked_weight(source - start, weights)


def table_kernel(
    lengths, waves, stencil, inner, outer, columns, rows_of, own_waves, points, length_rows
):
    wave_place = lax.axis_index("wave")
    core = wave_place % 2
    peer = lax.axis_index("lat") * 4 + wave_place // 2
    slots = jnp.where(core == 0, waves[:SLOTS, :], waves[SLOTS:, :])
    lane = lax.broadcasted_iota(jnp.int32, (SLOTS, PEERS), 1)
    mine = jnp.sum(jnp.where(lane == peer, slots, 0.0), axis=1, keepdims=True)
    own_waves[...] = jnp.broadcast_to(mine, (SLOTS, 128))
    groups = [
        jnp.concatenate([slots[k : k + 1], slots[k + 1 : k + 2]], axis=1)
        for k in range(0, SLOTS, 2)
    ]
    for row in range(BAND):
        length_rows[row] = lengths[row : row + 1, :]
    step = lax.broadcasted_iota(jnp.int32, (8, 128), 0)
    other_place = wave_place ^ 1
    away = (other_place - wave_place) * WIDE
    before = ring_start(wave_place - 1) + (WIDE - 128)
    behind = ring_start(wave_place + 1)
    other_before = ring_start(other_place - 1) + (WIDE - 128)
    other_behind = ring_start(other_place + 1)
    outside = jnp.where(core == 0, before, behind)
    other_outside = jnp.where(core == 0, other_behind, other_before) - away
    shift = 128 * step + wave_place * WIDE
    for at, value in ((5, outside), (6, other_outside), (7, away)):
        shift = jnp.where(step == at, value, shift)
    shift = shift.astype(F32)
    fine = step.astype(F32)

    def one(row, carry):
        length = length_rows[row]
        inverse = 1.0 / length
        norm = lax.rsqrt(length)
        for group, wave in enumerate(groups):
            lanes = slice(group * 256, group * 256 + 128)
            lanes_two = slice(group * 256 + 128, group * 256 + 256)
            moved = turn(shift * wave, length, inverse)
            outer[row, :, lanes] = moved[0] * norm
            outer[row, :, lanes_two] = moved[1] * norm
            other = [part[7:8] for part in moved]
            small = turn(fine * wave, length, inverse)
            low = turn(8.0 * fine * wave, length, inverse)
            half = rotated([part[7:8] for part in low], [part[1:2] for part in low])
            for tile in range(2):
                if tile:
                    low = rotated(low, other)
                high = rotated(low, half)
                for coarse in range(0, 16, 2):
                    source = low if coarse < 8 else high
                    at = coarse % 8
                    pairs = [
                        rotated([part[k : k + 1] for part in source], small) for k in (at, at + 1)
                    ]
                    rows = slice(128 * tile + 8 * coarse, 128 * tile + 8 * coarse + 16)
                    for side, to in enumerate((lanes, lanes_two)):
                        inner[row, rows, to] = jnp.concatenate(
                            [pair[side] for pair in pairs], axis=0
                        ).astype(BF16)
        return carry

    lax.fori_loop(0, BAND, one, 0)

    column = lax.broadcasted_iota(jnp.int32, (BAND, WIDE), 1)
    values = [stencil[k] for k in range(4)]
    spread_points(points, lengths, values, WIDE, column + wave_place * WIDE)

    def one_pair(pair, carry):
        for block in range(BLOCKS):
            pick = picks(points, pair, block)
            columns[pair, block, 0:144, :] = pick(144, 0)
            columns[pair, block, 144:240, :] = jnp.zeros((96, 256), BF16)
            columns[pair, block, 240:256, :] = pick(16, -16)
            rows_of[pair, block] = row_table(points, pair, block)
        return carry

    lax.fori_loop(0, BAND // 2, one_pair, 0)


def wrap_kernel(lengths, from_left, from_right, wrap_columns, wrap_rows, points):
    wave_place = lax.axis_index("wave")
    before = ring_start(wave_place - 1) + (WIDE - 128)
    behind = ring_start(wave_place + 1)
    column = lax.broadcasted_iota(jnp.int32, (BAND, 128), 1)
    values = [jnp.where(column < 64, from_right[k], from_left[k]) for k in range(4)]
    position = column + jnp.where(column < 64, behind, before)
    spread_points(points, lengths, values, 128, position)
    for pair in range(BAND // 2):
        pick = picks(points, pair, 0)
        wrap_columns[pair, 0:16, :] = pick(16, 128)
        wrap_columns[pair, 16:112, :] = jnp.zeros((96, 256), BF16)
        wrap_columns[pair, 112:128, :] = pick(16, -16)
        wrap_rows[pair] = row_table(points, pair, 0)


def fourier(first, mine, other, inner, outer, sums, shuffled):
    odd = jnp.full((SLICES, 128), lax.axis_index("wave") % 2, jnp.int32).astype(F32)
    low = (lax.broadcasted_iota(jnp.int32, (SLICES, 128), 1) < 64).astype(F32)
    to_mine = (low * odd, (1.0 - low) * (1.0 - odd))
    to_other = (low * (1.0 - odd), (1.0 - low) * odd)
    last = SLICES * (BLOCKS - 1)
    nothing = jnp.zeros((SLICES, 128), F32)

    for row in range(ROWS):
        own = mine[row].astype(F32)
        far = other[row].astype(F32)
        own_wrap, far_wrap = own[last + SLICES :], far[last + SLICES :]
        halves = [
            [
                own[:SLICES] + far_wrap * to_mine[0],
                own[SLICES:last],
                own[last : last + SLICES] + far_wrap * to_mine[1],
                own_wrap * (to_mine[0] + to_mine[1]),
                nothing,
                nothing[:8],
            ],
            [
                far[:SLICES] + own_wrap * to_other[0],
                far[SLICES:last],
                far[last : last + SLICES] + own_wrap * to_other[1],
                nothing,
                far_wrap * (to_other[0] + to_other[1]),
                nothing[:8],
            ],
        ]
        left = jnp.concatenate([jnp.concatenate(half, axis=0) for half in halves], axis=1)
        left = left.astype(BF16)
        base = 256 * row
        sums[base + 240 : base + 256, :] = jnp.zeros((16, 128), F32)
        for group in range(GROUPS):
            lanes = slice(256 * group, 256 * group + 256)
            parts = jnp.dot(left, inner[first + row, :, lanes], preferred_element_type=F32)
            real = jnp.zeros((SLICES, 128), F32)
            imag = jnp.zeros((SLICES, 128), F32)
            for block in range(BLOCKS + 2):
                rows = slice(SLICES * block, SLICES * block + SLICES)
                cosine, sine = parts[rows, :128], parts[rows, 128:]
                factor = outer[first + row, block : block + 1, lanes]
                c, s = factor[:, :128], factor[:, 128:]
                real = real + (c * cosine - s * sine)
                imag = imag - (s * cosine + c * sine)
            sums[pl.ds(base + group * 48, SLICES, stride=2), :] = real
            sums[pl.ds(base + group * 48 + 1, SLICES, stride=2), :] = imag
        for half in range(2):
            turned = sums[base + 128 * half : base + 128 * half + 128, :].T
            for side in range(2):
                at = 4 * row + 2 * side + half
                shuffled[pl.ds(at, PEERS, stride=16), :] = turned[PEERS * side : PEERS * side + PEERS]


def upper_fourier_kernel(mine, other, inner, outer, message, sums, shuffled):
    fourier(0, mine, other, inner, outer, sums, shuffled)
    message[...] = shuffled[...].astype(BF16)


def lower_fourier_kernel(mine, other, inner, outer, upper, message, sums, shuffled):
    fourier(ROWS, mine, other, inner, outer, sums, shuffled)
    for peer in range(PEERS):
        rows = slice(16 * peer, 16 * peer + 16)
        message[32 * peer : 32 * peer + 16, :] = upper[rows, :]
        message[32 * peer + 16 : 32 * peer + 32, :] = shuffled[rows, :].astype(BF16)


def legendre_kernel(waves, message, table, out, flat, sorted_rows, left, result, done):
    for band in range(16):
        total = message[4 * band].astype(F32)
        for z in range(1, 4):
            total = total + message[4 * band + z].astype(F32)
        flat[32 * band : 32 * band + 32, :] = total
    for row in range(BAND):
        for part in range(4):
            sorted_rows[pl.ds(128 * part + row, 16, stride=8), :] = flat[
                pl.ds(4 * row + part, 16, stride=32), :
            ]
    for part in range(4):
        rows = slice(128 * part, 128 * part + 128)
        left[rows, :] = sorted_rows[rows, :].T.astype(BF16)
    copies = []
    for slot in range(SLOTS):
        first = 256 * (slot % 2) + 48 * (slot // 2)
        product = jnp.dot(left[first : first + 48, :], table[slot], preferred_element_type=F32)
        wave = jnp.concatenate([waves[slot : slot + 1, :]] * (product.shape[1] // 128), axis=1)
        degree = lax.broadcasted_iota(jnp.int32, product.shape, 1).astype(F32)
        result[slot] = jnp.where(degree >= wave, product, 0.0)
        copy = pltpu.make_async_copy(result.at[slot], out.at[slot], done.at[slot])
        copy.start()
        copies.append(copy)
    for copy in copies:
        copy.wait()


def local(fields, row_length, wave_order, depart_row, depart_col, frac_row, frac_col, legendre):
    ring = lax.axis_size("wave")
    bands = lax.axis_size("lat")
    scalars = lax.optimization_barrier(jnp.concatenate([row_length, wave_order]))
    lengths = scalars[:BAND]
    limit = lengths - lax.axis_index("wave") * WIDE
    live_mask = jnp.arange(WIDE, dtype=jnp.int32)[None, :] < limit[:, None]
    masked = jnp.where(live_mask[None], fields, jnp.zeros_like(fields))
    own = masked.transpose(1, 0, 2).reshape(BAND * SLICES, WIDE)

    def swapped(first):
        pairs = [(i, i + 1) for i in range(first, bands - 1, 2)]
        return lax.ppermute(own, "lat", pairs + [(j, i) for i, j in pairs])

    over = swapped(1)
    under = swapped(0)

    own, depart_row = lax.optimization_barrier((own, depart_row))
    item = lax.broadcasted_iota(jnp.int32, (4, BAND, WIDE), 0)
    departs = jnp.where(item == 0, depart_row[None], depart_col[None]).astype(F32)
    fractions = jnp.where(item == 2, frac_row[None], frac_col[None])
    stencil = jnp.where(item < 2, departs, fractions)
    stencil, scalars = lax.optimization_barrier((stencil, scalars))
    ordered = scalars[BAND:].reshape(PEERS, 2 * SLOTS).T.astype(F32)
    from_left = lax.ppermute(
        stencil[:, :, WIDE - 128 :], "wave", [(i, (i + 1) % ring) for i in range(ring)]
    )
    from_right = lax.ppermute(
        stencil[:, :, :128], "wave", [((i + 1) % ring, i) for i in range(ring)]
    )
    length_table = jnp.broadcast_to(lengths.astype(F32)[:, None], (BAND, 128))
    inner, outer, columns, rows_of, own_waves = pl.pallas_call(
        table_kernel,
        out_shape=(
            jax.ShapeDtypeStruct((BAND, 256, GROUPS * 256), BF16),
            jax.ShapeDtypeStruct((BAND, 8, GROUPS * 256), F32),
            jax.ShapeDtypeStruct((BAND // 2, BLOCKS, 256, 256), BF16),
            jax.ShapeDtypeStruct((BAND // 2, BLOCKS, 24, 256), F32),
            jax.ShapeDtypeStruct((SLOTS, 128), F32),
        ),
        in_specs=[VMEM] * 3,
        out_specs=(VMEM,) * 5,
        scratch_shapes=[pltpu.VMEM((BAND, 16, WIDE), F32), pltpu.VMEM((BAND, 1, 128), F32)],
        compiler_params=pltpu.CompilerParams(vmem_limit_bytes=LIMIT),
        cost_estimate=pl.CostEstimate(flops=5_000_000_000, bytes_accessed=3_000_000, transcendentals=0),
        name="tables",
    )(length_table, ordered, stencil)
    wrap_columns, wrap_rows = pl.pallas_call(
        wrap_kernel,
        out_shape=(
            jax.ShapeDtypeStruct((BAND // 2, 128, 256), BF16),
            jax.ShapeDtypeStruct((BAND // 2, 24, 256), F32),
        ),
        in_specs=[VMEM] * 3,
        out_specs=(VMEM,) * 2,
        scratch_shapes=[pltpu.VMEM((BAND, 16, 128), F32)],
        compiler_params=pltpu.CompilerParams(vmem_limit_bytes=LIMIT),
        name="wrap_tables",
    )(length_table, from_left, from_right)

    weights = (columns, rows_of, wrap_columns, wrap_rows)
    part = jax.ShapeDtypeStruct((ROWS, STACK, 128), BF16)
    upper, main, edge = pl.pallas_call(
        upper_kernel,
        out_shape=(
            part,
            jax.ShapeDtypeStruct((COUNT, WIDE), BF16),
            jax.ShapeDtypeStruct((COUNT, WIDE + 128), BF16),
        ),
        in_specs=[VMEM] * 7,
        out_specs=(VMEM,) * 3,
        compiler_params=pltpu.CompilerParams(vmem_limit_bytes=LIMIT),
        name="interpolate_upper",
    )(own, under, over, *weights)
    cores = [(i, i ^ 1) for i in range(ring)]
    other_upper = lax.ppermute(upper, "wave", cores)
    lower = pl.pallas_call(
        lower_kernel,
        out_shape=part,
        in_specs=[VMEM] * 6,
        out_specs=VMEM,
        compiler_params=pltpu.CompilerParams(vmem_limit_bytes=LIMIT),
        cost_estimate=pl.CostEstimate(flops=5_000_000_000, bytes_accessed=3_000_000, transcendentals=0),
        name="interpolate_lower",
    )(main, edge, *weights)
    other_lower = lax.ppermute(lower, "wave", cores)
    scratch = [pltpu.VMEM((ROWS * 256, 128), F32), pltpu.VMEM((PEERS * 16, 128), F32)]
    message = pl.pallas_call(
        upper_fourier_kernel,
        out_shape=jax.ShapeDtypeStruct((PEERS * 16, 128), BF16),
        in_specs=[VMEM] * 4,
        out_specs=VMEM,
        scratch_shapes=scratch,
        compiler_params=pltpu.CompilerParams(vmem_limit_bytes=LIMIT),
        cost_estimate=pl.CostEstimate(flops=5_000_000_000, bytes_accessed=3_000_000, transcendentals=0),
        name="fourier_upper",
    )(upper, other_upper, inner, outer)
    message = pl.pallas_call(
        lower_fourier_kernel,
        out_shape=jax.ShapeDtypeStruct((PEERS * 32, 128), BF16),
        in_specs=[VMEM] * 5,
        out_specs=VMEM,
        scratch_shapes=scratch,
        compiler_params=pltpu.CompilerParams(vmem_limit_bytes=LIMIT),
        name="fourier_lower",
    )(lower, other_lower, inner, outer, message)
    message = lax.all_to_all(
        message.reshape(PEERS, 32, 128),
        ("lat", "wave"),
        split_axis=0,
        concat_axis=0,
        tiled=True,
        axis_index_groups=[[2 * peer + core for peer in range(PEERS)] for core in range(2)],
    )
    degrees = legendre.shape[2]
    return pl.pallas_call(
        legendre_kernel,
        out_shape=jax.ShapeDtypeStruct((SLOTS, 2 * SLICES, degrees), F32),
        in_specs=[VMEM] * 3,
        out_specs=pl.BlockSpec(memory_space=pl.ANY),
        scratch_shapes=[
            pltpu.VMEM((512, 128), F32),
            pltpu.VMEM((512, 128), F32),
            pltpu.VMEM((512, 128), BF16),
            pltpu.VMEM((SLOTS, 2 * SLICES, degrees), F32),
            pltpu.SemaphoreType.DMA((SLOTS,)),
        ],
        compiler_params=pltpu.CompilerParams(vmem_limit_bytes=LIMIT),
        name="legendre",
    )(own_waves, message, legendre)


def solution(mesh):
    placed = (
        P(None, "lat", "wave"),
        P("lat"),
        P(),
        P("lat", "wave"),
        P("lat", "wave"),
        P("lat", "wave"),
        P("lat", "wave"),
        P(("lat", "wave"), None, None),
    )
    return jax.shard_map(
        local, mesh=mesh, in_specs=placed, out_specs=P(("lat", "wave"), None, None), check_vma=False
    )
```

```python
import math

import jax
import jax.numpy as jnp
from jax import lax
from jax.experimental import pallas as pl
from jax.experimental.pallas import tpu as pltpu
from jax.sharding import PartitionSpec as P

F32 = jnp.float32
BF16 = jnp.bfloat16
VMEM = pl.BlockSpec(memory_space=pltpu.VMEM)
LIMIT = 24 * 1024 * 1024

SLICES = 24
BAND = 8
WIDE = 640
BLOCKS = 5
SLOTS = 10
PEERS = 64
GROUPS = 5
ROWS = 4
STACK = 144
COUNT = 3 * BAND * SLICES


def cubic_weights(fraction):
    return (
        -fraction * (fraction - 1.0) * (fraction - 2.0) / 6.0,
        (fraction + 1.0) * (fraction - 1.0) * (fraction - 2.0) / 2.0,
        -(fraction + 1.0) * fraction * (fraction - 2.0) / 2.0,
        (fraction + 1.0) * fraction * (fraction - 1.0) / 6.0,
    )


def picked_weight(distance, weights):
    chosen = jnp.where(distance == 3, weights[3], jnp.zeros_like(weights[3]))
    for step in (2, 1, 0):
        chosen = jnp.where(distance == step, weights[step], chosen)
    return chosen


def weighted(spread, rows_of, half):
    side = slice(128 * half, 128 * half + 128)
    total = jnp.zeros((SLICES, 128), F32)
    for row in range(half, half + 17):
        total = total + rows_of[row : row + 1, side] * spread[
            SLICES * row : SLICES * row + SLICES, side
        ]
    return total


def interpolate(steps, main, edge, columns, rows_of, wrap_columns, wrap_rows, out):
    for pair in steps:
        window = slice(pair * 2 * SLICES, pair * 2 * SLICES + 18 * SLICES)
        totals = ([], [])
        for block in range(BLOCKS + 1):
            lanes = slice(128 * block, 128 * block + 128)
            if block < BLOCKS:
                left = jnp.concatenate([main[window, lanes], edge[window, lanes]], axis=1)
                table, rows = columns[pair, block], rows_of.at[pair, block]
            else:
                left, table, rows = edge[window, lanes], wrap_columns[pair], wrap_rows.at[pair]
            spread = jnp.dot(left, table, preferred_element_type=F32)
            for half in range(2):
                totals[half].append(weighted(spread, rows, half))
        for half in range(2):
            out[(2 * pair + half) % ROWS] = jnp.concatenate(totals[half], axis=0).astype(BF16)


def upper_kernel(
    own, second, first, columns, rows_of, wrap_columns, wrap_rows, out, main, edge
):
    size = BAND * SLICES
    odd = lax.axis_index("lat") % 2
    main[pl.ds(pl.multiple_of(odd * 2 * size, size), size), :] = first[...]
    main[size : 2 * size, :] = own[...]
    main[pl.ds(pl.multiple_of((1 - odd) * 2 * size, size), size), :] = second[...]
    nothing = jnp.zeros((COUNT, 64), BF16)
    for block in range(BLOCKS):
        at = 128 * block
        sides = [
            main[:, at + 128 : at + 192] if block < BLOCKS - 1 else nothing,
            main[:, at - 64 : at] if block else nothing,
        ]
        edge[:, at : at + 128] = jnp.concatenate(sides, axis=1)
    edge[:, WIDE:] = jnp.concatenate([main[:, :64], main[:, WIDE - 64 :]], axis=1)
    interpolate((0, 1), main, edge, columns, rows_of, wrap_columns, wrap_rows, out)


def lower_kernel(main, edge, columns, rows_of, wrap_columns, wrap_rows, out):
    interpolate((2, 3), main, edge, columns, rows_of, wrap_columns, wrap_rows, out)


def turn(count, length, inverse):
    whole = jnp.floor(count * inverse + 0.5)
    angle = (count - whole * length) * (inverse * math.pi)
    square = angle * angle
    sine = angle * (
        1.0
        + square
        * (
            -1.0 / 6
            + square
            * (1.0 / 120 + square * (-1.0 / 5040 + square * (1.0 / 362880 - square / 39916800)))
        )
    )
    cosine = 1.0 + square * (
        -0.5
        + square
        * (
            1.0 / 24
            + square
            * (-1.0 / 720 + square * (1.0 / 40320 + square * (-1.0 / 3628800 + square / 479001600)))
        )
    )
    return 1.0 - 2.0 * sine * sine, 2.0 * sine * cosine


def rotated(one, two):
    return one[0] * two[0] - one[1] * two[1], one[1] * two[0] + one[0] * two[1]


def ring_start(place):
    return lax.rem(place + 8, 8) * WIDE


def spread_points(target, lengths, values, width, position):
    lane = (lax.broadcasted_iota(jnp.int32, (1, width), 1) % 128).astype(F32)
    limit = jnp.concatenate([lengths[...]] * (width // 128), axis=1)
    live = position.astype(F32) < limit
    for base, first, fraction in (
        (0, values[1] + (lane - 1.0), values[3]),
        (8, values[0] + (BAND - 1.0), values[2]),
    ):
        for k, value in enumerate((first,) + cubic_weights(fraction)):
            if base and k:
                value = jnp.where(live, value, 0.0)
            for row in range(BAND):
                target[row, base + k : base + k + 1, :] = value[row : row + 1, :]


def row_of(ref, pair, item, block):
    return jnp.concatenate(
        [
            ref[2 * pair + half, item : item + 1, 128 * block : 128 * block + 128]
            for half in range(2)
        ],
        axis=1,
    )


def picks(ref, pair, block):
    start = row_of(ref, pair, 0, block).astype(BF16)
    weights = [row_of(ref, pair, 1 + k, block).astype(BF16) for k in range(4)]

    def pick(count, first):
        source = lax.broadcasted_iota(jnp.int32, (count, 256), 0) + first
        return picked_weight(source.astype(F32).astype(BF16) - start, weights)

    return pick


def row_table(ref, pair, block):
    half = (lax.broadcasted_iota(jnp.int32, (1, 256), 1) >= 128).astype(F32)
    start = row_of(ref, pair, 8, block) + half
    weights = [row_of(ref, pair, 9 + k, block) for k in range(4)]
    source = lax.broadcasted_iota(jnp.int32, (24, 256), 0).astype(F32)
    return picked_weight(source - start, weights)


def table_kernel(
    lengths, waves, stencil, inner, outer, columns, rows_of, own_waves, points, length_rows
):
    wave_place = lax.axis_index("wave")
    core = wave_place % 2
    peer = lax.axis_index("lat") * 4 + wave_place // 2
    slots = jnp.where(core == 0, waves[:SLOTS, :], waves[SLOTS:, :])
    lane = lax.broadcasted_iota(jnp.int32, (SLOTS, PEERS), 1)
    mine = jnp.sum(jnp.where(lane == peer, slots, 0.0), axis=1, keepdims=True)
    own_waves[...] = jnp.broadcast_to(mine, (SLOTS, 128))
    groups = [
        jnp.concatenate([slots[k : k + 1], slots[k + 1 : k + 2]], axis=1)
        for k in range(0, SLOTS, 2)
    ]
    for row in range(BAND):
        length_rows[row] = lengths[row : row + 1, :]
    step = lax.broadcasted_iota(jnp.int32, (8, 128), 0)
    other_place = wave_place ^ 1
    away = (other_place - wave_place) * WIDE
    before = ring_start(wave_place - 1) + (WIDE - 128)
    behind = ring_start(wave_place + 1)
    other_before = ring_start(other_place - 1) + (WIDE - 128)
    other_behind = ring_start(other_place + 1)
    outside = jnp.where(core == 0, before, behind)
    other_outside = jnp.where(core == 0, other_behind, other_before) - away
    shift = 128 * step + wave_place * WIDE
    for at, value in ((5, outside), (6, other_outside), (7, away)):
        shift = jnp.where(step == at, value, shift)
    shift = shift.astype(F32)
    fine = step.astype(F32)
    coarse = 16.0 * fine

    def one(row, carry):
        length = length_rows[row]
        inverse = 1.0 / length
        norm = lax.rsqrt(length)
        for group, wave in enumerate(groups):
            lanes = slice(group * 256, group * 256 + 128)
            lanes_two = slice(group * 256 + 128, group * 256 + 256)
            moved = turn(shift * wave, length, inverse)
            outer[row, :, lanes] = moved[0] * norm
            outer[row, :, lanes_two] = moved[1] * norm
            other = [part[7:8] for part in moved]
            near = turn(fine * wave, length, inverse)
            eight = rotated([part[7:8] for part in near], [part[1:2] for part in near])
            small = [
                jnp.concatenate(parts, axis=0).astype(BF16)
                for parts in zip(near, rotated(eight, near))
            ]
            low = turn(coarse * wave, length, inverse)
            for tile in range(2):
                if tile:
                    low = rotated(low, other)
                for k in range(8):
                    start = [
                        jnp.broadcast_to(part[k : k + 1], (16, 128)).astype(BF16) for part in low
                    ]
                    rows = slice(128 * tile + 16 * k, 128 * tile + 16 * k + 16)
                    inner[row, rows, lanes], inner[row, rows, lanes_two] = rotated(start, small)
        return carry

    lax.fori_loop(0, BAND, one, 0)

    column = lax.broadcasted_iota(jnp.int32, (BAND, WIDE), 1)
    values = [stencil[k] for k in range(4)]
    spread_points(points, lengths, values, WIDE, column + wave_place * WIDE)

    def one_pair(pair, carry):
        for block in range(BLOCKS):
            pick = picks(points, pair, block)
            columns[pair, block, 0:144, :] = pick(144, 0)
            columns[pair, block, 144:240, :] = jnp.zeros((96, 256), BF16)
            columns[pair, block, 240:256, :] = pick(16, -16)
            rows_of[pair, block] = row_table(points, pair, block)
        return carry

    lax.fori_loop(0, BAND // 2, one_pair, 0)


def wrap_kernel(lengths, from_left, from_right, wrap_columns, wrap_rows, points):
    wave_place = lax.axis_index("wave")
    before = ring_start(wave_place - 1) + (WIDE - 128)
    behind = ring_start(wave_place + 1)
    column = lax.broadcasted_iota(jnp.int32, (BAND, 128), 1)
    values = [jnp.where(column < 64, from_right[k], from_left[k]) for k in range(4)]
    position = column + jnp.where(column < 64, behind, before)
    spread_points(points, lengths, values, 128, position)
    for pair in range(BAND // 2):
        pick = picks(points, pair, 0)
        wrap_columns[pair, 0:16, :] = pick(16, 128)
        wrap_columns[pair, 16:112, :] = jnp.zeros((96, 256), BF16)
        wrap_columns[pair, 112:128, :] = pick(16, -16)
        wrap_rows[pair] = row_table(points, pair, 0)


def fourier(first, mine, other, inner, outer, sums, shuffled):
    odd = jnp.full((SLICES, 128), lax.axis_index("wave") % 2, jnp.int32).astype(F32)
    low = (lax.broadcasted_iota(jnp.int32, (SLICES, 128), 1) < 64).astype(F32)
    to_mine = (low * odd, (1.0 - low) * (1.0 - odd))
    to_other = (low * (1.0 - odd), (1.0 - low) * odd)
    last = SLICES * (BLOCKS - 1)
    nothing = jnp.zeros((SLICES, 128), F32)

    for row in range(ROWS):
        own = mine[row].astype(F32)
        far = other[row].astype(F32)
        own_wrap, far_wrap = own[last + SLICES :], far[last + SLICES :]
        halves = [
            [
                own[:SLICES] + far_wrap * to_mine[0],
                own[SLICES:last],
                own[last : last + SLICES] + far_wrap * to_mine[1],
                own_wrap * (to_mine[0] + to_mine[1]),
                nothing,
                nothing[:8],
            ],
            [
                far[:SLICES] + own_wrap * to_other[0],
                far[SLICES:last],
                far[last : last + SLICES] + own_wrap * to_other[1],
                nothing,
                far_wrap * (to_other[0] + to_other[1]),
                nothing[:8],
            ],
        ]
        left = jnp.concatenate([jnp.concatenate(half, axis=0) for half in halves], axis=1)
        left = left.astype(BF16)
        base = 256 * row
        sums[base + 240 : base + 256, :] = jnp.zeros((16, 128), F32)
        for group in range(GROUPS):
            lanes = slice(256 * group, 256 * group + 256)
            parts = jnp.dot(left, inner[first + row, :, lanes], preferred_element_type=F32)
            real = jnp.zeros((SLICES, 128), F32)
            imag = jnp.zeros((SLICES, 128), F32)
            for block in range(BLOCKS + 2):
                rows = slice(SLICES * block, SLICES * block + SLICES)
                cosine, sine = parts[rows, :128], parts[rows, 128:]
                factor = outer[first + row, block : block + 1, lanes]
                c, s = factor[:, :128], factor[:, 128:]
                real = real + (c * cosine - s * sine)
                imag = imag - (s * cosine + c * sine)
            sums[pl.ds(base + group * 48, SLICES, stride=2), :] = real
            sums[pl.ds(base + group * 48 + 1, SLICES, stride=2), :] = imag
        for half in range(2):
            turned = sums[base + 128 * half : base + 128 * half + 128, :].T
            for side in range(2):
                at = 4 * row + 2 * side + half
                shuffled[pl.ds(at, PEERS, stride=16), :] = turned[PEERS * side : PEERS * side + PEERS]


def upper_fourier_kernel(mine, other, inner, outer, message, sums, shuffled):
    fourier(0, mine, other, inner, outer, sums, shuffled)
    message[...] = shuffled[...].astype(BF16)


def lower_fourier_kernel(mine, other, inner, outer, upper, message, sums, shuffled):
    fourier(ROWS, mine, other, inner, outer, sums, shuffled)
    for peer in range(PEERS):
        rows = slice(16 * peer, 16 * peer + 16)
        message[32 * peer : 32 * peer + 16, :] = upper[rows, :]
        message[32 * peer + 16 : 32 * peer + 32, :] = shuffled[rows, :].astype(BF16)


def legendre_kernel(waves, message, table, out, flat, sorted_rows, left, result, done):
    for band in range(16):
        total = message[4 * band].astype(F32)
        for z in range(1, 4):
            total = total + message[4 * band + z].astype(F32)
        flat[32 * band : 32 * band + 32, :] = total
    copies = []
    for part in range(4):
        for row in range(BAND):
            sorted_rows[pl.ds(128 * part + row, 16, stride=8), :] = flat[
                pl.ds(4 * row + part, 16, stride=32), :
            ]
        rows = slice(128 * part, 128 * part + 128)
        left[rows, :] = sorted_rows[rows, :].T.astype(BF16)
        for group in ((2, 3, 4) if part % 2 else (0, 1)):
            slot = 2 * group + part // 2
            first = 256 * (part // 2) + 48 * group
            product = jnp.dot(left[first : first + 48, :], table[slot], preferred_element_type=F32)
            wave = jnp.concatenate([waves[slot : slot + 1, :]] * (product.shape[1] // 128), axis=1)
            degree = lax.broadcasted_iota(jnp.int32, product.shape, 1).astype(F32)
            result[slot] = jnp.where(degree >= wave, product, 0.0)
            copy = pltpu.make_async_copy(result.at[slot], out.at[slot], done.at[slot])
            copy.start()
            copies.append(copy)
    for copy in copies:
        copy.wait()


def local(fields, row_length, wave_order, depart_row, depart_col, frac_row, frac_col, legendre):
    ring = lax.axis_size("wave")
    bands = lax.axis_size("lat")
    scalars = lax.optimization_barrier(jnp.concatenate([row_length, wave_order]))
    lengths = scalars[:BAND]
    limit = lengths - lax.axis_index("wave") * WIDE
    live_mask = jnp.arange(WIDE, dtype=jnp.int32)[None, :] < limit[:, None]
    masked = jnp.where(live_mask[None], fields, jnp.zeros_like(fields))
    own = masked.transpose(1, 0, 2).reshape(BAND * SLICES, WIDE)

    def swapped(first):
        pairs = [(i, i + 1) for i in range(first, bands - 1, 2)]
        return lax.ppermute(own, "lat", pairs + [(j, i) for i, j in pairs])

    over = swapped(1)
    under = swapped(0)

    own, depart_row = lax.optimization_barrier((own, depart_row))
    item = lax.broadcasted_iota(jnp.int32, (4, BAND, WIDE), 0)
    departs = jnp.where(item == 0, depart_row[None], depart_col[None]).astype(F32)
    fractions = jnp.where(item == 2, frac_row[None], frac_col[None])
    stencil = jnp.where(item < 2, departs, fractions)
    stencil, scalars = lax.optimization_barrier((stencil, scalars))
    ordered = scalars[BAND:].reshape(PEERS, 2 * SLOTS).T.astype(F32)
    from_left = lax.ppermute(
        stencil[:, :, WIDE - 128 :], "wave", [(i, (i + 1) % ring) for i in range(ring)]
    )
    from_right = lax.ppermute(
        stencil[:, :, :128], "wave", [((i + 1) % ring, i) for i in range(ring)]
    )
    length_table = jnp.broadcast_to(lengths.astype(F32)[:, None], (BAND, 128))
    inner, outer, columns, rows_of, own_waves = pl.pallas_call(
        table_kernel,
        out_shape=(
            jax.ShapeDtypeStruct((BAND, 256, GROUPS * 256), BF16),
            jax.ShapeDtypeStruct((BAND, 8, GROUPS * 256), F32),
            jax.ShapeDtypeStruct((BAND // 2, BLOCKS, 256, 256), BF16),
            jax.ShapeDtypeStruct((BAND // 2, BLOCKS, 24, 256), F32),
            jax.ShapeDtypeStruct((SLOTS, 128), F32),
        ),
        in_specs=[VMEM] * 3,
        out_specs=(VMEM,) * 5,
        scratch_shapes=[pltpu.VMEM((BAND, 16, WIDE), F32), pltpu.VMEM((BAND, 1, 128), F32)],
        compiler_params=pltpu.CompilerParams(vmem_limit_bytes=LIMIT),
        cost_estimate=pl.CostEstimate(flops=5_000_000_000, bytes_accessed=3_000_000, transcendentals=0),
        name="tables",
    )(length_table, ordered, stencil)
    wrap_columns, wrap_rows = pl.pallas_call(
        wrap_kernel,
        out_shape=(
            jax.ShapeDtypeStruct((BAND // 2, 128, 256), BF16),
            jax.ShapeDtypeStruct((BAND // 2, 24, 256), F32),
        ),
        in_specs=[VMEM] * 3,
        out_specs=(VMEM,) * 2,
        scratch_shapes=[pltpu.VMEM((BAND, 16, 128), F32)],
        compiler_params=pltpu.CompilerParams(vmem_limit_bytes=LIMIT),
        name="wrap_tables",
    )(length_table, from_left, from_right)

    weights = (columns, rows_of, wrap_columns, wrap_rows)
    part = jax.ShapeDtypeStruct((ROWS, STACK, 128), BF16)
    upper, main, edge = pl.pallas_call(
        upper_kernel,
        out_shape=(
            part,
            jax.ShapeDtypeStruct((COUNT, WIDE), BF16),
            jax.ShapeDtypeStruct((COUNT, WIDE + 128), BF16),
        ),
        in_specs=[VMEM] * 7,
        out_specs=(VMEM,) * 3,
        compiler_params=pltpu.CompilerParams(vmem_limit_bytes=LIMIT),
        name="interpolate_upper",
    )(own, under, over, *weights)
    cores = [(i, i ^ 1) for i in range(ring)]
    other_upper = lax.ppermute(upper, "wave", cores)
    lower = pl.pallas_call(
        lower_kernel,
        out_shape=part,
        in_specs=[VMEM] * 6,
        out_specs=VMEM,
        compiler_params=pltpu.CompilerParams(vmem_limit_bytes=LIMIT),
        cost_estimate=pl.CostEstimate(flops=5_000_000_000, bytes_accessed=3_000_000, transcendentals=0),
        name="interpolate_lower",
    )(main, edge, *weights)
    other_lower = lax.ppermute(lower, "wave", cores)
    scratch = [pltpu.VMEM((ROWS * 256, 128), F32), pltpu.VMEM((PEERS * 16, 128), F32)]
    message = pl.pallas_call(
        upper_fourier_kernel,
        out_shape=jax.ShapeDtypeStruct((PEERS * 16, 128), BF16),
        in_specs=[VMEM] * 4,
        out_specs=VMEM,
        scratch_shapes=scratch,
        compiler_params=pltpu.CompilerParams(vmem_limit_bytes=LIMIT),
        cost_estimate=pl.CostEstimate(flops=5_000_000_000, bytes_accessed=3_000_000, transcendentals=0),
        name="fourier_upper",
    )(upper, other_upper, inner, outer)
    message = pl.pallas_call(
        lower_fourier_kernel,
        out_shape=jax.ShapeDtypeStruct((PEERS * 32, 128), BF16),
        in_specs=[VMEM] * 5,
        out_specs=VMEM,
        scratch_shapes=scratch,
        compiler_params=pltpu.CompilerParams(vmem_limit_bytes=LIMIT),
        name="fourier_lower",
    )(lower, other_lower, inner, outer, message)
    message = lax.all_to_all(
        message.reshape(PEERS, 32, 128),
        ("lat", "wave"),
        split_axis=0,
        concat_axis=0,
        tiled=True,
        axis_index_groups=[[2 * peer + core for peer in range(PEERS)] for core in range(2)],
    )
    degrees = legendre.shape[2]
    return pl.pallas_call(
        legendre_kernel,
        out_shape=jax.ShapeDtypeStruct((SLOTS, 2 * SLICES, degrees), F32),
        in_specs=[VMEM] * 3,
        out_specs=pl.BlockSpec(memory_space=pl.ANY),
        scratch_shapes=[
            pltpu.VMEM((512, 128), F32),
            pltpu.VMEM((512, 128), F32),
            pltpu.VMEM((512, 128), BF16),
            pltpu.VMEM((SLOTS, 2 * SLICES, degrees), F32),
            pltpu.SemaphoreType.DMA((SLOTS,)),
        ],
        compiler_params=pltpu.CompilerParams(vmem_limit_bytes=LIMIT),
        name="legendre",
    )(own_waves, message, legendre)


def solution(mesh):
    placed = (
        P(None, "lat", "wave"),
        P("lat"),
        P(),
        P("lat", "wave"),
        P("lat", "wave"),
        P("lat", "wave"),
        P("lat", "wave"),
        P(("lat", "wave"), None, None),
    )
    return jax.shard_map(
        local, mesh=mesh, in_specs=placed, out_specs=P(("lat", "wave"), None, None), check_vma=False
    )
```

```python
import math

import jax
import jax.numpy as jnp
import numpy as np
from jax import lax
from jax.experimental import pallas as pl
from jax.experimental.pallas import tpu as pltpu
from jax.sharding import PartitionSpec as P

F32 = jnp.float32
BF16 = jnp.bfloat16
VMEM = pl.BlockSpec(memory_space=pltpu.VMEM)
LIMIT = 24 * 1024 * 1024

SLICES = 24
BAND = 8
WIDE = 640
BLOCKS = 5
SLOTS = 10
PEERS = 64
ORDER = [int(peer) for peer in np.random.RandomState(0).permutation(PEERS)]
STANDS = [ORDER.index(peer) for peer in range(PEERS)]
GROUPS = 5
ROWS = 4
STACK = 144
COUNT = 3 * BAND * SLICES


def cubic_weights(fraction):
    return (
        -fraction * (fraction - 1.0) * (fraction - 2.0) / 6.0,
        (fraction + 1.0) * (fraction - 1.0) * (fraction - 2.0) / 2.0,
        -(fraction + 1.0) * fraction * (fraction - 2.0) / 2.0,
        (fraction + 1.0) * fraction * (fraction - 1.0) / 6.0,
    )


def picked_weight(distance, weights):
    chosen = jnp.where(distance == 3, weights[3], jnp.zeros_like(weights[3]))
    for step in (2, 1, 0):
        chosen = jnp.where(distance == step, weights[step], chosen)
    return chosen


def weighted(spread, rows_of, half):
    side = slice(128 * half, 128 * half + 128)
    total = jnp.zeros((SLICES, 128), F32)
    for row in range(half, half + 17):
        total = total + rows_of[row : row + 1, side] * spread[
            SLICES * row : SLICES * row + SLICES, side
        ]
    return total


def interpolate(steps, main, edge, columns, rows_of, wrap_columns, wrap_rows, out):
    for pair in steps:
        window = slice(pair * 2 * SLICES, pair * 2 * SLICES + 18 * SLICES)
        totals = ([], [])
        for block in range(BLOCKS + 1):
            lanes = slice(128 * block, 128 * block + 128)
            if block < BLOCKS:
                left = jnp.concatenate([main[window, lanes], edge[window, lanes]], axis=1)
                table, rows = columns[pair, block], rows_of.at[pair, block]
            else:
                left, table, rows = edge[window, lanes], wrap_columns[pair], wrap_rows.at[pair]
            spread = jnp.dot(left, table, preferred_element_type=F32)
            for half in range(2):
                totals[half].append(weighted(spread, rows, half))
        for half in range(2):
            out[(2 * pair + half) % ROWS] = jnp.concatenate(totals[half], axis=0).astype(BF16)


def upper_kernel(
    own, second, first, columns, rows_of, wrap_columns, wrap_rows, out, main, edge
):
    size = BAND * SLICES
    odd = lax.axis_index("lat") % 2
    main[pl.ds(pl.multiple_of(odd * 2 * size, size), size), :] = first[...]
    main[size : 2 * size, :] = own[...]
    main[pl.ds(pl.multiple_of((1 - odd) * 2 * size, size), size), :] = second[...]
    nothing = jnp.zeros((COUNT, 64), BF16)
    for block in range(BLOCKS):
        at = 128 * block
        sides = [
            main[:, at + 128 : at + 192] if block < BLOCKS - 1 else nothing,
            main[:, at - 64 : at] if block else nothing,
        ]
        edge[:, at : at + 128] = jnp.concatenate(sides, axis=1)
    edge[:, WIDE:] = jnp.concatenate([main[:, :64], main[:, WIDE - 64 :]], axis=1)
    interpolate((0, 1), main, edge, columns, rows_of, wrap_columns, wrap_rows, out)


def lower_kernel(main, edge, columns, rows_of, wrap_columns, wrap_rows, out):
    interpolate((2, 3), main, edge, columns, rows_of, wrap_columns, wrap_rows, out)


def turn(count, length, inverse):
    whole = jnp.floor(count * inverse + 0.5)
    angle = (count - whole * length) * (inverse * math.pi)
    square = angle * angle
    sine = angle * (
        1.0
        + square
        * (
            -1.0 / 6
            + square
            * (1.0 / 120 + square * (-1.0 / 5040 + square * (1.0 / 362880 - square / 39916800)))
        )
    )
    cosine = 1.0 + square * (
        -0.5
        + square
        * (
            1.0 / 24
            + square
            * (-1.0 / 720 + square * (1.0 / 40320 + square * (-1.0 / 3628800 + square / 479001600)))
        )
    )
    return 1.0 - 2.0 * sine * sine, 2.0 * sine * cosine


def rotated(one, two):
    return one[0] * two[0] - one[1] * two[1], one[1] * two[0] + one[0] * two[1]


def ring_start(place):
    return lax.rem(place + 8, 8) * WIDE


def spread_points(target, lengths, values, width, position):
    lane = (lax.broadcasted_iota(jnp.int32, (1, width), 1) % 128).astype(F32)
    limit = jnp.concatenate([lengths[...]] * (width // 128), axis=1)
    live = position.astype(F32) < limit
    for base, first, fraction in (
        (0, values[1] + (lane - 1.0), values[3]),
        (8, values[0] + (BAND - 1.0), values[2]),
    ):
        for k, value in enumerate((first,) + cubic_weights(fraction)):
            if base and k:
                value = jnp.where(live, value, 0.0)
            for row in range(BAND):
                target[row, base + k : base + k + 1, :] = value[row : row + 1, :]


def row_of(ref, pair, item, block):
    return jnp.concatenate(
        [
            ref[2 * pair + half, item : item + 1, 128 * block : 128 * block + 128]
            for half in range(2)
        ],
        axis=1,
    )


def picks(ref, pair, block):
    start = row_of(ref, pair, 0, block).astype(BF16)
    weights = [row_of(ref, pair, 1 + k, block).astype(BF16) for k in range(4)]

    def pick(count, first):
        source = lax.broadcasted_iota(jnp.int32, (count, 256), 0) + first
        return picked_weight(source.astype(F32).astype(BF16) - start, weights)

    return pick


def row_table(ref, pair, block):
    half = (lax.broadcasted_iota(jnp.int32, (1, 256), 1) >= 128).astype(F32)
    start = row_of(ref, pair, 8, block) + half
    weights = [row_of(ref, pair, 9 + k, block) for k in range(4)]
    source = lax.broadcasted_iota(jnp.int32, (24, 256), 0).astype(F32)
    return picked_weight(source - start, weights)


def table_kernel(
    lengths, waves, stencil, inner, outer, columns, rows_of, own_waves, points, length_rows
):
    wave_place = lax.axis_index("wave")
    core = wave_place % 2
    peer = lax.axis_index("lat") * 4 + wave_place // 2
    slots = jnp.where(core == 0, waves[:SLOTS, :], waves[SLOTS:, :])
    lane = lax.broadcasted_iota(jnp.int32, (SLOTS, PEERS), 1)
    mine = jnp.sum(jnp.where(lane == peer, slots, 0.0), axis=1, keepdims=True)
    own_waves[...] = jnp.broadcast_to(mine, (SLOTS, 128))
    column = lax.broadcasted_iota(jnp.int32, (1, PEERS), 1)
    order = jnp.zeros((1, PEERS), jnp.int32)
    for at, peer in enumerate(ORDER):
        order = jnp.where(column == at, peer, order)
    chosen = (lax.broadcasted_iota(jnp.int32, (PEERS, PEERS), 0) == order).astype(F32).astype(BF16)
    high = jnp.floor(slots * 0.125)
    slots = 8.0 * jnp.dot(high.astype(BF16), chosen, preferred_element_type=F32) + jnp.dot(
        (slots - 8.0 * high).astype(BF16), chosen, preferred_element_type=F32
    )
    groups = [
        jnp.concatenate([slots[k : k + 1], slots[k + 1 : k + 2]], axis=1)
        for k in range(0, SLOTS, 2)
    ]
    for row in range(BAND):
        length_rows[row] = lengths[row : row + 1, :]
    step = lax.broadcasted_iota(jnp.int32, (8, 128), 0)
    other_place = wave_place ^ 1
    away = (other_place - wave_place) * WIDE
    before = ring_start(wave_place - 1) + (WIDE - 128)
    behind = ring_start(wave_place + 1)
    other_before = ring_start(other_place - 1) + (WIDE - 128)
    other_behind = ring_start(other_place + 1)
    outside = jnp.where(core == 0, before, behind)
    other_outside = jnp.where(core == 0, other_behind, other_before) - away
    shift = 128 * step + wave_place * WIDE
    for at, value in ((5, outside), (6, other_outside), (7, away)):
        shift = jnp.where(step == at, value, shift)
    shift = shift.astype(F32)
    fine = step.astype(F32)
    coarse = 16.0 * fine

    def one(row, carry):
        length = length_rows[row]
        inverse = 1.0 / length
        norm = lax.rsqrt(length)
        for group, wave in enumerate(groups):
            lanes = slice(group * 256, group * 256 + 128)
            lanes_two = slice(group * 256 + 128, group * 256 + 256)
            moved = turn(shift * wave, length, inverse)
            outer[row, :, lanes] = moved[0] * norm
            outer[row, :, lanes_two] = moved[1] * norm
            other = [part[7:8] for part in moved]
            near = turn(fine * wave, length, inverse)
            eight = rotated([part[7:8] for part in near], [part[1:2] for part in near])
            small = [
                jnp.concatenate(parts, axis=0).astype(BF16)
                for parts in zip(near, rotated(eight, near))
            ]
            low = turn(coarse * wave, length, inverse)
            for tile in range(2):
                if tile:
                    low = rotated(low, other)
                for k in range(8):
                    start = [
                        jnp.broadcast_to(part[k : k + 1], (16, 128)).astype(BF16) for part in low
                    ]
                    rows = slice(128 * tile + 16 * k, 128 * tile + 16 * k + 16)
                    inner[row, rows, lanes], inner[row, rows, lanes_two] = rotated(start, small)
        return carry

    lax.fori_loop(0, BAND, one, 0)

    column = lax.broadcasted_iota(jnp.int32, (BAND, WIDE), 1)
    values = [stencil[k] for k in range(4)]
    spread_points(points, lengths, values, WIDE, column + wave_place * WIDE)

    def one_pair(pair, carry):
        for block in range(BLOCKS):
            pick = picks(points, pair, block)
            columns[pair, block, 0:144, :] = pick(144, 0)
            columns[pair, block, 144:240, :] = jnp.zeros((96, 256), BF16)
            columns[pair, block, 240:256, :] = pick(16, -16)
            rows_of[pair, block] = row_table(points, pair, block)
        return carry

    lax.fori_loop(0, BAND // 2, one_pair, 0)


def wrap_kernel(lengths, from_left, from_right, wrap_columns, wrap_rows, points):
    wave_place = lax.axis_index("wave")
    before = ring_start(wave_place - 1) + (WIDE - 128)
    behind = ring_start(wave_place + 1)
    column = lax.broadcasted_iota(jnp.int32, (BAND, 128), 1)
    values = [jnp.where(column < 64, from_right[k], from_left[k]) for k in range(4)]
    position = column + jnp.where(column < 64, behind, before)
    spread_points(points, lengths, values, 128, position)
    for pair in range(BAND // 2):
        pick = picks(points, pair, 0)
        wrap_columns[pair, 0:16, :] = pick(16, 128)
        wrap_columns[pair, 16:112, :] = jnp.zeros((96, 256), BF16)
        wrap_columns[pair, 112:128, :] = pick(16, -16)
        wrap_rows[pair] = row_table(points, pair, 0)


def fourier(first, mine, other, inner, outer, sums, shuffled):
    odd = jnp.full((SLICES, 128), lax.axis_index("wave") % 2, jnp.int32).astype(F32)
    low = (lax.broadcasted_iota(jnp.int32, (SLICES, 128), 1) < 64).astype(F32)
    to_mine = (low * odd, (1.0 - low) * (1.0 - odd))
    to_other = (low * (1.0 - odd), (1.0 - low) * odd)
    last = SLICES * (BLOCKS - 1)
    nothing = jnp.zeros((SLICES, 128), F32)

    for row in range(ROWS):
        own = mine[row].astype(F32)
        far = other[row].astype(F32)
        own_wrap, far_wrap = own[last + SLICES :], far[last + SLICES :]
        halves = [
            [
                own[:SLICES] + far_wrap * to_mine[0],
                own[SLICES:last],
                own[last : last + SLICES] + far_wrap * to_mine[1],
                own_wrap * (to_mine[0] + to_mine[1]),
                nothing,
                nothing[:8],
            ],
            [
                far[:SLICES] + own_wrap * to_other[0],
                far[SLICES:last],
                far[last : last + SLICES] + own_wrap * to_other[1],
                nothing,
                far_wrap * (to_other[0] + to_other[1]),
                nothing[:8],
            ],
        ]
        left = jnp.concatenate([jnp.concatenate(half, axis=0) for half in halves], axis=1)
        left = left.astype(BF16)
        base = 256 * row
        sums[base + 240 : base + 256, :] = jnp.zeros((16, 128), F32)
        for group in range(GROUPS):
            lanes = slice(256 * group, 256 * group + 256)
            parts = jnp.dot(left, inner[first + row, :, lanes], preferred_element_type=F32)
            real = jnp.zeros((SLICES, 128), F32)
            imag = jnp.zeros((SLICES, 128), F32)
            for block in range(BLOCKS + 2):
                rows = slice(SLICES * block, SLICES * block + SLICES)
                cosine, sine = parts[rows, :128], parts[rows, 128:]
                factor = outer[first + row, block : block + 1, lanes]
                c, s = factor[:, :128], factor[:, 128:]
                real = real + (c * cosine - s * sine)
                imag = imag - (s * cosine + c * sine)
            sums[pl.ds(base + group * 48, SLICES, stride=2), :] = real
            sums[pl.ds(base + group * 48 + 1, SLICES, stride=2), :] = imag
        for half in range(2):
            turned = sums[base + 128 * half : base + 128 * half + 128, :].T
            for side in range(2):
                at = 4 * row + 2 * side + half
                shuffled[pl.ds(at, PEERS, stride=16), :] = turned[PEERS * side : PEERS * side + PEERS]


def upper_fourier_kernel(mine, other, inner, outer, message, sums, shuffled):
    fourier(0, mine, other, inner, outer, sums, shuffled)
    message[...] = shuffled[...].astype(BF16)


def lower_fourier_kernel(mine, other, inner, outer, upper, message, sums, shuffled):
    fourier(ROWS, mine, other, inner, outer, sums, shuffled)
    for peer in range(PEERS):
        rows = slice(16 * peer, 16 * peer + 16)
        message[32 * peer : 32 * peer + 16, :] = upper[rows, :]
        message[32 * peer + 16 : 32 * peer + 32, :] = shuffled[rows, :].astype(BF16)


def legendre_kernel(waves, message, table, out, flat, sorted_rows, left, result, done):
    for band in range(16):
        total = message[STANDS[4 * band]].astype(F32)
        for z in range(1, 4):
            total = total + message[STANDS[4 * band + z]].astype(F32)
        flat[32 * band : 32 * band + 32, :] = total
    copies = []
    for part in range(4):
        for row in range(BAND):
            sorted_rows[pl.ds(128 * part + row, 16, stride=8), :] = flat[
                pl.ds(4 * row + part, 16, stride=32), :
            ]
        rows = slice(128 * part, 128 * part + 128)
        left[rows, :] = sorted_rows[rows, :].T.astype(BF16)
        for group in ((2, 3, 4) if part % 2 else (0, 1)):
            slot = 2 * group + part // 2
            first = 256 * (part // 2) + 48 * group
            product = jnp.dot(left[first : first + 48, :], table[slot], preferred_element_type=F32)
            wave = jnp.concatenate([waves[slot : slot + 1, :]] * (product.shape[1] // 128), axis=1)
            degree = lax.broadcasted_iota(jnp.int32, product.shape, 1).astype(F32)
            result[slot] = jnp.where(degree >= wave, product, 0.0)
            copy = pltpu.make_async_copy(result.at[slot], out.at[slot], done.at[slot])
            copy.start()
            copies.append(copy)
    for copy in copies:
        copy.wait()


def local(fields, row_length, wave_order, depart_row, depart_col, frac_row, frac_col, legendre):
    ring = lax.axis_size("wave")
    bands = lax.axis_size("lat")
    scalars = lax.optimization_barrier(jnp.concatenate([row_length, wave_order]))
    lengths = scalars[:BAND]
    limit = lengths - lax.axis_index("wave") * WIDE
    live_mask = jnp.arange(WIDE, dtype=jnp.int32)[None, :] < limit[:, None]
    masked = jnp.where(live_mask[None], fields, jnp.zeros_like(fields))
    own = masked.transpose(1, 0, 2).reshape(BAND * SLICES, WIDE)

    def swapped(first):
        pairs = [(i, i + 1) for i in range(first, bands - 1, 2)]
        return lax.ppermute(own, "lat", pairs + [(j, i) for i, j in pairs])

    over = swapped(1)
    under = swapped(0)

    own, depart_row = lax.optimization_barrier((own, depart_row))
    item = lax.broadcasted_iota(jnp.int32, (4, BAND, WIDE), 0)
    departs = jnp.where(item == 0, depart_row[None], depart_col[None]).astype(F32)
    fractions = jnp.where(item == 2, frac_row[None], frac_col[None])
    stencil = jnp.where(item < 2, departs, fractions)
    stencil, scalars = lax.optimization_barrier((stencil, scalars))
    ordered = scalars[BAND:].reshape(PEERS, 2 * SLOTS).T.astype(F32)
    from_left = lax.ppermute(
        stencil[:, :, WIDE - 128 :], "wave", [(i, (i + 1) % ring) for i in range(ring)]
    )
    from_right = lax.ppermute(
        stencil[:, :, :128], "wave", [((i + 1) % ring, i) for i in range(ring)]
    )
    length_table = jnp.broadcast_to(lengths.astype(F32)[:, None], (BAND, 128))
    inner, outer, columns, rows_of, own_waves = pl.pallas_call(
        table_kernel,
        out_shape=(
            jax.ShapeDtypeStruct((BAND, 256, GROUPS * 256), BF16),
            jax.ShapeDtypeStruct((BAND, 8, GROUPS * 256), F32),
            jax.ShapeDtypeStruct((BAND // 2, BLOCKS, 256, 256), BF16),
            jax.ShapeDtypeStruct((BAND // 2, BLOCKS, 24, 256), F32),
            jax.ShapeDtypeStruct((SLOTS, 128), F32),
        ),
        in_specs=[VMEM] * 3,
        out_specs=(VMEM,) * 5,
        scratch_shapes=[pltpu.VMEM((BAND, 16, WIDE), F32), pltpu.VMEM((BAND, 1, 128), F32)],
        compiler_params=pltpu.CompilerParams(vmem_limit_bytes=LIMIT),
        cost_estimate=pl.CostEstimate(flops=5_000_000_000, bytes_accessed=3_000_000, transcendentals=0),
        name="tables",
    )(length_table, ordered, stencil)
    wrap_columns, wrap_rows = pl.pallas_call(
        wrap_kernel,
        out_shape=(
            jax.ShapeDtypeStruct((BAND // 2, 128, 256), BF16),
            jax.ShapeDtypeStruct((BAND // 2, 24, 256), F32),
        ),
        in_specs=[VMEM] * 3,
        out_specs=(VMEM,) * 2,
        scratch_shapes=[pltpu.VMEM((BAND, 16, 128), F32)],
        compiler_params=pltpu.CompilerParams(vmem_limit_bytes=LIMIT),
        name="wrap_tables",
    )(length_table, from_left, from_right)

    weights = (columns, rows_of, wrap_columns, wrap_rows)
    part = jax.ShapeDtypeStruct((ROWS, STACK, 128), BF16)
    upper, main, edge = pl.pallas_call(
        upper_kernel,
        out_shape=(
            part,
            jax.ShapeDtypeStruct((COUNT, WIDE), BF16),
            jax.ShapeDtypeStruct((COUNT, WIDE + 128), BF16),
        ),
        in_specs=[VMEM] * 7,
        out_specs=(VMEM,) * 3,
        compiler_params=pltpu.CompilerParams(vmem_limit_bytes=LIMIT),
        name="interpolate_upper",
    )(own, under, over, *weights)
    cores = [(i, i ^ 1) for i in range(ring)]
    other_upper = lax.ppermute(upper, "wave", cores)
    lower = pl.pallas_call(
        lower_kernel,
        out_shape=part,
        in_specs=[VMEM] * 6,
        out_specs=VMEM,
        compiler_params=pltpu.CompilerParams(vmem_limit_bytes=LIMIT),
        cost_estimate=pl.CostEstimate(flops=5_000_000_000, bytes_accessed=3_000_000, transcendentals=0),
        name="interpolate_lower",
    )(main, edge, *weights)
    other_lower = lax.ppermute(lower, "wave", cores)
    scratch = [pltpu.VMEM((ROWS * 256, 128), F32), pltpu.VMEM((PEERS * 16, 128), F32)]
    message = pl.pallas_call(
        upper_fourier_kernel,
        out_shape=jax.ShapeDtypeStruct((PEERS * 16, 128), BF16),
        in_specs=[VMEM] * 4,
        out_specs=VMEM,
        scratch_shapes=scratch,
        compiler_params=pltpu.CompilerParams(vmem_limit_bytes=LIMIT),
        cost_estimate=pl.CostEstimate(flops=5_000_000_000, bytes_accessed=3_000_000, transcendentals=0),
        name="fourier_upper",
    )(upper, other_upper, inner, outer)
    message = pl.pallas_call(
        lower_fourier_kernel,
        out_shape=jax.ShapeDtypeStruct((PEERS * 32, 128), BF16),
        in_specs=[VMEM] * 5,
        out_specs=VMEM,
        scratch_shapes=scratch,
        compiler_params=pltpu.CompilerParams(vmem_limit_bytes=LIMIT),
        name="fourier_lower",
    )(lower, other_lower, inner, outer, message)
    message = lax.all_to_all(
        message.reshape(PEERS, 32, 128),
        ("lat", "wave"),
        split_axis=0,
        concat_axis=0,
        tiled=True,
        axis_index_groups=[[2 * peer + core for peer in ORDER] for core in range(2)],
    )
    degrees = legendre.shape[2]
    return pl.pallas_call(
        legendre_kernel,
        out_shape=jax.ShapeDtypeStruct((SLOTS, 2 * SLICES, degrees), F32),
        in_specs=[VMEM] * 3,
        out_specs=pl.BlockSpec(memory_space=pl.ANY),
        scratch_shapes=[
            pltpu.VMEM((512, 128), F32),
            pltpu.VMEM((512, 128), F32),
            pltpu.VMEM((512, 128), BF16),
            pltpu.VMEM((SLOTS, 2 * SLICES, degrees), F32),
            pltpu.SemaphoreType.DMA((SLOTS,)),
        ],
        compiler_params=pltpu.CompilerParams(vmem_limit_bytes=LIMIT),
        name="legendre",
    )(own_waves, message, legendre)


def solution(mesh):
    placed = (
        P(None, "lat", "wave"),
        P("lat"),
        P(),
        P("lat", "wave"),
        P("lat", "wave"),
        P("lat", "wave"),
        P("lat", "wave"),
        P(("lat", "wave"), None, None),
    )
    return jax.shard_map(
        local, mesh=mesh, in_specs=placed, out_specs=P(("lat", "wave"), None, None), check_vma=False
    )
```

```python
import math

import jax
import jax.numpy as jnp
import numpy as np
from jax import lax
from jax.experimental import pallas as pl
from jax.experimental.pallas import tpu as pltpu
from jax.sharding import PartitionSpec as P

F32 = jnp.float32
BF16 = jnp.bfloat16
VMEM = pl.BlockSpec(memory_space=pltpu.VMEM)
LIMIT = 24 * 1024 * 1024

SLICES = 24
BAND = 8
WIDE = 640
BLOCKS = 5
SLOTS = 10
PEERS = 64
ORDER = [int(peer) for peer in np.random.RandomState(6).permutation(PEERS)]
STANDS = [ORDER.index(peer) for peer in range(PEERS)]
GROUPS = 5
ROWS = 4
STACK = 144
COUNT = 3 * BAND * SLICES


def cubic_weights(fraction):
    return (
        -fraction * (fraction - 1.0) * (fraction - 2.0) / 6.0,
        (fraction + 1.0) * (fraction - 1.0) * (fraction - 2.0) / 2.0,
        -(fraction + 1.0) * fraction * (fraction - 2.0) / 2.0,
        (fraction + 1.0) * fraction * (fraction - 1.0) / 6.0,
    )


def picked_weight(distance, weights):
    chosen = jnp.where(distance == 3, weights[3], jnp.zeros_like(weights[3]))
    for step in (2, 1, 0):
        chosen = jnp.where(distance == step, weights[step], chosen)
    return chosen


def weighted(spread, rows_of, half):
    side = slice(128 * half, 128 * half + 128)
    total = jnp.zeros((SLICES, 128), F32)
    for row in range(half, half + 17):
        total = total + rows_of[row : row + 1, side] * spread[
            SLICES * row : SLICES * row + SLICES, side
        ]
    return total


def interpolate(steps, main, edge, columns, rows_of, wrap_columns, wrap_rows, out):
    for pair in steps:
        window = slice(pair * 2 * SLICES, pair * 2 * SLICES + 18 * SLICES)
        totals = ([], [])
        for block in range(BLOCKS + 1):
            lanes = slice(128 * block, 128 * block + 128)
            if block < BLOCKS:
                left = jnp.concatenate([main[window, lanes], edge[window, lanes]], axis=1)
                table, rows = columns[pair, block], rows_of.at[pair, block]
            else:
                left, table, rows = edge[window, lanes], wrap_columns[pair], wrap_rows.at[pair]
            spread = jnp.dot(left, table, preferred_element_type=F32)
            for half in range(2):
                totals[half].append(weighted(spread, rows, half))
        for half in range(2):
            out[(2 * pair + half) % ROWS] = jnp.concatenate(totals[half], axis=0).astype(BF16)


def upper_kernel(
    own, second, first, columns, rows_of, wrap_columns, wrap_rows, out, main, edge
):
    size = BAND * SLICES
    odd = lax.axis_index("lat") % 2
    main[pl.ds(pl.multiple_of(odd * 2 * size, size), size), :] = first[...]
    main[size : 2 * size, :] = own[...]
    main[pl.ds(pl.multiple_of((1 - odd) * 2 * size, size), size), :] = second[...]
    nothing = jnp.zeros((COUNT, 64), BF16)
    for block in range(BLOCKS):
        at = 128 * block
        sides = [
            main[:, at + 128 : at + 192] if block < BLOCKS - 1 else nothing,
            main[:, at - 64 : at] if block else nothing,
        ]
        edge[:, at : at + 128] = jnp.concatenate(sides, axis=1)
    edge[:, WIDE:] = jnp.concatenate([main[:, :64], main[:, WIDE - 64 :]], axis=1)
    interpolate((0, 1), main, edge, columns, rows_of, wrap_columns, wrap_rows, out)


def lower_kernel(main, edge, columns, rows_of, wrap_columns, wrap_rows, out):
    interpolate((2, 3), main, edge, columns, rows_of, wrap_columns, wrap_rows, out)


def turn(count, length, inverse):
    whole = jnp.floor(count * inverse + 0.5)
    angle = (count - whole * length) * (inverse * math.pi)
    square = angle * angle
    sine = angle * (
        1.0
        + square
        * (
            -1.0 / 6
            + square
            * (1.0 / 120 + square * (-1.0 / 5040 + square * (1.0 / 362880 - square / 39916800)))
        )
    )
    cosine = 1.0 + square * (
        -0.5
        + square
        * (
            1.0 / 24
            + square
            * (-1.0 / 720 + square * (1.0 / 40320 + square * (-1.0 / 3628800 + square / 479001600)))
        )
    )
    return 1.0 - 2.0 * sine * sine, 2.0 * sine * cosine


def rotated(one, two):
    return one[0] * two[0] - one[1] * two[1], one[1] * two[0] + one[0] * two[1]


def ring_start(place):
    return lax.rem(place + 8, 8) * WIDE


def spread_points(target, lengths, values, width, position):
    lane = (lax.broadcasted_iota(jnp.int32, (1, width), 1) % 128).astype(F32)
    limit = jnp.concatenate([lengths[...]] * (width // 128), axis=1)
    live = position.astype(F32) < limit
    for base, first, fraction in (
        (0, values[1] + (lane - 1.0), values[3]),
        (8, values[0] + (BAND - 1.0), values[2]),
    ):
        for k, value in enumerate((first,) + cubic_weights(fraction)):
            if base and k:
                value = jnp.where(live, value, 0.0)
            for row in range(BAND):
                target[row, base + k : base + k + 1, :] = value[row : row + 1, :]


def row_of(ref, pair, item, block):
    return jnp.concatenate(
        [
            ref[2 * pair + half, item : item + 1, 128 * block : 128 * block + 128]
            for half in range(2)
        ],
        axis=1,
    )


def picks(ref, pair, block):
    start = row_of(ref, pair, 0, block).astype(BF16)
    weights = [row_of(ref, pair, 1 + k, block).astype(BF16) for k in range(4)]

    def pick(count, first):
        source = lax.broadcasted_iota(jnp.int32, (count, 256), 0) + first
        return picked_weight(source.astype(F32).astype(BF16) - start, weights)

    return pick


def row_table(ref, pair, block):
    half = (lax.broadcasted_iota(jnp.int32, (1, 256), 1) >= 128).astype(F32)
    start = row_of(ref, pair, 8, block) + half
    weights = [row_of(ref, pair, 9 + k, block) for k in range(4)]
    source = lax.broadcasted_iota(jnp.int32, (24, 256), 0).astype(F32)
    return picked_weight(source - start, weights)


def table_kernel(
    lengths, waves, stencil, inner, outer, columns, rows_of, own_waves, points, length_rows
):
    wave_place = lax.axis_index("wave")
    core = wave_place % 2
    peer = lax.axis_index("lat") * 4 + wave_place // 2
    slots = jnp.where(core == 0, waves[:SLOTS, :], waves[SLOTS:, :])
    lane = lax.broadcasted_iota(jnp.int32, (SLOTS, PEERS), 1)
    mine = jnp.sum(jnp.where(lane == peer, slots, 0.0), axis=1, keepdims=True)
    own_waves[...] = jnp.broadcast_to(mine, (SLOTS, 128))
    column = lax.broadcasted_iota(jnp.int32, (1, PEERS), 1)
    order = jnp.zeros((1, PEERS), jnp.int32)
    for at, peer in enumerate(ORDER):
        order = jnp.where(column == at, peer, order)
    chosen = (lax.broadcasted_iota(jnp.int32, (PEERS, PEERS), 0) == order).astype(F32).astype(BF16)
    high = jnp.floor(slots * 0.125)
    slots = 8.0 * jnp.dot(high.astype(BF16), chosen, preferred_element_type=F32) + jnp.dot(
        (slots - 8.0 * high).astype(BF16), chosen, preferred_element_type=F32
    )
    groups = [
        jnp.concatenate([slots[k : k + 1], slots[k + 1 : k + 2]], axis=1)
        for k in range(0, SLOTS, 2)
    ]
    for row in range(BAND):
        length_rows[row] = lengths[row : row + 1, :]
    step = lax.broadcasted_iota(jnp.int32, (8, 128), 0)
    other_place = wave_place ^ 1
    away = (other_place - wave_place) * WIDE
    before = ring_start(wave_place - 1) + (WIDE - 128)
    behind = ring_start(wave_place + 1)
    other_before = ring_start(other_place - 1) + (WIDE - 128)
    other_behind = ring_start(other_place + 1)
    outside = jnp.where(core == 0, before, behind)
    other_outside = jnp.where(core == 0, other_behind, other_before) - away
    shift = 128 * step + wave_place * WIDE
    for at, value in ((5, outside), (6, other_outside), (7, away)):
        shift = jnp.where(step == at, value, shift)
    shift = shift.astype(F32)
    fine = step.astype(F32)
    coarse = 16.0 * fine

    def one(row, carry):
        length = length_rows[row]
        inverse = 1.0 / length
        norm = lax.rsqrt(length)
        for group, wave in enumerate(groups):
            lanes = slice(group * 256, group * 256 + 128)
            lanes_two = slice(group * 256 + 128, group * 256 + 256)
            moved = turn(shift * wave, length, inverse)
            outer[row, :, lanes] = moved[0] * norm
            outer[row, :, lanes_two] = moved[1] * norm
            other = [part[7:8] for part in moved]
            near = turn(fine * wave, length, inverse)
            eight = rotated([part[7:8] for part in near], [part[1:2] for part in near])
            small = [
                jnp.concatenate(parts, axis=0).astype(BF16)
                for parts in zip(near, rotated(eight, near))
            ]
            low = turn(coarse * wave, length, inverse)
            for tile in range(2):
                if tile:
                    low = rotated(low, other)
                for k in range(8):
                    start = [
                        jnp.broadcast_to(part[k : k + 1], (16, 128)).astype(BF16) for part in low
                    ]
                    rows = slice(128 * tile + 16 * k, 128 * tile + 16 * k + 16)
                    inner[row, rows, lanes], inner[row, rows, lanes_two] = rotated(start, small)
        return carry

    lax.fori_loop(0, BAND, one, 0)

    column = lax.broadcasted_iota(jnp.int32, (BAND, WIDE), 1)
    values = [stencil[k] for k in range(4)]
    spread_points(points, lengths, values, WIDE, column + wave_place * WIDE)

    def one_pair(pair, carry):
        for block in range(BLOCKS):
            pick = picks(points, pair, block)
            columns[pair, block, 0:144, :] = pick(144, 0)
            columns[pair, block, 144:240, :] = jnp.zeros((96, 256), BF16)
            columns[pair, block, 240:256, :] = pick(16, -16)
            rows_of[pair, block] = row_table(points, pair, block)
        return carry

    for pair in range(BAND // 2):
        one_pair(pair, 0)


def wrap_kernel(lengths, from_left, from_right, wrap_columns, wrap_rows, points):
    wave_place = lax.axis_index("wave")
    before = ring_start(wave_place - 1) + (WIDE - 128)
    behind = ring_start(wave_place + 1)
    column = lax.broadcasted_iota(jnp.int32, (BAND, 128), 1)
    values = [jnp.where(column < 64, from_right[k], from_left[k]) for k in range(4)]
    position = column + jnp.where(column < 64, behind, before)
    spread_points(points, lengths, values, 128, position)
    for pair in range(BAND // 2):
        pick = picks(points, pair, 0)
        wrap_columns[pair, 0:16, :] = pick(16, 128)
        wrap_columns[pair, 16:112, :] = jnp.zeros((96, 256), BF16)
        wrap_columns[pair, 112:128, :] = pick(16, -16)
        wrap_rows[pair] = row_table(points, pair, 0)


def fourier(first, mine, other, inner, outer, sums, shuffled):
    odd = jnp.full((SLICES, 128), lax.axis_index("wave") % 2, jnp.int32).astype(F32)
    low = (lax.broadcasted_iota(jnp.int32, (SLICES, 128), 1) < 64).astype(F32)
    to_mine = (low * odd, (1.0 - low) * (1.0 - odd))
    to_other = (low * (1.0 - odd), (1.0 - low) * odd)
    last = SLICES * (BLOCKS - 1)
    nothing = jnp.zeros((SLICES, 128), F32)

    for row in range(ROWS):
        own = mine[row].astype(F32)
        far = other[row].astype(F32)
        own_wrap, far_wrap = own[last + SLICES :], far[last + SLICES :]
        halves = [
            [
                own[:SLICES] + far_wrap * to_mine[0],
                own[SLICES:last],
                own[last : last + SLICES] + far_wrap * to_mine[1],
                own_wrap * (to_mine[0] + to_mine[1]),
                nothing,
                nothing[:8],
            ],
            [
                far[:SLICES] + own_wrap * to_other[0],
                far[SLICES:last],
                far[last : last + SLICES] + own_wrap * to_other[1],
                nothing,
                far_wrap * (to_other[0] + to_other[1]),
                nothing[:8],
            ],
        ]
        left = jnp.concatenate([jnp.concatenate(half, axis=0) for half in halves], axis=1)
        left = left.astype(BF16)
        base = 256 * row
        sums[base + 240 : base + 256, :] = jnp.zeros((16, 128), F32)
        for group in range(GROUPS):
            lanes = slice(256 * group, 256 * group + 256)
            parts = jnp.dot(left, inner[first + row, :, lanes], preferred_element_type=F32)
            real = jnp.zeros((SLICES, 128), F32)
            imag = jnp.zeros((SLICES, 128), F32)
            for block in range(BLOCKS + 2):
                rows = slice(SLICES * block, SLICES * block + SLICES)
                cosine, sine = parts[rows, :128], parts[rows, 128:]
                factor = outer[first + row, block : block + 1, lanes]
                c, s = factor[:, :128], factor[:, 128:]
                real = real + (c * cosine - s * sine)
                imag = imag - (s * cosine + c * sine)
            sums[pl.ds(base + group * 48, SLICES, stride=2), :] = real
            sums[pl.ds(base + group * 48 + 1, SLICES, stride=2), :] = imag
        for half in range(2):
            turned = sums[base + 128 * half : base + 128 * half + 128, :].T
            for side in range(2):
                at = 4 * row + 2 * side + half
                shuffled[pl.ds(at, PEERS, stride=16), :] = turned[PEERS * side : PEERS * side + PEERS]


def upper_fourier_kernel(mine, other, inner, outer, message, sums, shuffled):
    fourier(0, mine, other, inner, outer, sums, shuffled)
    message[...] = shuffled[...].astype(BF16)


def lower_fourier_kernel(mine, other, inner, outer, upper, message, sums, shuffled):
    fourier(ROWS, mine, other, inner, outer, sums, shuffled)
    for peer in range(PEERS):
        rows = slice(16 * peer, 16 * peer + 16)
        message[32 * peer : 32 * peer + 16, :] = upper[rows, :]
        message[32 * peer + 16 : 32 * peer + 32, :] = shuffled[rows, :].astype(BF16)


def legendre_kernel(waves, message, table, out, flat, sorted_rows, left, result, done):
    for band in range(16):
        total = message[STANDS[4 * band]].astype(F32)
        for z in range(1, 4):
            total = total + message[STANDS[4 * band + z]].astype(F32)
        flat[32 * band : 32 * band + 32, :] = total
    copies = []
    for part in range(4):
        for row in range(BAND):
            sorted_rows[pl.ds(128 * part + row, 16, stride=8), :] = flat[
                pl.ds(4 * row + part, 16, stride=32), :
            ]
        rows = slice(128 * part, 128 * part + 128)
        left[rows, :] = sorted_rows[rows, :].T.astype(BF16)
        for group in ((2, 3, 4) if part % 2 else (0, 1)):
            slot = 2 * group + part // 2
            first = 256 * (part // 2) + 48 * group
            product = jnp.dot(left[first : first + 48, :], table[slot], preferred_element_type=F32)
            wave = jnp.concatenate([waves[slot : slot + 1, :]] * (product.shape[1] // 128), axis=1)
            degree = lax.broadcasted_iota(jnp.int32, product.shape, 1).astype(F32)
            result[slot] = jnp.where(degree >= wave, product, 0.0)
            copy = pltpu.make_async_copy(result.at[slot], out.at[slot], done.at[slot])
            copy.start()
            copies.append(copy)
    for copy in copies:
        copy.wait()


def local(fields, row_length, wave_order, depart_row, depart_col, frac_row, frac_col, legendre):
    ring = lax.axis_size("wave")
    bands = lax.axis_size("lat")
    scalars = lax.optimization_barrier(jnp.concatenate([row_length, wave_order]))
    lengths = scalars[:BAND]
    limit = lengths - lax.axis_index("wave") * WIDE
    live_mask = jnp.arange(WIDE, dtype=jnp.int32)[None, :] < limit[:, None]
    masked = jnp.where(live_mask[None], fields, jnp.zeros_like(fields))
    own = masked.transpose(1, 0, 2).reshape(BAND * SLICES, WIDE)

    def swapped(first):
        pairs = [(i, i + 1) for i in range(first, bands - 1, 2)]
        return lax.ppermute(own, "lat", pairs + [(j, i) for i, j in pairs])

    over = swapped(1)
    under = swapped(0)

    own, depart_row = lax.optimization_barrier((own, depart_row))
    item = lax.broadcasted_iota(jnp.int32, (4, BAND, WIDE), 0)
    departs = jnp.where(item == 0, depart_row[None], depart_col[None]).astype(F32)
    fractions = jnp.where(item == 2, frac_row[None], frac_col[None])
    stencil = jnp.where(item < 2, departs, fractions)
    stencil, scalars = lax.optimization_barrier((stencil, scalars))
    ordered = scalars[BAND:].reshape(PEERS, 2 * SLOTS).T.astype(F32)
    from_left = lax.ppermute(
        stencil[:, :, WIDE - 128 :], "wave", [(i, (i + 1) % ring) for i in range(ring)]
    )
    from_right = lax.ppermute(
        stencil[:, :, :128], "wave", [((i + 1) % ring, i) for i in range(ring)]
    )
    length_table = jnp.broadcast_to(lengths.astype(F32)[:, None], (BAND, 128))
    inner, outer, columns, rows_of, own_waves = pl.pallas_call(
        table_kernel,
        out_shape=(
            jax.ShapeDtypeStruct((BAND, 256, GROUPS * 256), BF16),
            jax.ShapeDtypeStruct((BAND, 8, GROUPS * 256), F32),
            jax.ShapeDtypeStruct((BAND // 2, BLOCKS, 256, 256), BF16),
            jax.ShapeDtypeStruct((BAND // 2, BLOCKS, 24, 256), F32),
            jax.ShapeDtypeStruct((SLOTS, 128), F32),
        ),
        in_specs=[VMEM] * 3,
        out_specs=(VMEM,) * 5,
        scratch_shapes=[pltpu.VMEM((BAND, 16, WIDE), F32), pltpu.VMEM((BAND, 1, 128), F32)],
        compiler_params=pltpu.CompilerParams(vmem_limit_bytes=LIMIT),
        cost_estimate=pl.CostEstimate(flops=5_000_000_000, bytes_accessed=3_000_000, transcendentals=0),
        name="tables",
    )(length_table, ordered, stencil)
    wrap_columns, wrap_rows = pl.pallas_call(
        wrap_kernel,
        out_shape=(
            jax.ShapeDtypeStruct((BAND // 2, 128, 256), BF16),
            jax.ShapeDtypeStruct((BAND // 2, 24, 256), F32),
        ),
        in_specs=[VMEM] * 3,
        out_specs=(VMEM,) * 2,
        scratch_shapes=[pltpu.VMEM((BAND, 16, 128), F32)],
        compiler_params=pltpu.CompilerParams(vmem_limit_bytes=LIMIT),
        name="wrap_tables",
    )(length_table, from_left, from_right)

    weights = (columns, rows_of, wrap_columns, wrap_rows)
    part = jax.ShapeDtypeStruct((ROWS, STACK, 128), BF16)
    upper, main, edge = pl.pallas_call(
        upper_kernel,
        out_shape=(
            part,
            jax.ShapeDtypeStruct((COUNT, WIDE), BF16),
            jax.ShapeDtypeStruct((COUNT, WIDE + 128), BF16),
        ),
        in_specs=[VMEM] * 7,
        out_specs=(VMEM,) * 3,
        compiler_params=pltpu.CompilerParams(vmem_limit_bytes=LIMIT),
        name="interpolate_upper",
    )(own, under, over, *weights)
    cores = [(i, i ^ 1) for i in range(ring)]
    other_upper = lax.ppermute(upper, "wave", cores)
    lower = pl.pallas_call(
        lower_kernel,
        out_shape=part,
        in_specs=[VMEM] * 6,
        out_specs=VMEM,
        compiler_params=pltpu.CompilerParams(vmem_limit_bytes=LIMIT),
        cost_estimate=pl.CostEstimate(flops=5_000_000_000, bytes_accessed=3_000_000, transcendentals=0),
        name="interpolate_lower",
    )(main, edge, *weights)
    other_lower = lax.ppermute(lower, "wave", cores)
    scratch = [pltpu.VMEM((ROWS * 256, 128), F32), pltpu.VMEM((PEERS * 16, 128), F32)]
    message = pl.pallas_call(
        upper_fourier_kernel,
        out_shape=jax.ShapeDtypeStruct((PEERS * 16, 128), BF16),
        in_specs=[VMEM] * 4,
        out_specs=VMEM,
        scratch_shapes=scratch,
        compiler_params=pltpu.CompilerParams(vmem_limit_bytes=LIMIT),
        cost_estimate=pl.CostEstimate(flops=5_000_000_000, bytes_accessed=3_000_000, transcendentals=0),
        name="fourier_upper",
    )(upper, other_upper, inner, outer)
    message = pl.pallas_call(
        lower_fourier_kernel,
        out_shape=jax.ShapeDtypeStruct((PEERS * 32, 128), BF16),
        in_specs=[VMEM] * 5,
        out_specs=VMEM,
        scratch_shapes=scratch,
        compiler_params=pltpu.CompilerParams(vmem_limit_bytes=LIMIT),
        name="fourier_lower",
    )(lower, other_lower, inner, outer, message)
    message = lax.all_to_all(
        message.reshape(PEERS, 32, 128),
        ("lat", "wave"),
        split_axis=0,
        concat_axis=0,
        tiled=True,
        axis_index_groups=[[2 * peer + core for peer in ORDER] for core in range(2)],
    )
    degrees = legendre.shape[2]
    return pl.pallas_call(
        legendre_kernel,
        out_shape=jax.ShapeDtypeStruct((SLOTS, 2 * SLICES, degrees), F32),
        in_specs=[VMEM] * 3,
        out_specs=pl.BlockSpec(memory_space=pl.ANY),
        scratch_shapes=[
            pltpu.VMEM((512, 128), F32),
            pltpu.VMEM((512, 128), F32),
            pltpu.VMEM((512, 128), BF16),
            pltpu.VMEM((SLOTS, 2 * SLICES, degrees), F32),
            pltpu.SemaphoreType.DMA((SLOTS,)),
        ],
        compiler_params=pltpu.CompilerParams(vmem_limit_bytes=LIMIT),
        name="legendre",
    )(own_waves, message, legendre)


def solution(mesh):
    placed = (
        P(None, "lat", "wave"),
        P("lat"),
        P(),
        P("lat", "wave"),
        P("lat", "wave"),
        P("lat", "wave"),
        P("lat", "wave"),
        P(("lat", "wave"), None, None),
    )
    return jax.shard_map(
        local, mesh=mesh, in_specs=placed, out_specs=P(("lat", "wave"), None, None), check_vma=False
    )
```
